32 devices in a mesh: dp: 8 (over z, x), tensor: 4 (over y, core).
Axes of the slice: x: 2, y: 2, z: 4, core: 2. Of those that a mesh axis runs over, the one named last changes fastest.
Arguments:
- hidden_in: bfloat16 [2, 8, 256, 1152], P(None, 'dp'), may hold values from -6 to 6
- grad_out: bfloat16 [2, 8, 256, 1152], P(None, 'dp'), may hold values from -0.0059814453 to 0.0059814453
- features: bfloat16 [2, 8, 256, 768], P(None, 'dp'), may hold values from -6 to 6
- seg_ids: int32 [2, 8, 256], P(None, 'dp'), may hold values from 0 to 3, never falling along the last dimension, each value on 1 to 128 neighbouring positions
- valid_mask: int32 [2, 8, 256], P(None, 'dp'), may hold values 0 or 1
- time_ids: int32 [2, 8, 4], P(None, 'dp'), may hold values from 0 to 999
- class_ids: int32 [2, 8, 4], P(None, 'dp'), may hold values from 0 to 1000
- class_table: bfloat16 [1152, 1001], P('dp'), may hold values from -6 to 6
- ada_w: bfloat16 [6912, 1152], P('dp'), may hold values from -0.1875 to 0.1875
- ada_b: bfloat16 [6912], P('dp'), may hold values from -3 to 3
- qkv_w: bfloat16 [3, 1152, 1152], P(None, None, 'tensor'), may hold values from -0.1875 to 0.1875
- qv_bias: bfloat16 [2, 1152], P(None, 'tensor'), may hold values from -3 to 3
- out_w: bfloat16 [1152, 1152], P('tensor'), may hold values from -0.75 to 0.75
- out_b: bfloat16 [1152], replicated, may hold values from -3 to 3
- fc1_w: bfloat16 [1152, 4608], P(None, 'tensor'), may hold values from -0.1875 to 0.1875
- fc1_b: bfloat16 [4608], P('tensor'), may hold values from -3 to 3
- fc2_w: bfloat16 [4608, 1152], P('tensor'), may hold values from -0.09375 to 0.09375
- fc2_b: bfloat16 [1152], replicated, may hold values from -3 to 3
- repa_w1: bfloat16 [1152, 2048], P('dp'), may hold values from -0.1875 to 0.1875
- repa_b1: bfloat16 [2048], P('dp'), may hold values from -3 to 3
- repa_w2: bfloat16 [2048, 2048], P('dp'), may hold values from -0.125 to 0.125
- repa_b2: bfloat16 [2048], P('dp'), may hold values from -3 to 3
- repa_w3: bfloat16 [2048, 768], P('dp'), may hold values from -0.125 to 0.125
- repa_b3: bfloat16 [768], P('dp'), may hold values from -3 to 3
Outputs:
- block_out: bfloat16 [2, 8, 256, 1152], P(None, 'dp')
- grad_in: float32 [2, 8, 256, 1152], P(None, 'dp')
- grad_class_table: float32 [1152, 1001], P('dp')
- grad_ada_w: float32 [6912, 1152], P('dp')
- grad_ada_b: float32 [6912], P('dp')
- grad_qkv_w: float32 [3, 1152, 1152], P(None, 'dp', 'tensor')
- grad_qv_bias: float32 [2, 1152], P(None, 'tensor')
- grad_out_w: float32 [1152, 1152], P('tensor', 'dp')
- grad_out_b: float32 [1152], replicated
- grad_fc1_w: float32 [1152, 4608], P('dp', 'tensor')
- grad_fc1_b: float32 [4608], P('tensor')
- grad_fc2_w: float32 [4608, 1152], P('tensor', 'dp')
- grad_fc2_b: float32 [1152], replicated
- grad_repa_w1: float32 [1152, 2048], P('dp')
- grad_repa_b1: float32 [2048], P('dp')
- grad_repa_w2: float32 [2048, 2048], P('dp')
- grad_repa_b2: float32 [2048], P('dp')
- grad_repa_w3: float32 [2048, 768], P('dp')
- grad_repa_b3: float32 [768], P('dp')
The draws below stay inside these ranges and needn't reach their ends.
Inputs may be any that keep to these rules, and one draw needn't show every extreme that they name: `seg_ids`: within each row the ids never fall, every image 0 to 3 appears, and no image has more than half of 256 tokens.
All inputs are finite; a program needn't handle non-finite values. No bound on the sum of `valid_mask` on one device may be relied on, other than what follows from the above.
Results may differ from the reference program's by a relative error of at most 0.02615.
Values may be sent and summed in bfloat16 or wider, within the bound.
No kernel may reach another device: no remote copies, remote signals or barrier semaphores. Data moves between devices by JAX's collectives and lax.ppermute only.
A program may use at most 320 MiB of HBM per device.

```python
import math
import jax
import jax.numpy as jnp
import numpy as np
from jax import lax

D = 1152
HEAD_DIM = 72
FF = 4608
CLASSES = 1001
PROJ = 2048
REPR = 768
SEQ = 256
SEGS = 4
MICRO = 2
ROWS = 8


def set_ends(drawn, key, low, high):
    shape = drawn.shape
    spot = [jax.random.randint(jax.random.fold_in(key, axis), (), 0, shape[axis]) for axis in range(len(shape))]
    drawn = drawn.at[tuple(spot)].set(low)
    longest = shape.index(max(shape))
    spot[longest] = (spot[longest] + 1) % shape[longest]
    return drawn.at[tuple(spot)].set(high)


def block_levels(own_key, extent, cuts, smallest, top_value):
    def one(axis_at, blocks):
        draws = jax.random.uniform(jax.random.fold_in(jax.random.fold_in(own_key, 6), axis_at), (blocks,), jnp.float32, smallest / len(cuts), top_value / len(cuts))
        return jnp.repeat(jnp.exp(draws), extent[axis_at] // blocks).reshape((-1,) + (1,) * (len(extent) - axis_at - 1))

    gain = one(*cuts[0])
    for cut in cuts[1:]:
        gain = gain * one(*cut)
    return gain


def split_up(count, total, most, slope):
    loads = [(1 << 20) // math.isqrt(standing ** slope) + 1 for standing in range(2, count + 1)]
    surplus, holding = total - most - (count - 1), [1] * (count - 1)
    while surplus > 0:
        movable = [i for i in range(count - 1) if holding[i] < most]
        pool, remaining = sum([loads[i] for i in movable]), surplus
        for i in movable:
            more = min(most - holding[i], max(1, remaining * loads[i] // pool), surplus)
            holding[i] = holding[i] + more
            surplus = surplus - more
    return np.array([most] + holding)


def ragged_sizes(key, count, total, bound, slope):
    if count == 2:
        one = jax.random.randint(key, (), max(1, total - bound), min(bound, total - 1) + 1)
        return jnp.stack([one, total - one])
    tallies = jnp.asarray(split_up(count, total, bound, slope), jnp.int32)
    couples = (count - 1) // 2
    donor, receiver = tallies[1:1 + 2 * couples:2], tallies[2:2 + 2 * couples:2]
    margin = jnp.minimum(donor - 1, bound - receiver)
    moved = jax.random.randint(jax.random.fold_in(key, 1), (couples,), 0, 1 << 20) % (margin + 1)
    tallies = tallies.at[1:1 + 2 * couples:2].set(donor - moved).at[2:2 + 2 * couples:2].set(receiver + moved)
    return tallies[jax.random.permutation(jax.random.fold_in(key, 2), count)]


def bell_draw(stream_key, shape, deviation, bound, shards=(), kind=jnp.bfloat16):
    array = jax.random.normal(stream_key, shape, jnp.float32) * deviation
    if len(shards) > 0:
        array = block_levels(stream_key, shape, shards, -0.22, 0.18) * array
    return jnp.clip(array, min=-bound, max=bound).astype(kind)


def setup_inputs(seed: int = 0) -> dict:
    arg_keys = jax.random.split(jax.random.key(seed), 25)
    return {
        "hidden_in": bell_draw(arg_keys[0], (MICRO, ROWS, SEQ, D), 1.0, 6.0, ((1, 8),)),
        "grad_out": bell_draw(arg_keys[1], (MICRO, ROWS, SEQ, D), 0.001, 0.0059814453, ((1, 8),)),
        "features": bell_draw(arg_keys[2], (MICRO, ROWS, SEQ, REPR), 1.0, 6.0, ((1, 8),)),
        "seg_ids": jax.vmap(lambda own: jnp.searchsorted(jnp.cumsum(ragged_sizes(own, SEGS, SEQ, SEQ // 2, 1)), jnp.arange(SEQ), side="right"))(jax.random.split(arg_keys[3], MICRO * ROWS)).reshape((MICRO, ROWS, SEQ)).astype(jnp.int32),
        "valid_mask": set_ends((jax.random.randint(arg_keys[4], (MICRO, ROWS, SEQ), 0, 8) < 7).astype(jnp.int32), jax.random.fold_in(arg_keys[4], 1), 0, 1),
        "time_ids": set_ends(jax.random.randint(arg_keys[5], (MICRO, ROWS, SEGS), 0, 1000), jax.random.fold_in(arg_keys[5], 1), 0, 999).astype(jnp.int32),
        "class_ids": set_ends(jax.random.randint(arg_keys[6], (MICRO, ROWS, SEGS), 0, CLASSES), jax.random.fold_in(arg_keys[6], 1), 0, CLASSES - 1).astype(jnp.int32),
        "class_table": bell_draw(arg_keys[7], (D, CLASSES), 1.0, 6.0, ((0, 8),)),
        "ada_w": bell_draw(arg_keys[8], (6 * D, D), D ** -0.5, 0.1875, ((0, 8),)),
        "ada_b": bell_draw(arg_keys[9], (6 * D,), 0.5, 3.0, ((0, 8),)),
        "qkv_w": bell_draw(arg_keys[10], (3, D, D), D ** -0.5, 0.1875, ((2, 4),)),
        "qv_bias": bell_draw(arg_keys[11], (2, D), 0.5, 3.0, ((1, 4),)),
        "out_w": bell_draw(arg_keys[12], (D, D), (D // 16) ** -0.5, 0.75, ((0, 4),)),
        "out_b": bell_draw(arg_keys[13], (D,), 0.5, 3.0),
        "fc1_w": bell_draw(arg_keys[14], (D, FF), D ** -0.5, 0.1875, ((1, 4),)),
        "fc1_b": bell_draw(arg_keys[15], (FF,), 0.5, 3.0, ((0, 4),)),
        "fc2_w": bell_draw(arg_keys[16], (FF, D), FF ** -0.5, 0.09375, ((0, 4),)),
        "fc2_b": bell_draw(arg_keys[17], (D,), 0.5, 3.0),
        "repa_w1": bell_draw(arg_keys[18], (D, PROJ), D ** -0.5, 0.1875, ((0, 8),)),
        "repa_b1": bell_draw(arg_keys[19], (PROJ,), 0.5, 3.0, ((0, 8),)),
        "repa_w2": bell_draw(arg_keys[20], (PROJ, PROJ), PROJ ** -0.5, 0.125, ((0, 8),)),
        "repa_b2": bell_draw(arg_keys[21], (PROJ,), 0.5, 3.0, ((0, 8),)),
        "repa_w3": bell_draw(arg_keys[22], (PROJ, REPR), PROJ ** -0.5, 0.125, ((0, 8),)),
        "repa_b3": bell_draw(arg_keys[23], (REPR,), 0.5, 3.0, ((0, 8),)),
    }


HIGH = lax.Precision.HIGHEST
norm_eps = 1e-06
cos_eps = 1e-06
repa_weight = 0.5

@jax.custom_vjp
def low(v):
    return lax.optimization_barrier(v.astype(jnp.bfloat16)).astype(jnp.float32)

@jax.custom_vjp
def low_back(v):
    return v

def low_keep(v):
    return (low(v), None)

def low_pass(kept, grad):
    return (grad,)

def back_keep(v):
    return (v, None)

def back_low(kept, grad):
    return (low(grad),)
low.defvjp(low_keep, low_pass)
low_back.defvjp(back_keep, back_low)

def matmul(first, second):
    return jnp.dot(first, second, precision=HIGH, preferred_element_type=jnp.float32)

def sinusoid(times, model_width):
    half_width = model_width // 2
    freqs = jnp.exp(-math.log(10000.0) * jnp.arange(half_width, dtype=jnp.float32) / half_width)
    angles = times.astype(jnp.float32)[:, None] * freqs[None, :]
    return jnp.concatenate([jnp.cos(angles), jnp.sin(angles)], axis=-1)

def layer_norm(field):
    centered = field - lax.optimization_barrier(jnp.mean(field, axis=-1, keepdims=True))
    return centered * lax.rsqrt(lax.optimization_barrier(jnp.mean(centered * centered, axis=-1, keepdims=True)) + norm_eps)

def row_forward(params, row_x, row_feat, row_seg, row_valid, row_time, row_class):
    table, ada_mat, ada_bias, qkv_mat, qv_vec, out_mat, out_vec, fc1_mat, fc1_vec, fc2_mat, fc2_vec, repa_m1, repa_v1, repa_m2, repa_v2, repa_m3, repa_v3 = params
    seq_len, model_width = row_x.shape
    heads_all = model_width // HEAD_DIM
    condition = sinusoid(row_time, model_width) + jnp.take(table, row_class, axis=1).T
    cond_act = low(jax.nn.silu(condition))
    modulation = low_back(matmul(cond_act, ada_mat.T) + ada_bias)
    token_mod = jnp.take(modulation, row_seg, axis=0)
    shift1, scale1, gate1, shift2, scale2, gate2 = jnp.split(token_mod, 6, axis=-1)
    m_one = low(layer_norm(row_x) * (1.0 + scale1) + shift1)
    queries = low(low_back(matmul(m_one, qkv_mat[0]) + qv_vec[0]))
    key_rows = low(low_back(matmul(m_one, qkv_mat[1])))
    value_rows = low(low_back(matmul(m_one, qkv_mat[2]) + qv_vec[1]))
    shape3 = (seq_len, heads_all, HEAD_DIM)
    scores = jnp.einsum('qhd,khd->hqk', queries.reshape(shape3), key_rows.reshape(shape3), precision=HIGH) * HEAD_DIM ** (-0.5)
    places = jnp.arange(seq_len)
    opened = (row_seg[:, None] == row_seg[None, :]) & ((row_valid[None, :] == 1) | (places[:, None] == places[None, :]))
    scores = low_back(jnp.where(opened[None], scores, -1e+30))
    row_top = lax.optimization_barrier(jnp.max(scores, axis=-1, keepdims=True))
    exponent = jnp.exp(scores - row_top)
    probs = exponent / lax.optimization_barrier(jnp.sum(exponent, axis=-1, keepdims=True))
    mixed = jnp.einsum('hqk,khd->qhd', low(probs), value_rows.reshape(shape3), precision=HIGH).reshape(seq_len, model_width)
    mixed = low(low_back(mixed))
    attn_out = low_back(matmul(mixed, out_mat) + out_vec)
    h_one = row_x + gate1 * attn_out
    m_two = low(layer_norm(h_one) * (1.0 + scale2) + shift2)
    hidden_pre = low_back(matmul(m_two, fc1_mat) + fc1_vec)
    hidden_act = low(jax.nn.gelu(hidden_pre, approximate=True))
    mlp_out = low_back(matmul(hidden_act, fc2_mat) + fc2_vec)
    h_out = h_one + gate2 * mlp_out
    h_low = low(h_out)
    a_one = low_back(matmul(h_low, repa_m1) + repa_v1)
    s_one = low(jax.nn.silu(a_one))
    a_two = low_back(matmul(s_one, repa_m2) + repa_v2)
    s_two = low(jax.nn.silu(a_two))
    z_proj = low_back(matmul(s_two, repa_m3) + repa_v3)
    cosine = lax.optimization_barrier(jnp.sum(z_proj * row_feat, axis=-1)) * lax.rsqrt(lax.optimization_barrier(jnp.sum(z_proj * z_proj, axis=-1)) + cos_eps) * lax.rsqrt(lax.optimization_barrier(jnp.sum(row_feat * row_feat, axis=-1)) + cos_eps)
    repa_loss = -repa_weight * jnp.sum(cosine * row_valid.astype(jnp.float32))
    return (h_out, repa_loss)

def reference(hidden_in, grad_out, features, seg_ids, valid_mask, time_ids, class_ids, class_table, ada_w, ada_b, qkv_w, qv_bias, out_w, out_b, fc1_w, fc1_b, fc2_w, fc2_b, repa_w1, repa_b1, repa_w2, repa_b2, repa_w3, repa_b3):
    micro_count, row_count, seq_len, model_width = hidden_in.shape
    all_rows = micro_count * row_count
    params = tuple((item.astype(jnp.float32) for item in (class_table, ada_w, ada_b, qkv_w, qv_bias, out_w, out_b, fc1_w, fc1_b, fc2_w, fc2_b, repa_w1, repa_b1, repa_w2, repa_b2, repa_w3, repa_b3)))
    rows_x = hidden_in.reshape(all_rows, seq_len, model_width).astype(jnp.float32)
    rows_feat = features.reshape(all_rows, seq_len, -1).astype(jnp.float32)
    rows_seg = seg_ids.reshape(all_rows, seq_len)
    rows_valid = valid_mask.reshape(all_rows, seq_len)
    rows_time = time_ids.reshape(all_rows, -1)
    rows_class = class_ids.reshape(all_rows, -1)

    def total_loss(param_set, inputs_x):

        def one_row(pieces):
            return jax.checkpoint(row_forward)(param_set, *pieces)
        h_rows, losses = lax.map(one_row, (inputs_x, rows_feat, rows_seg, rows_valid, rows_time, rows_class))
        return (h_rows, jnp.sum(losses))
    (h_rows, loss_value), pullback = jax.vjp(total_loss, params, rows_x)
    grads, grad_rows = pullback((grad_out.reshape(all_rows, seq_len, model_width).astype(jnp.float32), jnp.ones((), jnp.float32)))
    g_table, g_ada_w, g_ada_b, g_qkv_w, g_qv_bias, g_out_w, g_out_b, g_fc1_w, g_fc1_b, g_fc2_w, g_fc2_b, g_w1, g_b1, g_w2, g_b2, g_w3, g_b3 = grads
    return (h_rows.reshape(hidden_in.shape).astype(jnp.bfloat16), grad_rows.reshape(hidden_in.shape), g_table, g_ada_w, g_ada_b, g_qkv_w, g_qv_bias, g_out_w, g_out_b, g_fc1_w, g_fc1_b, g_fc2_w, g_fc2_b, g_w1, g_b1, g_w2, g_b2, g_w3, g_b3)
```

```python
import functools
import math

import jax
import jax.numpy as jnp
from jax import lax
from jax.experimental import pallas as pl
from jax.experimental.pallas import tpu as pltpu
from jax.sharding import PartitionSpec as P

HEAD_DIM = 72
norm_eps = 1e-06
cos_eps = 1e-06
repa_weight = 0.5
F32 = jnp.float32
BF16 = jnp.bfloat16
VMEM = pl.BlockSpec(memory_space=pltpu.VMEM)
SMEM = pl.BlockSpec(memory_space=pltpu.SMEM)
ANY = pl.BlockSpec(memory_space=pl.ANY)
VMEM_LIMIT = 58 * 1024 * 1024


def shape_of(shape, dtype):
    return jax.ShapeDtypeStruct(tuple(shape), dtype)


def call(kernel, outs, ins, in_specs=None, out_specs=None, scratch=(), flops=0, limit=VMEM_LIMIT, name=None):
    moved = sum(math.prod(a.shape) * a.dtype.itemsize for a in list(ins) + list(outs))
    return pl.pallas_call(
        kernel,
        out_shape=tuple(outs),
        in_specs=in_specs or [VMEM] * len(ins),
        out_specs=tuple(out_specs or [VMEM] * len(outs)),
        scratch_shapes=list(scratch),
        compiler_params=pltpu.CompilerParams(vmem_limit_bytes=limit),
        cost_estimate=pl.CostEstimate(flops=flops, bytes_accessed=moved, transcendentals=0),
        name=name,
    )(*ins)


def dot(a, b):
    return jnp.dot(a, b, preferred_element_type=F32)


def dot_nt(a, b):
    return lax.dot_general(a, b, (((1,), (1,)), ((), ())), preferred_element_type=F32)


def dot_tn(a, b):
    return lax.dot_general(a, b, (((0,), (0,)), ((), ())), preferred_element_type=F32)


def sigmoid(v):
    return 1.0 / (1.0 + jnp.exp(-v))


def silu_slope(v):
    s = sigmoid(v)
    return s * (1.0 + v * (1.0 - s))


def pick(seg, table):
    out = jnp.broadcast_to(table[0:1, :], (seg.shape[0], table.shape[1]))
    for s in range(1, table.shape[0]):
        out = jnp.where(seg == s, table[s : s + 1, :], out)
    return out


def by_image(seg, values, slots):
    rows = [jnp.sum(jnp.where(seg == s, values, 0.0), axis=0, keepdims=True) for s in range(slots)]
    return jnp.concatenate(rows, axis=0)


def norm_parts(v):
    centered = v - jnp.mean(v, axis=-1, keepdims=True)
    inv = lax.rsqrt(jnp.mean(centered * centered, axis=-1, keepdims=True) + norm_eps)
    return centered * inv, inv


def norm_back(g, xhat, inv):
    return inv * (g - jnp.mean(g, axis=-1, keepdims=True) - xhat * jnp.mean(g * xhat, axis=-1, keepdims=True))


def attend(q, k, v, open_mask, scale):
    s = dot_nt(q, k) * scale
    s = jnp.where(open_mask, s, -1e30)
    e = jnp.exp(s - jnp.max(s, axis=-1, keepdims=True))
    return e * (1.0 / jnp.sum(e, axis=-1, keepdims=True))


def open_of(segc, segr, valr):
    n = segc.shape[0]
    same = lax.broadcasted_iota(jnp.int32, (n, n), 0) == lax.broadcasted_iota(jnp.int32, (n, n), 1)
    return (segc == segr) & ((valr == 1) | same)


def fwd_kernel(heads, order, hid, mods, segc, segr, valr, w, b, m_ref, q_ref, k_ref, v_ref, mix_ref):
    half, width = hid.shape[1], hid.shape[2]
    seq = 2 * half
    scale = HEAD_DIM ** (-0.5)
    for micro in range(2):
        x = jnp.concatenate([hid[order[2 * micro]], hid[order[2 * micro + 1]]], axis=0).astype(F32)
        rows = slice(micro * seq, (micro + 1) * seq)
        seg = segc[rows, :]
        xhat, _ = norm_parts(x)
        shift = pick(seg, mods[micro][:, 0:width])
        scaling = pick(seg, mods[micro][:, width : 2 * width])
        m = (xhat * (1.0 + scaling) + shift).astype(BF16)
        m_ref[rows, :] = m
        q = (dot(m, w[0]) + b[0:1, :]).astype(BF16)
        k = dot(m, w[1]).astype(BF16)
        v = (dot(m, w[2]) + b[1:2, :]).astype(BF16)
        q_ref[rows, :] = q
        k_ref[rows, :] = k
        v_ref[rows, :] = v
        mask = open_of(seg, segr[micro : micro + 1, :], valr[micro : micro + 1, :])
        mixed = []
        for h in range(heads):
            cols = slice(h * HEAD_DIM, (h + 1) * HEAD_DIM)
            p = attend(q[:, cols], k[:, cols], v[:, cols], mask, scale)
            mixed.append(dot(p.astype(BF16), v[:, cols]).astype(BF16))
        mix_ref[rows, :] = jnp.concatenate(mixed, axis=1)


def bwd_kernel(heads, g0, g1, g2, g3, out_w, q_ref, k_ref, v_ref, segc, segr, valr, w, gqkv_ref, part_q, part_y, send_q, send_y, bias_ref, gfull_ref):
    half = g0.shape[0]
    seq = 2 * half
    scale = HEAD_DIM ** (-0.5)
    wide = heads * HEAD_DIM
    sums = []
    for micro in range(2):
        rows = slice(micro * seq, (micro + 1) * seq)
        g = jnp.concatenate([g0[...], g1[...]] if micro == 0 else [g2[...], g3[...]], axis=0)
        gfull_ref[rows, :] = g
        gm = dot_nt(g, out_w[...]).astype(BF16)
        q, k, v = q_ref[rows, :], k_ref[rows, :], v_ref[rows, :]
        mask = open_of(segc[rows, :], segr[micro : micro + 1, :], valr[micro : micro + 1, :])
        gq, gk, gv = [], [], []
        for h in range(heads):
            cols = slice(h * HEAD_DIM, (h + 1) * HEAD_DIM)
            qh, kh, vh, gh = q[:, cols], k[:, cols], v[:, cols], gm[:, cols]
            p = attend(qh, kh, vh, mask, scale)
            gp = dot_nt(gh, vh)
            gs = (p * (gp - jnp.sum(p * gp, axis=-1, keepdims=True))).astype(BF16)
            gq.append((dot(gs, kh) * scale).astype(BF16))
            gk.append((dot_tn(gs, qh) * scale).astype(BF16))
            gv.append(dot_tn(p.astype(BF16), gh).astype(BF16))
        gq, gk, gv = (jnp.concatenate(a, axis=1) for a in (gq, gk, gv))
        gqkv_ref[rows, 0:wide] = gq
        gqkv_ref[rows, wide : 2 * wide] = gk
        gqkv_ref[rows, 2 * wide : 3 * wide] = gv
        sums.append(
            jnp.concatenate(
                [jnp.sum(gq.astype(F32), axis=0, keepdims=True), jnp.sum(gv.astype(F32), axis=0, keepdims=True)],
                axis=0,
            )
        )
        part = dot_nt(gq, w[0]) + dot_nt(gk, w[1]) + dot_nt(gv, w[2])
        if micro == 0:
            part_q[...] = part[:half]
            part_y[...] = part[half:]
        else:
            send_q[...] = part[:half].astype(BF16)
            send_y[...] = part[half:].astype(BF16)
    bias_ref[...] = sums[0] + sums[1]


def mid_kernel(order, hid, mods, segc, m0, m1, m2, m3, w0, w1, w2, w3, out_b, attn_q, h_q, m_two):
    half, width = hid.shape[1], hid.shape[2]
    seq = 2 * half
    x = jnp.concatenate([hid[order[0]], hid[order[1]]], axis=0).astype(F32)
    seg = segc[0:seq, :]
    m2, m3 = (jnp.concatenate([m[half:, :], m[:half, :]], axis=0) for m in (m2, m3))
    attn = dot(m0[...], w0[...]) + dot(m1[...], w1[...]) + dot(m2, w2[...]) + dot(m3, w3[...])
    attn = attn + out_b[...]
    h = x + pick(seg, mods[:, 2 * width : 3 * width]) * attn
    attn_q[...] = attn[:half]
    h_q[...] = h[:half]
    xhat, _ = norm_parts(h)
    m_two[...] = (
        xhat * (1.0 + pick(seg, mods[:, 4 * width : 5 * width])) + pick(seg, mods[:, 3 * width : 4 * width])
    ).astype(BF16)


SPLITS = ((0, 512), (512, 1152))
K0 = math.sqrt(2.0 / math.pi)


def mlp_kernel(m_own, m_par, fc1, b1, fc2, m_full, pre_ref, act_ref, part_q, part_y, send_q, send_y):
    seq = m_own.shape[0]
    half = seq // 2
    for micro, m_ref in enumerate((m_own, m_par)):
        rows = slice(micro * seq, (micro + 1) * seq)
        m = m_ref[...]
        m_full[rows, :] = m
        for lo, hi in SPLITS:
            pre = dot(m, fc1[:, lo:hi]) + b1[:, lo:hi]
            pre_ref[rows, lo:hi] = pre
            t = jnp.tanh(K0 * (pre + 0.044715 * (pre * pre * pre)))
            act_ref[rows, lo:hi] = (0.5 * pre * (1.0 + t)).astype(BF16)
        act = act_ref[rows, :]
        for lo, hi in SPLITS:
            part = dot(act, fc2[:, lo:hi])
            if micro == 0:
                part_q[:, lo:hi] = part[:half]
                part_y[:, lo:hi] = part[half:]
            else:
                send_q[:, lo:hi] = part[:half].astype(BF16)
                send_y[:, lo:hi] = part[half:].astype(BF16)


def mlp_back_kernel(g0, g1, g2, g3, pre_ref, fc1, fc2, g_full, gpre_ref, part_q, part_y, send_q, send_y, bias):
    half = g0.shape[0]
    seq = 2 * half
    for micro in range(2):
        rows = slice(micro * seq, (micro + 1) * seq)
        g = jnp.concatenate([g0[...], g1[...]] if micro == 0 else [g2[...], g3[...]], axis=0)
        g_full[rows, :] = g
        for lo, hi in SPLITS:
            ga = dot_nt(g, fc2[lo:hi, :])
            v = pre_ref[rows, lo:hi]
            t = jnp.tanh(K0 * (v + 0.044715 * (v * v * v)))
            slope = 0.5 * (1.0 + t) + 0.5 * v * (1.0 - t * t) * (K0 * (1.0 + 3.0 * 0.044715 * (v * v)))
            gp = (ga * slope).astype(BF16)
            gpre_ref[rows, lo:hi] = gp
            total = jnp.sum(gp.astype(F32), axis=0, keepdims=True)
            bias[:, lo:hi] = total if micro == 0 else bias[:, lo:hi] + total
        gp = gpre_ref[rows, :]
        for lo, hi in SPLITS:
            part = dot_nt(gp, fc1[lo:hi, :])
            if micro == 0:
                part_q[:, lo:hi] = part[:half]
                part_y[:, lo:hi] = part[half:]
            else:
                send_q[:, lo:hi] = part[:half].astype(BF16)
                send_y[:, lo:hi] = part[half:].astype(BF16)


def proj_kernel(plan, n_pieces, meta, *refs):
    (part, rq, ry, h_one, mods, seg_ref, fc2_b, grad_out, feat_ref, keep_ref, b1, b2, b3) = refs[:13]
    pieces = refs[13 : 13 + n_pieces]
    (h_low, grad_h, g_mlp, gate_sum, s1, s2, gz_ref, ga2_ref, ga1_ref, gb1, gb2, gb3, gbf) = refs[13 + n_pieces : 26 + n_pieces]
    w1, w2, w3, a1, a2, sems = refs[26 + n_pieces :]
    weights = (w1, w2, w3)
    width = h_low.shape[1]
    slots = mods.shape[0]
    for piece, (which, place) in zip(pieces, plan):
        for source, target in place(piece, weights[which], meta):
            pltpu.make_async_copy(source, target, sems.at[which]).start()
    seg = seg_ref[...]
    gate = pick(seg, mods[:, 5 * width : 6 * width])
    mlp = part[...] + rq[...].astype(F32) + ry[...].astype(F32) + fc2_b[...]
    h = h_one[...] + gate * mlp
    hl = h.astype(BF16)
    h_low[...] = hl
    hidden = w1.shape[1]
    step = 512
    pltpu.make_async_copy(w1, w1, sems.at[0]).wait()
    for lo in range(0, hidden, step):
        a = dot(hl, w1[:, lo : lo + step]) + b1[:, lo : lo + step]
        a1[:, lo : lo + step] = a
        s1[:, lo : lo + step] = (a * sigmoid(a)).astype(BF16)
    pltpu.make_async_copy(w2, w2, sems.at[1]).wait()
    s = s1[...]
    for lo in range(0, hidden, step):
        a = dot(s, w2[:, lo : lo + step]) + b2[:, lo : lo + step]
        a2[:, lo : lo + step] = a
        s2[:, lo : lo + step] = (a * sigmoid(a)).astype(BF16)
    pltpu.make_async_copy(w3, w3, sems.at[2]).wait()
    z = dot(s2[...], w3[...]) + b3[...]
    feat = feat_ref[...].astype(F32)
    inv_z = lax.rsqrt(jnp.sum(z * z, axis=-1, keepdims=True) + cos_eps)
    inv_f = lax.rsqrt(jnp.sum(feat * feat, axis=-1, keepdims=True) + cos_eps)
    zf = jnp.sum(z * feat, axis=-1, keepdims=True)
    coeff = -repa_weight * keep_ref[...] * inv_z * inv_f
    gz = (coeff * (feat - (zf * inv_z * inv_z) * z)).astype(BF16)
    gz_ref[...] = gz
    gb3[...] = jnp.sum(gz.astype(F32), axis=0, keepdims=True)
    for lo in range(0, hidden, step):
        g = (dot_nt(gz, w3[lo : lo + step, :]) * silu_slope(a2[:, lo : lo + step])).astype(BF16)
        ga2_ref[:, lo : lo + step] = g
        gb2[:, lo : lo + step] = jnp.sum(g.astype(F32), axis=0, keepdims=True)
    ga2 = ga2_ref[...]
    for lo in range(0, hidden, step):
        g = (dot_nt(ga2, w2[lo : lo + step, :]) * silu_slope(a1[:, lo : lo + step])).astype(BF16)
        ga1_ref[:, lo : lo + step] = g
        gb1[:, lo : lo + step] = jnp.sum(g.astype(F32), axis=0, keepdims=True)
    gh = grad_out[...].astype(F32) + dot_nt(ga1_ref[...], w1[...])
    grad_h[...] = gh
    gm = (gate * gh).astype(BF16)
    g_mlp[...] = gm
    gbf[...] = jnp.sum(gm.astype(F32), axis=0, keepdims=True)
    gate_sum[...] = by_image(seg, gh * mlp, slots)


def second_back_kernel(part, rq, ry, grad_h, h_one, attn, mods, seg_ref, g_one, g_attn, gate_sum, shift_sum, scale_sum, bias):
    width = h_one.shape[1]
    slots = mods.shape[0]
    seg = seg_ref[...]
    g = part[...] + rq[...].astype(F32) + ry[...].astype(F32)
    xhat, inv = norm_parts(h_one[...])
    total = grad_h[...] + norm_back(g * (1.0 + pick(seg, mods[:, 4 * width : 5 * width])), xhat, inv)
    g_one[...] = total
    ga = (pick(seg, mods[:, 2 * width : 3 * width]) * total).astype(BF16)
    g_attn[...] = ga
    bias[...] = jnp.sum(ga.astype(F32), axis=0, keepdims=True)
    gate_sum[...] = by_image(seg, total * attn[...], slots)
    shift_sum[...] = by_image(seg, g, slots)
    scale_sum[...] = by_image(seg, g * xhat, slots)


def first_back_kernel(order, part, rq, ry, g_one, hid, mods, seg_ref, g_in, shift_sum, scale_sum):
    width = g_one.shape[1]
    slots = mods.shape[0]
    seg = seg_ref[...]
    g = part[...] + rq[...].astype(F32) + ry[...].astype(F32)
    xhat, inv = norm_parts(hid[order[0]].astype(F32))
    total = g_one[...] + norm_back(g * (1.0 + pick(seg, mods[:, width : 2 * width])), xhat, inv)
    g_in[...] = total.astype(BF16)
    shift_sum[...] = by_image(seg, g, slots)
    scale_sum[...] = by_image(seg, g * xhat, slots)


def wgrad_kernel(place, n_outs, step, meta, a_ref, b_ref, *refs):
    outs, (g, sem) = refs[:n_outs], refs[n_outs:]
    rows = g.shape[0]
    for lo in range(0, rows, step):
        hi = min(lo + step, rows)
        g[lo:hi, :] = dot_tn(a_ref[:, lo:hi], b_ref[...]).astype(BF16)
    place(g, outs, sem, meta)
    pltpu.make_async_copy(g, g, sem).wait()


def body(mesh, hidden_in, grad_out, features, seg_ids, valid_mask, time_ids, class_ids, class_table, ada_w, ada_b, qkv_w, qv_bias, out_w, out_b, fc1_w, fc1_b, fc2_w, fc2_b, repa_w1, repa_b1, repa_w2, repa_b2, repa_w3, repa_b3):
    n_dp = mesh.shape["dp"]
    inner = 4 if n_dp % 16 == 0 else 2
    outer = n_dp // inner
    micro_count, rows_dev, seq, width = hidden_in.shape
    slots = time_ids.shape[-1]
    images = micro_count * rows_dev * slots
    half = seq // 2
    wide = qkv_w.shape[2]
    heads = wide // HEAD_DIM
    ff = fc1_w.shape[1]
    hidden = repa_w1.shape[1]
    repr_width = repa_w3.shape[1]

    d = lax.axis_index("dp")
    t = lax.axis_index("tensor")
    o, i = d // inner, d % inner
    y, c = t // 2, t % 2
    meta = jnp.stack([o, i, y, c]).astype(jnp.int32)

    def from_inner(x, r):
        return lax.ppermute(x, "dp", [(k * inner + (j + r) % inner, k * inner + j) for k in range(outer) for j in range(inner)])

    def from_outer(x, r):
        return lax.ppermute(x, "dp", [(((k + r) % outer) * inner + j, k * inner + j) for k in range(outer) for j in range(inner)])

    def swap_y(x):
        return lax.ppermute(x, "tensor", [(0, 2), (2, 0), (1, 3), (3, 1)])

    def swap_core(x):
        return lax.ppermute(x, "tensor", [(0, 1), (1, 0), (2, 3), (3, 2)])

    def to_natural(stack, me, n, axis=0):
        twice = jnp.concatenate([stack, stack], axis=axis)
        return lax.dynamic_slice_in_dim(twice, n - me, n, axis=axis)

    def to_relative(stack, me, n, axis=0):
        twice = jnp.concatenate([stack, stack], axis=axis)
        return lax.dynamic_slice_in_dim(twice, me, n, axis=axis)

    def gather_dp(x):
        xs = jnp.stack([x] + [from_inner(x, r) for r in range(1, inner)])
        xs = jnp.stack([xs] + [from_outer(xs, r) for r in range(1, outer)])
        xs = to_natural(to_natural(xs, i, inner, 1), o, outer, 0)
        return xs.reshape((n_dp,) + x.shape)

    def exchange_dp(x):
        x = x.reshape((outer, inner) + x.shape[1:])
        rel = to_relative(x, i, inner, 1)
        ys = jnp.stack([rel[:, 0]] + [from_inner(rel[:, inner - r], r) for r in range(1, inner)])
        rel = to_relative(ys, o, outer, 1)
        zs = jnp.stack([rel[:, 0]] + [from_outer(rel[:, outer - r], r) for r in range(1, outer)])
        zs = to_natural(to_natural(zs, i, inner, 1), o, outer, 0)
        return zs.reshape((n_dp,) + zs.shape[2:])

    def bulk_gather(piece):
        zs = jnp.stack([piece] + [from_outer(piece, r) for r in range(1, outer)])
        xs = [zs] + [from_inner(zs, r) for r in range(1, inner)]
        ys = [swap_y(a) for a in xs]
        found = {}
        for yr, group in ((0, xs), (1, ys)):
            for r, a in enumerate(group):
                found[(yr, 0, r)] = a
                found[(yr, 1, r)] = swap_core(a)
        return found

    def cols_of(w):
        n = w.shape[1] // 4
        return lax.dynamic_slice_in_dim(w, t * n, n, axis=1)

    def rows_of(w):
        n = w.shape[0] // 4
        return lax.dynamic_slice_in_dim(w, t * n, n, axis=0)

    w1_found = bulk_gather(cols_of(repa_w1))
    w3_found = bulk_gather(rows_of(repa_w3))
    w2_found = bulk_gather(cols_of(repa_w2))
    out_y = swap_y(out_w)
    out_c = swap_core(out_w)
    out_yc = swap_core(out_y)
    b_all = gather_dp(jnp.concatenate([repa_b1, repa_b2, repa_b3]))
    n1, n2 = repa_b1.shape[0], repa_b2.shape[0]
    b_one = b_all[:, :n1].reshape(1, -1).astype(F32)
    b_two = b_all[:, n1 : n1 + n2].reshape(1, -1).astype(F32)
    b_three = b_all[:, n1 + n2 :].reshape(1, -1).astype(F32)

    ids = gather_dp(jnp.concatenate([class_ids.reshape(images), time_ids.reshape(images)]))
    all_class = ids[:, :images].reshape(1, n_dp * images)
    all_time = ids[:, images:].reshape(1, n_dp * images)
    feats = class_table.shape[0]
    class_hot = lax.broadcasted_iota(jnp.int32, (class_table.shape[1], n_dp * images), 0) == all_class
    place = d * feats + lax.broadcasted_iota(jnp.int32, (feats, 1), 0)
    half_width = width // 2
    freqs = jnp.exp(-math.log(10000.0) * (place % half_width).astype(F32) / half_width)
    angles = all_time.astype(F32) * freqs
    condition = jnp.where(place < half_width, jnp.cos(angles), jnp.sin(angles)) + dot(class_table, class_hot.astype(BF16))
    cond_act = gather_dp(jax.nn.silu(condition).astype(BF16)).reshape(width, n_dp * images)
    mod_part = lax.dot_general(cond_act, ada_w, (((0,), (1,)), ((), ())), preferred_element_type=F32) + ada_b.astype(F32)
    mod_parts = exchange_dp(mod_part.reshape(n_dp, images, -1))
    modulation = mod_parts.transpose(1, 0, 2).reshape(micro_count, slots, -1)
    mods_own = lax.dynamic_index_in_dim(modulation, c, 0, keepdims=False)
    mods_par = lax.dynamic_index_in_dim(modulation, 1 - c, 0, keepdims=False)

    order = jnp.stack([2 * c + y, 2 * c + 1 - y, 2 * (1 - c) + y, 2 * (1 - c) + 1 - y]).astype(jnp.int32)
    hid = hidden_in.reshape(4, half, width)

    def ordered(a):
        a = a.reshape(4, half)
        return jnp.concatenate([lax.dynamic_index_in_dim(a, order[n], 0, keepdims=False) for n in range(4)])

    seg_line = ordered(seg_ids)
    val_line = ordered(valid_mask)
    seg_rows = seg_line.reshape(2, seq)
    val_rows = val_line.reshape(2, seq)
    seg_cols = seg_line.reshape(2 * seq, 1)
    seg_q = seg_cols[:half]
    keep_q = val_line[:half].reshape(half, 1).astype(F32)
    go_q = lax.dynamic_index_in_dim(grad_out.reshape(4, half, width), order[0], 0, keepdims=False)
    feat_q = lax.dynamic_index_in_dim(features.reshape(4, half, repr_width), order[0], 0, keepdims=False)

    tokens = 2 * seq
    T = tokens

    def fwd(order_, hid_, a, b, *rest):
        return functools.partial(fwd_kernel, heads)(order_, hid_, (a, b), *rest)

    m_one, q, k, v, mixed = call(
        fwd,
        [shape_of((T, width), BF16)] + [shape_of((T, wide), BF16)] * 4,
        [order, hid, mods_own, mods_par, seg_cols, seg_rows, val_rows, qkv_w, qv_bias.astype(F32)],
        in_specs=[SMEM] + [VMEM] * 8,
        flops=2 * T * width * wide * 3 + 4 * T * seq * wide,
        name="attention",
    )

    mix_own, mix_send = mixed[:seq], mixed[seq:]
    mix_y = swap_y(mix_own)
    mix_c = swap_core(mix_send)
    mix_yc = swap_y(mix_c)
    attn_q, h_q, m_two = call(
        mid_kernel,
        [shape_of((half, width), F32), shape_of((half, width), F32), shape_of((seq, width), BF16)],
        [order, hid, mods_own, seg_cols, mix_own, mix_c, mix_y, mix_yc, out_w, out_c, out_y, out_yc, out_b.astype(F32).reshape(1, width)],
        in_specs=[SMEM] + [VMEM] * 12,
        flops=2 * seq * width * width,
        name="middle",
    )
    m_par = swap_core(m_two)

    quarter = [shape_of((half, width), F32), shape_of((half, width), F32), shape_of((half, width), BF16), shape_of((half, width), BF16)]

    def settle_quarter(part_y, send_q, send_y):
        ry = swap_core(send_y)
        rq = swap_core(send_q)
        passed = swap_y((part_y + ry.astype(F32)).astype(BF16))
        return rq, passed

    def spread_quarter(g):
        gy = swap_y(g)
        return g, gy, swap_core(g), swap_core(gy)

    m_full, pre, act, part_q, part_y, send_q, send_y = call(
        mlp_kernel,
        [shape_of((T, width), BF16), shape_of((T, ff), F32), shape_of((T, ff), BF16)] + quarter,
        [m_two, m_par, fc1_w, fc1_b.astype(F32).reshape(1, ff), fc2_w],
        flops=4 * T * width * ff,
        name="mlp",
    )
    rq, ry = settle_quarter(part_y, send_q, send_y)

    def k_of(w):
        return w.shape[0]

    def position(meta_, r, n, zr):
        zo = lax.rem(meta_[0] + zr, outer)
        zi = lax.rem(meta_[1] + r, inner)
        return zo * inner + zi

    def quarter_of(meta_, yr, cr):
        ty = meta_[2] if yr == 0 else 1 - meta_[2]
        tc = meta_[3] if cr == 0 else 1 - meta_[3]
        return ty * 2 + tc

    def col_place(key, depth):
        yr, cr, r = key

        def places(piece, target, meta_):
            n = piece.shape[2]
            col = pl.ds(pl.multiple_of(quarter_of(meta_, yr, cr) * n, 128), n)
            return [
                (piece.at[zr], target.at[pl.ds(pl.multiple_of(position(meta_, r, n, zr) * depth, 16), depth), col])
                for zr in range(outer)
            ]

        return places

    def row_place(key, depth):
        yr, cr, r = key

        def places(piece, target, meta_):
            n = piece.shape[1]
            return [
                (
                    piece.at[zr],
                    target.at[pl.ds(pl.multiple_of(position(meta_, r, n, zr) * depth + quarter_of(meta_, yr, cr) * n, 16), n), :],
                )
                for zr in range(outer)
            ]

        return places

    def whole(piece, target, meta_):
        return [(piece, target)]

    def pair(stack, me, axis):
        first, second = stack
        same = me == 0
        return jnp.concatenate([jnp.where(same, first, second), jnp.where(same, second, first)], axis=axis)

    plan, pieces = [], []
    for which, (found, w, by_cols) in enumerate(((w1_found, repa_w1, True), (w2_found, repa_w2, True), (w3_found, repa_w3, False))):
        depth = k_of(w)
        aligned = depth % 16 == 0 if by_cols else (depth // 4) % 16 == 0
        if aligned:
            for key, a in found.items():
                plan.append((which, (col_place if by_cols else row_place)(key, depth)))
                pieces.append(a)
        else:
            natural = {}
            for yr in range(2):
                for cr in range(2):
                    a = jnp.stack([found[(yr, cr, r)] for r in range(inner)], axis=1)
                    natural[(yr, cr)] = to_natural(to_natural(a, i, inner, 1), o, outer, 0).reshape((n_dp,) + a.shape[2:])
            axis = 2 if by_cols else 1
            cat = pair([pair([natural[(yr, 0)], natural[(yr, 1)]], c, axis) for yr in range(2)], y, axis)
            plan.append((which, whole))
            pieces.append(cat.reshape(n_dp * depth, w.shape[1]))

    small_ins = [part_q, rq, ry, h_q, mods_own, seg_q, fc2_b.astype(F32).reshape(1, width), go_q, feat_q, keep_q, b_one, b_two, b_three]
    h_low, grad_h, g_mlp, gate_two, s_one, s_two, gz, ga_two, ga_one, g_b1, g_b2, g_b3, g_fc2_b = call(
        functools.partial(proj_kernel, plan, len(pieces)),
        [
            shape_of((half, width), BF16),
            shape_of((half, width), F32),
            shape_of((half, width), BF16),
            shape_of((slots, width), F32),
            shape_of((half, hidden), BF16),
            shape_of((half, hidden), BF16),
            shape_of((half, repr_width), BF16),
            shape_of((half, hidden), BF16),
            shape_of((half, hidden), BF16),
            shape_of((1, hidden), F32),
            shape_of((1, hidden), F32),
            shape_of((1, repr_width), F32),
            shape_of((1, width), F32),
        ],
        [meta] + small_ins + pieces,
        in_specs=[SMEM] + [VMEM] * len(small_ins) + [ANY] * len(pieces),
        scratch=[
            pltpu.VMEM((width, hidden), BF16),
            pltpu.VMEM((hidden, hidden), BF16),
            pltpu.VMEM((hidden, repr_width), BF16),
            pltpu.VMEM((half, hidden), F32),
            pltpu.VMEM((half, hidden), F32),
            pltpu.SemaphoreType.DMA((3,)),
        ],
        flops=4 * half * (width * hidden + hidden * hidden + hidden * repr_width),
        name="projector",
    )
    g_mlp_all = spread_quarter(g_mlp)

    def wgrad_dp(a, b, step, name):
        rows, cols = a.shape[1], b.shape[1]
        depth = rows // n_dp
        flops = 2 * a.shape[0] * rows * cols
        scratch = [pltpu.VMEM((rows, cols), BF16), pltpu.SemaphoreType.DMA]
        if depth % 16 == 0:

            def place(g, outs, sem, meta_):
                for r in range(inner):
                    for zr in range(outer):
                        at = position(meta_, r, 0, zr)
                        pltpu.make_async_copy(g.at[pl.ds(pl.multiple_of(at * depth, 16), depth), :], outs[r].at[zr], sem).start()

            return call(
                functools.partial(wgrad_kernel, place, inner, step),
                [shape_of((outer, depth, cols), BF16)] * inner,
                [meta, a, b],
                in_specs=[SMEM, VMEM, VMEM],
                out_specs=[ANY] * inner,
                scratch=scratch,
                flops=flops,
                name=name,
            )

        def place(g, outs, sem, meta_):
            pltpu.make_async_copy(g, outs[0], sem).start()

        (nat,) = call(
            functools.partial(wgrad_kernel, place, 1, step),
            [shape_of((rows, cols), BF16)],
            [meta, a, b],
            in_specs=[SMEM, VMEM, VMEM],
            out_specs=[ANY],
            scratch=scratch,
            flops=flops,
            name=name,
        )
        nat = nat.reshape(outer, inner, depth, cols)
        rel = to_relative(to_relative(nat, i, inner, 1), o, outer, 0)
        return [rel[:, r] for r in range(inner)]

    def reduce_dp(parts):
        v = parts[0].astype(F32)
        for r in range(1, inner):
            v = v + from_inner(parts[inner - r], r).astype(F32)
        out = v[0]
        for r in range(1, outer):
            out = out + from_outer(v[outer - r].astype(BF16), r).astype(F32)
        return out

    def wgrad_all(a, b, by_cols, step, name):
        rows, cols = a.shape[1], b.shape[1]
        depth = rows // n_dp
        rb, cb = (depth, cols // 4) if by_cols else (depth // 4, cols)
        flops = 2 * a.shape[0] * rows * cols
        scratch = [pltpu.VMEM((rows, cols), BF16), pltpu.SemaphoreType.DMA]
        n_outs = 4
        if rb % 16 == 0:

            def place(g, outs, sem, meta_):
                for cr in range(2):
                    for yr in range(2):
                        for r in range(inner):
                            for zr in range(outer):
                                at = position(meta_, r, 0, zr)
                                part = quarter_of(meta_, yr, cr)
                                if by_cols:
                                    source = g.at[pl.ds(pl.multiple_of(at * depth, 16), rb), pl.ds(pl.multiple_of(part * cb, 128), cb)]
                                else:
                                    source = g.at[pl.ds(pl.multiple_of(at * depth + part * rb, 16), rb), :]
                                pltpu.make_async_copy(source, outs[2 * cr + yr].at[r, zr], sem).start()

            keep_q_, keep_y_, send_q_, send_y_ = call(
                functools.partial(wgrad_kernel, place, n_outs, step),
                [shape_of((inner, outer, rb, cb), BF16)] * n_outs,
                [meta, a, b],
                in_specs=[SMEM, VMEM, VMEM],
                out_specs=[ANY] * n_outs,
                scratch=scratch,
                flops=flops,
                name=name,
            )
            return keep_q_, keep_y_, send_q_, send_y_

        def place(g, outs, sem, meta_):
            pltpu.make_async_copy(g, outs[0], sem).start()

        (nat,) = call(
            functools.partial(wgrad_kernel, place, 1, step),
            [shape_of((rows, cols), BF16)],
            [meta, a, b],
            in_specs=[SMEM, VMEM, VMEM],
            out_specs=[ANY],
            scratch=scratch,
            flops=flops,
            name=name,
        )
        if by_cols:
            nat = nat.reshape(outer, inner, rb, 2, 2, cb).transpose(4, 3, 1, 0, 2, 5)
        else:
            nat = nat.reshape(outer, inner, 2, 2, rb, cb).transpose(3, 2, 1, 0, 4, 5)
        rel = to_relative(to_relative(to_relative(to_relative(nat, c, 2, 0), y, 2, 1), i, inner, 2), o, outer, 3)
        return rel[0, 0], rel[0, 1], rel[1, 0], rel[1, 1]

    def reduce_all(parts):
        keep_q_, keep_y_, send_q_, send_y_ = parts
        ry_ = swap_core(send_y_)
        rq_ = swap_core(send_q_)
        passed = swap_y((keep_y_.astype(F32) + ry_.astype(F32)).astype(BF16))
        total = keep_q_.astype(F32) + rq_.astype(F32) + passed.astype(F32)
        rest = [total[0]] + [total[r].astype(BF16) for r in range(1, inner)]
        return reduce_dp(rest)

    def spread_tensor(block, by_cols):
        block = block.astype(BF16)
        axis = 1 if by_cols else 0
        other = swap_y(block)
        c0, c1 = swap_core(block), swap_core(other)
        own = pair([block, c0], c, axis)
        peer = pair([other, c1], c, axis)
        return pair([own, peer], y, axis).astype(F32)

    g_w3 = spread_tensor(reduce_all(wgrad_all(s_two, gz, False, 512, "grad_w3")), False)
    g_w2 = spread_tensor(reduce_all(wgrad_all(s_one, ga_two, True, 256, "grad_w2")), True)
    g_w1 = spread_tensor(reduce_all(wgrad_all(h_low, ga_one, True, 384, "grad_w1")), True)

    g_mlp_full, gpre, part_q, part_y, send_q, send_y, g_fc1_b = call(
        mlp_back_kernel,
        [shape_of((T, width), BF16), shape_of((T, ff), BF16)] + quarter + [shape_of((1, ff), F32)],
        list(g_mlp_all) + [pre, fc1_w, fc2_w],
        flops=4 * T * width * ff,
        name="mlp_back",
    )
    rq, ry = settle_quarter(part_y, send_q, send_y)
    g_one, g_attn, gate_one, shift_two, scale_two, g_out_b = call(
        second_back_kernel,
        [shape_of((half, width), F32), shape_of((half, width), BF16)] + [shape_of((slots, width), F32)] * 3 + [shape_of((1, width), F32)],
        [part_q, rq, ry, grad_h, h_q, attn_q, mods_own, seg_q],
        name="second_back",
    )
    g_attn_all = spread_quarter(g_attn)
    g_fc2_t = reduce_dp(wgrad_dp(g_mlp_full, act, 384, "grad_fc2"))
    g_fc1 = reduce_dp(wgrad_dp(m_full, gpre, 384, "grad_fc1"))

    gqkv, part_q, part_y, send_q, send_y, g_qv_b, g_attn_full = call(
        functools.partial(bwd_kernel, heads),
        [shape_of((T, 3 * wide), BF16)] + quarter + [shape_of((2, wide), F32), shape_of((T, width), BF16)],
        list(g_attn_all) + [out_w, q, k, v, seg_cols, seg_rows, val_rows, qkv_w],
        flops=8 * T * width * wide + 10 * T * seq * wide,
        name="attention_back",
    )
    rq, ry = settle_quarter(part_y, send_q, send_y)
    g_in, shift_one, scale_one = call(
        first_back_kernel,
        [shape_of((half, width), BF16)] + [shape_of((slots, width), F32)] * 2,
        [order, part_q, rq, ry, g_one, hid, mods_own, seg_q],
        in_specs=[SMEM] + [VMEM] * 7,
        name="first_back",
    )
    g_qkv = reduce_dp(wgrad_dp(m_one, gqkv, 384, "grad_qkv"))
    g_out_t = reduce_dp(wgrad_dp(g_attn_full, mixed, 384, "grad_out"))

    g_mod = jnp.concatenate([shift_one, scale_one, gate_one, shift_two, scale_two, gate_two], axis=-1)
    g_mod = (g_mod + swap_y(g_mod)).astype(BF16)
    g_mod = exchange_dp(g_mod.reshape(slots, n_dp, -1).transpose(1, 0, 2))
    g_mod = pair([g_mod, swap_core(g_mod)], c, 1).reshape(n_dp * images, -1)
    g_ada_w = lax.dot_general(g_mod, cond_act, (((0,), (1,)), ((), ())), preferred_element_type=F32)
    g_ada_b = jnp.sum(g_mod.astype(F32), axis=0)
    g_cond = lax.dot_general(ada_w, g_mod, (((0,), (1,)), ((), ())), preferred_element_type=F32)
    g_cond = g_cond.reshape(outer, inner, feats, n_dp * images)
    rel = to_relative(to_relative(g_cond, i, inner, 1), o, outer, 0)
    v_now = rel[:, 0]
    for r in range(1, inner):
        v_now = v_now + from_inner(rel[:, inner - r], r)
    g_cond = v_now[0]
    for r in range(1, outer):
        g_cond = g_cond + from_outer(v_now[outer - r], r)
    g_cond = g_cond * silu_slope(condition)
    g_table = lax.dot_general(
        g_cond, class_hot.astype(F32), (((1,), (1,)), ((), ())), precision=lax.Precision.HIGHEST, preferred_element_type=F32
    )

    def total_dp(x):
        step = 1
        while step < n_dp:
            x = x + lax.ppermute(x, "dp", [(k_, k_ ^ step) for k_ in range(n_dp)])
            step *= 2
        return x

    early = jnp.concatenate([g_b1, g_b2, g_b3, g_fc2_b], axis=1)
    early = early + swap_core(early)
    early = early + swap_y(early)
    early = total_dp(early)
    late_own = g_out_b + swap_core(g_out_b)
    late_own = late_own + swap_y(late_own)
    late = total_dp(jnp.concatenate([g_fc1_b, late_own, g_qv_b.reshape(1, 2 * wide)], axis=1))

    def my_part(x, n):
        return lax.dynamic_slice_in_dim(x.reshape(-1), d * n, n)

    s_b1 = my_part(early[:, :hidden], n1)
    s_b2 = my_part(early[:, hidden : 2 * hidden], n2)
    s_b3 = my_part(early[:, 2 * hidden : 2 * hidden + repr_width], repa_b3.shape[0])
    s_fc2_b = early[0, 2 * hidden + repr_width :]
    s_fc1_b = late[0, :ff]
    s_out_b = late[0, ff : ff + width]
    s_qv_b = late[0, ff + width :].reshape(2, wide)

    def spread_tokens(block):
        other = swap_y(block)
        c0, c1 = swap_core(block), swap_core(other)
        own = pair([block, other], y, 0)
        peer = pair([c0, c1], y, 0)
        return pair([own, peer], c, 0).reshape(micro_count, rows_dev, seq, width)

    block_out = spread_tokens(h_low)
    grad_in = spread_tokens(g_in).astype(F32)
    depth = width // n_dp
    return (
        block_out,
        grad_in,
        g_table,
        g_ada_w,
        g_ada_b,
        jnp.stack([g_qkv[:, :wide], g_qkv[:, wide : 2 * wide], g_qkv[:, 2 * wide :]]),
        s_qv_b,
        g_out_t.T,
        s_out_b,
        g_fc1,
        s_fc1_b,
        g_fc2_t.T,
        s_fc2_b,
        g_w1,
        s_b1,
        g_w2,
        s_b2,
        g_w3,
        s_b3,
    )


def solution(mesh):
    dp, tensor = "dp", "tensor"
    rows4, rows3 = P(None, dp, None, None), P(None, dp, None)
    ins = (rows4, rows4, rows4, rows3, rows3, rows3, rows3, P(dp, None), P(dp, None), P(dp), P(None, None, tensor), P(None, tensor), P(tensor, None), P(), P(None, tensor), P(tensor), P(tensor, None), P(), P(dp, None), P(dp), P(dp, None), P(dp), P(dp, None), P(dp))
    outs = (rows4, rows4, P(dp, None), P(dp, None), P(dp), P(None, dp, tensor), P(None, tensor), P(tensor, dp), P(), P(dp, tensor), P(tensor), P(tensor, dp), P(), P(dp, None), P(dp), P(dp, None), P(dp), P(dp, None), P(dp))
    return jax.shard_map(functools.partial(body, mesh), mesh=mesh, in_specs=ins, out_specs=outs, check_vma=False)
```

```python
import functools
import math

import jax
import jax.numpy as jnp
from jax import lax
from jax.experimental import pallas as pl
from jax.experimental.pallas import tpu as pltpu
from jax.sharding import PartitionSpec as P

HEAD_DIM = 72
norm_eps = 1e-06
cos_eps = 1e-06
repa_weight = 0.5
F32 = jnp.float32
BF16 = jnp.bfloat16
VMEM = pl.BlockSpec(memory_space=pltpu.VMEM)
SMEM = pl.BlockSpec(memory_space=pltpu.SMEM)
ANY = pl.BlockSpec(memory_space=pl.ANY)
VMEM_LIMIT = 58 * 1024 * 1024


def shape_of(shape, dtype):
    return jax.ShapeDtypeStruct(tuple(shape), dtype)


def call(kernel, outs, ins, in_specs=None, out_specs=None, scratch=(), flops=0, limit=VMEM_LIMIT, name=None):
    moved = sum(math.prod(a.shape) * a.dtype.itemsize for a in list(ins) + list(outs))
    return pl.pallas_call(
        kernel,
        out_shape=tuple(outs),
        in_specs=in_specs or [VMEM] * len(ins),
        out_specs=tuple(out_specs or [VMEM] * len(outs)),
        scratch_shapes=list(scratch),
        compiler_params=pltpu.CompilerParams(vmem_limit_bytes=limit),
        cost_estimate=pl.CostEstimate(flops=flops, bytes_accessed=moved, transcendentals=0),
        name=name,
    )(*ins)


def dot(a, b):
    return jnp.dot(a, b, preferred_element_type=F32)


def dot_nt(a, b):
    return lax.dot_general(a, b, (((1,), (1,)), ((), ())), preferred_element_type=F32)


def dot_tn(a, b):
    return lax.dot_general(a, b, (((0,), (0,)), ((), ())), preferred_element_type=F32)


def sigmoid(v):
    return 1.0 / (1.0 + jnp.exp(-v))


def silu_slope(v):
    s = sigmoid(v)
    return s * (1.0 + v * (1.0 - s))


def pick(seg, table):
    out = jnp.broadcast_to(table[0:1, :], (seg.shape[0], table.shape[1]))
    for s in range(1, table.shape[0]):
        out = jnp.where(seg == s, table[s : s + 1, :], out)
    return out


def by_image(seg, values, slots):
    rows = [jnp.sum(jnp.where(seg == s, values, 0.0), axis=0, keepdims=True) for s in range(slots)]
    return jnp.concatenate(rows, axis=0)


def norm_parts(v):
    centered = v - jnp.mean(v, axis=-1, keepdims=True)
    inv = lax.rsqrt(jnp.mean(centered * centered, axis=-1, keepdims=True) + norm_eps)
    return centered * inv, inv


def norm_back(g, xhat, inv):
    return inv * (g - jnp.mean(g, axis=-1, keepdims=True) - xhat * jnp.mean(g * xhat, axis=-1, keepdims=True))


def attend(q, k, v, open_mask, scale):
    s = dot_nt(q, k) * scale
    s = jnp.where(open_mask, s, -1e30)
    e = jnp.exp(s - jnp.max(s, axis=-1, keepdims=True))
    return e * (1.0 / jnp.sum(e, axis=-1, keepdims=True))


def open_of(segc, segr, valr):
    n = segc.shape[0]
    same = lax.broadcasted_iota(jnp.int32, (n, n), 0) == lax.broadcasted_iota(jnp.int32, (n, n), 1)
    return (segc == segr) & ((valr == 1) | same)


def fwd_kernel(heads, order, hid, mods, segc, segr, valr, w, b, m_ref, q_ref, k_ref, v_ref, mix_ref):
    half, width = hid.shape[1], hid.shape[2]
    seq = 2 * half
    scale = HEAD_DIM ** (-0.5)
    for micro in range(2):
        x = jnp.concatenate([hid[order[2 * micro]], hid[order[2 * micro + 1]]], axis=0).astype(F32)
        rows = slice(micro * seq, (micro + 1) * seq)
        seg = segc[rows, :]
        xhat, _ = norm_parts(x)
        shift = pick(seg, mods[micro][:, 0:width])
        scaling = pick(seg, mods[micro][:, width : 2 * width])
        m = (xhat * (1.0 + scaling) + shift).astype(BF16)
        m_ref[rows, :] = m
        q = (dot_nt(m, w[0]) + b[0:1, :]).astype(BF16)
        k = dot_nt(m, w[1]).astype(BF16)
        v = (dot_nt(m, w[2]) + b[1:2, :]).astype(BF16)
        q_ref[rows, :] = q
        k_ref[rows, :] = k
        v_ref[rows, :] = v
        mask = open_of(seg, segr[micro : micro + 1, :], valr[micro : micro + 1, :])
        mixed = []
        for h in range(heads):
            cols = slice(h * HEAD_DIM, (h + 1) * HEAD_DIM)
            p = attend(q[:, cols], k[:, cols], v[:, cols], mask, scale)
            mixed.append(dot(p.astype(BF16), v[:, cols]).astype(BF16))
        mix_ref[rows, :] = jnp.concatenate(mixed, axis=1)


def bwd_kernel(heads, g0, g1, g2, g3, out_w, q_ref, k_ref, v_ref, segc, segr, valr, w, gqkv_ref, part_q, part_y, send_q, send_y, bias_ref, gfull_ref):
    half = g0.shape[0]
    seq = 2 * half
    scale = HEAD_DIM ** (-0.5)
    wide = heads * HEAD_DIM
    sums = []
    for micro in range(2):
        rows = slice(micro * seq, (micro + 1) * seq)
        g = jnp.concatenate([g0[...], g1[...]] if micro == 0 else [g2[...], g3[...]], axis=0)
        gfull_ref[rows, :] = g
        gm = dot_nt(g, out_w[...]).astype(BF16)
        q, k, v = q_ref[rows, :], k_ref[rows, :], v_ref[rows, :]
        mask = open_of(segc[rows, :], segr[micro : micro + 1, :], valr[micro : micro + 1, :])
        gq, gk, gv = [], [], []
        for h in range(heads):
            cols = slice(h * HEAD_DIM, (h + 1) * HEAD_DIM)
            qh, kh, vh, gh = q[:, cols], k[:, cols], v[:, cols], gm[:, cols]
            p = attend(qh, kh, vh, mask, scale)
            gp = dot_nt(gh, vh)
            gs = (p * (gp - jnp.sum(p * gp, axis=-1, keepdims=True))).astype(BF16)
            gq.append((dot(gs, kh) * scale).astype(BF16))
            gk.append((dot_tn(gs, qh) * scale).astype(BF16))
            gv.append(dot_tn(p.astype(BF16), gh).astype(BF16))
        gq, gk, gv = (jnp.concatenate(a, axis=1) for a in (gq, gk, gv))
        gqkv_ref[rows, 0:wide] = gq
        gqkv_ref[rows, wide : 2 * wide] = gk
        gqkv_ref[rows, 2 * wide : 3 * wide] = gv
        sums.append(
            jnp.concatenate(
                [jnp.sum(gq.astype(F32), axis=0, keepdims=True), jnp.sum(gv.astype(F32), axis=0, keepdims=True)],
                axis=0,
            )
        )
        part = dot(gq, w[0]) + dot(gk, w[1]) + dot(gv, w[2])
        if micro == 0:
            part_q[...] = part[:half]
            part_y[...] = part[half:]
        else:
            send_q[...] = part[:half].astype(BF16)
            send_y[...] = part[half:].astype(BF16)
    bias_ref[...] = sums[0] + sums[1]


def mid_kernel(order, hid, mods, segc, m0, m1, m2, m3, w0, w1, w2, w3, out_b, attn_q, h_q, m_two):
    half, width = hid.shape[1], hid.shape[2]
    seq = 2 * half
    x = jnp.concatenate([hid[order[0]], hid[order[1]]], axis=0).astype(F32)
    seg = segc[0:seq, :]
    m2, m3 = (jnp.concatenate([m[half:, :], m[:half, :]], axis=0) for m in (m2, m3))
    attn = dot(m0[...], w0[...]) + dot(m1[...], w1[...]) + dot(m2, w2[...]) + dot(m3, w3[...])
    attn = attn + out_b[...]
    h = x + pick(seg, mods[:, 2 * width : 3 * width]) * attn
    attn_q[...] = attn[:half]
    h_q[...] = h[:half]
    xhat, _ = norm_parts(h)
    m_two[...] = (
        xhat * (1.0 + pick(seg, mods[:, 4 * width : 5 * width])) + pick(seg, mods[:, 3 * width : 4 * width])
    ).astype(BF16)


SPLITS = ((0, 512), (512, 1152))
K0 = math.sqrt(2.0 / math.pi)


def mlp_kernel(m_own, m_par, fc1, b1, fc2, m_full, pre_ref, act_ref, part_q, part_y, send_q, send_y):
    seq = m_own.shape[0]
    half = seq // 2
    for micro, m_ref in enumerate((m_own, m_par)):
        rows = slice(micro * seq, (micro + 1) * seq)
        m = m_ref[...]
        m_full[rows, :] = m
        for lo, hi in SPLITS:
            pre = dot(m, fc1[:, lo:hi]) + b1[:, lo:hi]
            pre_ref[rows, lo:hi] = pre
            t = jnp.tanh(K0 * (pre + 0.044715 * (pre * pre * pre)))
            act_ref[rows, lo:hi] = (0.5 * pre * (1.0 + t)).astype(BF16)
        act = act_ref[rows, :]
        for lo, hi in SPLITS:
            part = dot(act, fc2[:, lo:hi])
            if micro == 0:
                part_q[:, lo:hi] = part[:half]
                part_y[:, lo:hi] = part[half:]
            else:
                send_q[:, lo:hi] = part[:half].astype(BF16)
                send_y[:, lo:hi] = part[half:].astype(BF16)


def mlp_back_kernel(g0, g1, g2, g3, pre_ref, fc1, fc2, g_full, gpre_ref, part_q, part_y, send_q, send_y, bias):
    half = g0.shape[0]
    seq = 2 * half
    for micro in range(2):
        rows = slice(micro * seq, (micro + 1) * seq)
        g = jnp.concatenate([g0[...], g1[...]] if micro == 0 else [g2[...], g3[...]], axis=0)
        g_full[rows, :] = g
        for lo, hi in SPLITS:
            ga = dot_nt(g, fc2[lo:hi, :])
            v = pre_ref[rows, lo:hi]
            t = jnp.tanh(K0 * (v + 0.044715 * (v * v * v)))
            slope = 0.5 * (1.0 + t) + 0.5 * v * (1.0 - t * t) * (K0 * (1.0 + 3.0 * 0.044715 * (v * v)))
            gp = (ga * slope).astype(BF16)
            gpre_ref[rows, lo:hi] = gp
            total = jnp.sum(gp.astype(F32), axis=0, keepdims=True)
            bias[:, lo:hi] = total if micro == 0 else bias[:, lo:hi] + total
        gp = gpre_ref[rows, :]
        for lo, hi in SPLITS:
            part = dot_nt(gp, fc1[lo:hi, :])
            if micro == 0:
                part_q[:, lo:hi] = part[:half]
                part_y[:, lo:hi] = part[half:]
            else:
                send_q[:, lo:hi] = part[:half].astype(BF16)
                send_y[:, lo:hi] = part[half:].astype(BF16)


def proj_kernel(plan, n_pieces, *refs):
    (part, rq, ry, h_one, mods, seg_ref, fc2_b, grad_out, feat_ref, keep_ref, b1, b2, b3) = refs[:13]
    pieces = refs[13 : 13 + n_pieces]
    (h_low, grad_h, g_mlp, gate_sum, s1, s2, gz_ref, ga2_ref, ga1_ref, gb1, gb2, gb3, gbf) = refs[13 + n_pieces : 26 + n_pieces]
    w1, w2, w3, a1, a2, sems = refs[26 + n_pieces :]
    weights = (w1, w2, w3)
    width = h_low.shape[1]
    slots = mods.shape[0]
    for which, load in enumerate(plan):
        for source, target in load(pieces, weights[which]):
            pltpu.make_async_copy(source, target, sems.at[which]).start()
    seg = seg_ref[...]
    gate = pick(seg, mods[:, 5 * width : 6 * width])
    mlp = part[...] + rq[...].astype(F32) + ry[...].astype(F32) + fc2_b[...]
    h = h_one[...] + gate * mlp
    hl = h.astype(BF16)
    h_low[...] = hl
    hidden = w1.shape[1]
    step = 512
    pltpu.make_async_copy(w1, w1, sems.at[0]).wait()
    for lo in range(0, hidden, step):
        a = dot(hl, w1[:, lo : lo + step]) + b1[:, lo : lo + step]
        a1[:, lo : lo + step] = a
        s1[:, lo : lo + step] = (a * sigmoid(a)).astype(BF16)
    pltpu.make_async_copy(w2, w2, sems.at[1]).wait()
    s = s1[...]
    for lo in range(0, hidden, step):
        a = dot(s, w2[:, lo : lo + step]) + b2[:, lo : lo + step]
        a2[:, lo : lo + step] = a
        s2[:, lo : lo + step] = (a * sigmoid(a)).astype(BF16)
    pltpu.make_async_copy(w3, w3, sems.at[2]).wait()
    z = dot(s2[...], w3[...]) + b3[...]
    feat = feat_ref[...].astype(F32)
    inv_z = lax.rsqrt(jnp.sum(z * z, axis=-1, keepdims=True) + cos_eps)
    inv_f = lax.rsqrt(jnp.sum(feat * feat, axis=-1, keepdims=True) + cos_eps)
    zf = jnp.sum(z * feat, axis=-1, keepdims=True)
    coeff = -repa_weight * keep_ref[...] * inv_z * inv_f
    gz = (coeff * (feat - (zf * inv_z * inv_z) * z)).astype(BF16)
    gz_ref[...] = gz
    gb3[...] = jnp.sum(gz.astype(F32), axis=0, keepdims=True)
    for lo in range(0, hidden, step):
        g = (dot_nt(gz, w3[lo : lo + step, :]) * silu_slope(a2[:, lo : lo + step])).astype(BF16)
        ga2_ref[:, lo : lo + step] = g
        gb2[:, lo : lo + step] = jnp.sum(g.astype(F32), axis=0, keepdims=True)
    ga2 = ga2_ref[...]
    for lo in range(0, hidden, step):
        g = (dot_nt(ga2, w2[lo : lo + step, :]) * silu_slope(a1[:, lo : lo + step])).astype(BF16)
        ga1_ref[:, lo : lo + step] = g
        gb1[:, lo : lo + step] = jnp.sum(g.astype(F32), axis=0, keepdims=True)
    gh = grad_out[...].astype(F32) + dot_nt(ga1_ref[...], w1[...])
    grad_h[...] = gh
    gm = (gate * gh).astype(BF16)
    g_mlp[...] = gm
    gbf[...] = jnp.sum(gm.astype(F32), axis=0, keepdims=True)
    gate_sum[...] = by_image(seg, gh * mlp, slots)


def second_back_kernel(part, rq, ry, grad_h, h_one, attn, mods, seg_ref, g_one, g_attn, gate_sum, shift_sum, scale_sum, bias):
    width = h_one.shape[1]
    slots = mods.shape[0]
    seg = seg_ref[...]
    g = part[...] + rq[...].astype(F32) + ry[...].astype(F32)
    xhat, inv = norm_parts(h_one[...])
    total = grad_h[...] + norm_back(g * (1.0 + pick(seg, mods[:, 4 * width : 5 * width])), xhat, inv)
    g_one[...] = total
    ga = (pick(seg, mods[:, 2 * width : 3 * width]) * total).astype(BF16)
    g_attn[...] = ga
    bias[...] = jnp.sum(ga.astype(F32), axis=0, keepdims=True)
    gate_sum[...] = by_image(seg, total * attn[...], slots)
    shift_sum[...] = by_image(seg, g, slots)
    scale_sum[...] = by_image(seg, g * xhat, slots)


def first_back_kernel(order, part, rq, ry, g_one, hid, mods, seg_ref, g_in, shift_sum, scale_sum):
    width = g_one.shape[1]
    slots = mods.shape[0]
    seg = seg_ref[...]
    g = part[...] + rq[...].astype(F32) + ry[...].astype(F32)
    xhat, inv = norm_parts(hid[order[0]].astype(F32))
    total = g_one[...] + norm_back(g * (1.0 + pick(seg, mods[:, width : 2 * width])), xhat, inv)
    g_in[...] = total.astype(BF16)
    shift_sum[...] = by_image(seg, g, slots)
    scale_sum[...] = by_image(seg, g * xhat, slots)


def wgrad_kernel(place, jobs, n_outs, *refs):
    meta = refs[0]
    n_ins = 1 + max(max(a, b) for a, b, _ in jobs)
    ins, outs, (*results, sem) = refs[1 : 1 + n_ins], refs[1 + n_ins : 1 + n_ins + n_outs], refs[1 + n_ins + n_outs :]
    for n, (a, b, step) in enumerate(jobs):
        g = results[n]
        rows = g.shape[0]
        for lo in range(0, rows, step):
            hi = min(lo + step, rows)
            g[lo:hi, :] = dot_tn(ins[a][:, lo:hi], ins[b][...]).astype(BF16)
        for source, target in place(n, g, outs, meta):
            pltpu.make_async_copy(source, target, sem.at[n]).start()
    for n, g in enumerate(results):
        pltpu.make_async_copy(g, g, sem.at[n]).wait()


def body(mesh, hidden_in, grad_out, features, seg_ids, valid_mask, time_ids, class_ids, class_table, ada_w, ada_b, qkv_w, qv_bias, out_w, out_b, fc1_w, fc1_b, fc2_w, fc2_b, repa_w1, repa_b1, repa_w2, repa_b2, repa_w3, repa_b3):
    n_dp = mesh.shape["dp"]
    inner = 4 if n_dp % 16 == 0 else 2
    outer = n_dp // inner
    micro_count, rows_dev, seq, width = hidden_in.shape
    slots = time_ids.shape[-1]
    images = micro_count * rows_dev * slots
    half = seq // 2
    wide = qkv_w.shape[2]
    qkv_t = qkv_w.transpose(0, 2, 1)
    heads = wide // HEAD_DIM
    ff = fc1_w.shape[1]
    hidden = repa_w1.shape[1]
    repr_width = repa_w3.shape[1]

    d = lax.axis_index("dp")
    t = lax.axis_index("tensor")
    o, i = d // inner, d % inner
    y, c = t // 2, t % 2
    meta = jnp.stack([o, i, y, c]).astype(jnp.int32)

    def from_inner(x, r):
        return lax.ppermute(x, "dp", [(k * inner + (j + r) % inner, k * inner + j) for k in range(outer) for j in range(inner)])

    def from_outer(x, r):
        return lax.ppermute(x, "dp", [(((k + r) % outer) * inner + j, k * inner + j) for k in range(outer) for j in range(inner)])

    def swap_y(x):
        return lax.ppermute(x, "tensor", [(0, 2), (2, 0), (1, 3), (3, 1)])

    def swap_core(x):
        return lax.ppermute(x, "tensor", [(0, 1), (1, 0), (2, 3), (3, 2)])

    def to_natural(stack, me, n, axis=0):
        twice = jnp.concatenate([stack, stack], axis=axis)
        return lax.dynamic_slice_in_dim(twice, n - me, n, axis=axis)

    def to_relative(stack, me, n, axis=0):
        twice = jnp.concatenate([stack, stack], axis=axis)
        return lax.dynamic_slice_in_dim(twice, me, n, axis=axis)

    def gather_dp(x):
        xs = jnp.stack([x] + [from_inner(x, r) for r in range(1, inner)])
        xs = jnp.stack([xs] + [from_outer(xs, r) for r in range(1, outer)])
        xs = to_natural(to_natural(xs, i, inner, 1), o, outer, 0)
        return xs.reshape((n_dp,) + x.shape)

    def exchange_dp(x):
        x = x.reshape((outer, inner) + x.shape[1:])
        rel = to_relative(x, i, inner, 1)
        ys = jnp.stack([rel[:, 0]] + [from_inner(rel[:, inner - r], r) for r in range(1, inner)])
        rel = to_relative(ys, o, outer, 1)
        zs = jnp.stack([rel[:, 0]] + [from_outer(rel[:, outer - r], r) for r in range(1, outer)])
        zs = to_natural(to_natural(zs, i, inner, 1), o, outer, 0)
        return zs.reshape((n_dp,) + zs.shape[2:])

    def cols_of(w):
        n = w.shape[1] // 4
        return lax.dynamic_slice_in_dim(w, t * n, n, axis=1)

    def rows_of(w):
        n = w.shape[0] // 4
        return lax.dynamic_slice_in_dim(w, t * n, n, axis=0)

    k1, k2, k3 = repa_w1.shape[0], repa_w2.shape[0], repa_w3.shape[0]
    block = hidden // 4
    r3 = k3 // 4
    folds = repr_width * r3 // block
    third = rows_of(repa_w3)

    def fold(w):
        left, right = w[:, :block], w[:, block:]
        n = right.shape[0] // 2
        return jnp.concatenate([left, jnp.concatenate([right[:n], right[n:]], axis=1)], axis=0)

    def unfold(w):
        n = w.shape[-2] * 2 // 3
        left, low = w[..., :n, :], w[..., n:, :]
        m = block // 2
        return jnp.concatenate([left, jnp.concatenate([low[..., :m], low[..., m:]], axis=-2)], axis=-1)

    packed = jnp.concatenate([cols_of(repa_w2), fold(third), cols_of(repa_w1)], axis=0)
    gathered = lax.all_gather(packed, ("dp", "tensor"), axis=0)
    off3, off1 = k2, k2 + folds
    out_y = swap_y(out_w)
    out_c = swap_core(out_w)
    out_yc = swap_core(out_y)
    n1, n2, n3 = repa_b1.shape[0], repa_b2.shape[0], repa_b3.shape[0]

    ids = gather_dp(jnp.concatenate([class_ids.reshape(images), time_ids.reshape(images)]))
    all_class = ids[:, :images].reshape(1, n_dp * images)
    all_time = ids[:, images:].reshape(1, n_dp * images)
    feats = class_table.shape[0]
    class_hot = lax.broadcasted_iota(jnp.int32, (class_table.shape[1], n_dp * images), 0) == all_class
    place = d * feats + lax.broadcasted_iota(jnp.int32, (feats, 1), 0)
    half_width = width // 2
    freqs = jnp.exp(-math.log(10000.0) * (place % half_width).astype(F32) / half_width)
    angles = all_time.astype(F32) * freqs
    condition = jnp.where(place < half_width, jnp.cos(angles), jnp.sin(angles)) + dot(class_table, class_hot.astype(BF16))
    n_images = n_dp * images
    biases = jnp.concatenate([repa_b1, repa_b2, repa_b3])
    lines = -(-biases.shape[0] // n_images)
    biases = jnp.pad(biases, (0, lines * n_images - biases.shape[0])).reshape(lines, n_images)
    found = gather_dp(jnp.concatenate([jax.nn.silu(condition).astype(BF16), biases], axis=0))
    cond_act = found[:, :feats].reshape(width, n_images)
    b_all = found[:, feats:].reshape(n_dp, -1)
    b_one = b_all[:, :n1].reshape(1, -1).astype(F32)
    b_two = b_all[:, n1 : n1 + n2].reshape(1, -1).astype(F32)
    b_three = b_all[:, n1 + n2 : n1 + n2 + n3].reshape(1, -1).astype(F32)
    mod_part = lax.dot_general(cond_act, ada_w, (((0,), (1,)), ((), ())), preferred_element_type=F32) + ada_b.astype(F32)
    mod_parts = exchange_dp(mod_part.reshape(n_dp, images, -1))
    modulation = mod_parts.transpose(1, 0, 2).reshape(micro_count, slots, -1)
    mods_own = lax.dynamic_index_in_dim(modulation, c, 0, keepdims=False)
    mods_par = lax.dynamic_index_in_dim(modulation, 1 - c, 0, keepdims=False)

    order = jnp.stack([2 * c + y, 2 * c + 1 - y, 2 * (1 - c) + y, 2 * (1 - c) + 1 - y]).astype(jnp.int32)
    hid = hidden_in.reshape(4, half, width)

    def ordered(a):
        a = a.reshape(4, half)
        return jnp.concatenate([lax.dynamic_index_in_dim(a, order[n], 0, keepdims=False) for n in range(4)])

    seg_line = ordered(seg_ids)
    val_line = ordered(valid_mask)
    seg_rows = seg_line.reshape(2, seq)
    val_rows = val_line.reshape(2, seq)
    seg_cols = seg_line.reshape(2 * seq, 1)
    seg_q = seg_cols[:half]
    keep_q = val_line[:half].reshape(half, 1).astype(F32)
    go_q = lax.dynamic_index_in_dim(grad_out.reshape(4, half, width), order[0], 0, keepdims=False)
    feat_q = lax.dynamic_index_in_dim(features.reshape(4, half, repr_width), order[0], 0, keepdims=False)

    tokens = 2 * seq
    T = tokens

    def fwd(order_, hid_, a, b, *rest):
        return functools.partial(fwd_kernel, heads)(order_, hid_, (a, b), *rest)

    m_one, q, k, v, mixed = call(
        fwd,
        [shape_of((T, width), BF16)] + [shape_of((T, wide), BF16)] * 4,
        [order, hid, mods_own, mods_par, seg_cols, seg_rows, val_rows, qkv_t, qv_bias.astype(F32)],
        in_specs=[SMEM] + [VMEM] * 8,
        flops=2 * T * width * wide * 3 + 4 * T * seq * wide,
        name="attention",
    )

    mix_own, mix_send = mixed[:seq], mixed[seq:]
    mix_y = swap_y(mix_own)
    mix_c = swap_core(mix_send)
    mix_yc = swap_y(mix_c)
    attn_q, h_q, m_two = call(
        mid_kernel,
        [shape_of((half, width), F32), shape_of((half, width), F32), shape_of((seq, width), BF16)],
        [order, hid, mods_own, seg_cols, mix_own, mix_c, mix_y, mix_yc, out_w, out_c, out_y, out_yc, out_b.astype(F32).reshape(1, width)],
        in_specs=[SMEM] + [VMEM] * 12,
        flops=2 * seq * width * width,
        name="middle",
    )
    m_par = swap_core(m_two)

    quarter = [shape_of((half, width), F32), shape_of((half, width), F32), shape_of((half, width), BF16), shape_of((half, width), BF16)]

    def settle_quarter(part_y, send_q, send_y):
        ry = swap_core(send_y)
        rq = swap_core(send_q)
        passed = swap_y((part_y + ry.astype(F32)).astype(BF16))
        return rq, passed

    def spread_quarter(g):
        gy = swap_y(g)
        return g, gy, swap_core(g), swap_core(gy)

    m_full, pre, act, part_q, part_y, send_q, send_y = call(
        mlp_kernel,
        [shape_of((T, width), BF16), shape_of((T, ff), F32), shape_of((T, ff), BF16)] + quarter,
        [m_two, m_par, fc1_w, fc1_b.astype(F32).reshape(1, ff), fc2_w],
        flops=4 * T * width * ff,
        name="mlp",
    )
    rq, ry = settle_quarter(part_y, send_q, send_y)

    def k_of(w):
        return w.shape[0]

    def position(meta_, r, n, zr):
        zo = lax.rem(meta_[0] + zr, outer)
        zi = lax.rem(meta_[1] + r, inner)
        return zo * inner + zi

    def quarter_of(meta_, yr, cr):
        ty = meta_[2] if yr == 0 else 1 - meta_[2]
        tc = meta_[3] if cr == 0 else 1 - meta_[3]
        return ty * 2 + tc

    def pair(stack, me, axis):
        first, second = stack
        same = me == 0
        return jnp.concatenate([jnp.where(same, first, second), jnp.where(same, second, first)], axis=axis)

    aligned = k1 % 16 == 0 and k2 % 16 == 0 and r3 % 32 == 0
    n_all = 4 * n_dp

    def load_two(refs, target):
        for s in range(n_all):
            at, part = s // 4, s % 4
            yield refs[0].at[s, 0:k2, :], target.at[at * k2 : (at + 1) * k2, part * block : (part + 1) * block]

    def load_one(refs, target):
        for s in range(n_all):
            at, part = s // 4, s % 4
            yield refs[0].at[s, off1 : off1 + k1, :], target.at[at * k1 : (at + 1) * k1, part * block : (part + 1) * block]

    def load_three(refs, target):
        n, m = r3 // 2, block // 2
        for s in range(n_all):
            top = (s // 4) * k3 + (s % 4) * r3
            yield refs[0].at[s, off3 : off3 + r3, :], target.at[top : top + r3, 0:block]
            yield refs[0].at[s, off3 + r3 : off3 + r3 + n, 0:m], target.at[top : top + n, block : block + m]
            yield refs[0].at[s, off3 + r3 : off3 + r3 + n, m : 2 * m], target.at[top + n : top + r3, block : block + m]

    def whole(n):
        def load(refs, target):
            yield refs[n], target

        return load

    if aligned:
        pieces = [gathered]
        plan = [load_one, load_two, load_three]
    else:
        by_cols = lambda a: a.reshape(n_dp, 4, -1, block).transpose(0, 2, 1, 3).reshape(-1, hidden)
        pieces = [by_cols(gathered[:, off1:]), by_cols(gathered[:, :off3]), unfold(gathered[:, off3:off1]).reshape(hidden, repr_width)]
        plan = [whole(0), whole(1), whole(2)]

    small_ins = [part_q, rq, ry, h_q, mods_own, seg_q, fc2_b.astype(F32).reshape(1, width), go_q, feat_q, keep_q, b_one, b_two, b_three]
    h_low, grad_h, g_mlp, gate_two, s_one, s_two, gz, ga_two, ga_one, g_b1, g_b2, g_b3, g_fc2_b = call(
        functools.partial(proj_kernel, plan, len(pieces)),
        [
            shape_of((half, width), BF16),
            shape_of((half, width), F32),
            shape_of((half, width), BF16),
            shape_of((slots, width), F32),
            shape_of((half, hidden), BF16),
            shape_of((half, hidden), BF16),
            shape_of((half, repr_width), BF16),
            shape_of((half, hidden), BF16),
            shape_of((half, hidden), BF16),
            shape_of((1, hidden), F32),
            shape_of((1, hidden), F32),
            shape_of((1, repr_width), F32),
            shape_of((1, width), F32),
        ],
        small_ins + pieces,
        in_specs=[VMEM] * len(small_ins) + [ANY] * len(pieces),
        scratch=[
            pltpu.VMEM((width, hidden), BF16),
            pltpu.VMEM((hidden, hidden), BF16),
            pltpu.VMEM((hidden, repr_width), BF16),
            pltpu.VMEM((half, hidden), F32),
            pltpu.VMEM((half, hidden), F32),
            pltpu.SemaphoreType.DMA((3,)),
        ],
        flops=4 * half * (width * hidden + hidden * hidden + hidden * repr_width),
        name="projector",
    )
    g_mlp_all = spread_quarter(g_mlp)

    def wgrad(place, jobs, ins, outs, name):
        shapes = [(ins[a].shape[1], ins[b].shape[1]) for a, b, _ in jobs]
        return call(
            functools.partial(wgrad_kernel, place, jobs, len(outs)),
            outs,
            [meta] + ins,
            in_specs=[SMEM] + [VMEM] * len(ins),
            out_specs=[ANY] * len(outs),
            scratch=[pltpu.VMEM(s, BF16) for s in shapes] + [pltpu.SemaphoreType.DMA((len(jobs),))],
            flops=sum(2 * ins[a].shape[0] * r * n for (a, _, _), (r, n) in zip(jobs, shapes)),
            name=name,
        )

    def wgrad_natural(jobs, ins, name):
        outs = [shape_of((ins[a].shape[1], ins[b].shape[1]), BF16) for a, b, _ in jobs]
        return wgrad(lambda n, g, outs_, meta_: [(g, outs_[n])], jobs, ins, outs, name)

    def wgrad_dp(jobs, ins, name):
        rows = ins[jobs[0][0]].shape[1]
        widths = [ins[b].shape[1] for _, b, _ in jobs]
        depth = rows // n_dp
        if depth % 16 == 0 and all(w % 128 == 0 for w in widths[:-1]):

            def place(n, g, outs, meta_):
                lo = sum(widths[:n])
                for r in range(inner):
                    for zr in range(outer):
                        at = pl.multiple_of(position(meta_, r, 0, zr) * depth, 16)
                        yield g.at[pl.ds(at, depth), :], outs[r].at[zr, :, lo : lo + widths[n]]

            return wgrad(place, jobs, ins, [shape_of((outer, depth, sum(widths)), BF16)] * inner, name)
        nat = jnp.concatenate(wgrad_natural(jobs, ins, name), axis=1).reshape(outer, inner, depth, sum(widths))
        rel = to_relative(to_relative(nat, i, inner, 1), o, outer, 0)
        return [rel[:, r] for r in range(inner)]

    def reduce_dp(parts):
        v = parts[0].astype(F32)
        for r in range(1, inner):
            v = v + from_inner(parts[inner - r], r).astype(F32)
        out = v[0]
        for r in range(1, outer):
            out = out + from_outer(v[outer - r].astype(BF16), r).astype(F32)
        return out

    def relative_all(nat):
        nat = nat.transpose((3, 2, 1, 0) + tuple(range(4, nat.ndim)))
        return to_relative(to_relative(to_relative(to_relative(nat, c, 2, 0), y, 2, 1), i, inner, 2), o, outer, 3)

    def wgrad_two():
        jobs = [(0, 1, 256)]
        ins = [s_one, ga_two]
        shape = (2, inner, outer, k2, block)
        if aligned:

            def place(n, g, outs, meta_):
                for cr in range(2):
                    for yr in range(2):
                        part = pl.multiple_of(quarter_of(meta_, yr, cr) * block, 128)
                        for r in range(inner):
                            for zr in range(outer):
                                at = pl.multiple_of(position(meta_, r, 0, zr) * k2, 16)
                                yield g.at[pl.ds(at, k2), pl.ds(part, block)], outs[cr].at[yr, r, zr]

            return wgrad(place, jobs, ins, [shape_of(shape, BF16)] * 2, "grad_w2")
        (nat,) = wgrad_natural(jobs, ins, "grad_w2")
        rel = relative_all(nat.reshape(outer, inner, k2, 2, 2, block).transpose(0, 1, 3, 4, 2, 5))
        return rel[0], rel[1]

    def wgrad_others():
        jobs = [(0, 1, 512), (2, 3, 384)]
        ins = [s_two, gz, h_low, ga_one]
        shape = (2, inner, outer, folds + k1, block)
        if aligned:
            half3, half_block = r3 // 2, block // 2

            def place(n, g, outs, meta_):
                for cr in range(2):
                    for yr in range(2):
                        for r in range(inner):
                            for zr in range(outer):
                                part = quarter_of(meta_, yr, cr)
                                at = position(meta_, r, 0, zr)
                                to = outs[cr].at[yr, r, zr]
                                if n == 1:
                                    col = pl.ds(pl.multiple_of(part * block, 128), block)
                                    yield g.at[pl.ds(pl.multiple_of(at * k1, 16), k1), col], to.at[folds : folds + k1, :]
                                    continue
                                top = pl.multiple_of(at * k3 + part * r3, 16)
                                yield g.at[pl.ds(top, r3), 0:block], to.at[0:r3, :]
                                yield g.at[pl.ds(top, half3), block : block + half_block], to.at[r3 : r3 + half3, 0:half_block]
                                low = pl.multiple_of(at * k3 + part * r3 + half3, 16)
                                yield g.at[pl.ds(low, half3), block : block + half_block], to.at[r3 : r3 + half3, half_block:block]

            return wgrad(place, jobs, ins, [shape_of(shape, BF16)] * 2, "grad_w13")
        three, one = wgrad_natural(jobs, ins, "grad_w13")
        left, right = three[:, :block].reshape(n_all, r3, block), three[:, block:].reshape(n_all, 2, r3 // 2, block // 2)
        low = jnp.concatenate([right[:, 0], right[:, 1]], axis=-1)
        three = jnp.concatenate([left, low], axis=1).reshape(outer, inner, 2, 2, folds, block)
        one = one.reshape(outer, inner, k1, 2, 2, block).transpose(0, 1, 3, 4, 2, 5)
        rel = relative_all(jnp.concatenate([three, one], axis=4))
        return rel[0], rel[1]

    def reduce_all(parts):
        keep, send = parts
        got = swap_core(send)
        passed = swap_y((keep[1].astype(F32) + got[1].astype(F32)).astype(BF16))
        total = keep[0].astype(F32) + got[0].astype(F32) + passed.astype(F32)
        return reduce_dp([total[0]] + [total[r].astype(BF16) for r in range(1, inner)])

    def quarters(mine):
        mine = mine.astype(BF16)
        other = swap_y(mine)
        c0, c1 = swap_core(mine), swap_core(other)
        own = pair([mine[None], c0[None]], c, 0)
        peer = pair([other[None], c1[None]], c, 0)
        return pair([own, peer], y, 0)

    def side_by_side(q):
        return jnp.concatenate([q[n] for n in range(4)], axis=1).astype(F32)

    q2 = quarters(reduce_all(wgrad_two()))
    g_w2 = side_by_side(q2)
    q13 = quarters(reduce_all(wgrad_others()))
    g_w1 = side_by_side(q13[:, folds:])
    g_w3 = unfold(q13[:, :folds]).reshape(k3, repr_width).astype(F32)

    g_mlp_full, gpre, part_q, part_y, send_q, send_y, g_fc1_b = call(
        mlp_back_kernel,
        [shape_of((T, width), BF16), shape_of((T, ff), BF16)] + quarter + [shape_of((1, ff), F32)],
        list(g_mlp_all) + [pre, fc1_w, fc2_w],
        flops=4 * T * width * ff,
        name="mlp_back",
    )
    rq, ry = settle_quarter(part_y, send_q, send_y)
    g_one, g_attn, gate_one, shift_two, scale_two, g_out_b = call(
        second_back_kernel,
        [shape_of((half, width), F32), shape_of((half, width), BF16)] + [shape_of((slots, width), F32)] * 3 + [shape_of((1, width), F32)],
        [part_q, rq, ry, grad_h, h_q, attn_q, mods_own, seg_q],
        name="second_back",
    )
    g_attn_all = spread_quarter(g_attn)
    g_fc = reduce_dp(wgrad_dp([(0, 1, 384), (2, 3, 384)], [g_mlp_full, act, m_full, gpre], "grad_fc"))
    g_fc2_t, g_fc1 = g_fc[:, :ff], g_fc[:, ff:]

    gqkv, part_q, part_y, send_q, send_y, g_qv_b, g_attn_full = call(
        functools.partial(bwd_kernel, heads),
        [shape_of((T, 3 * wide), BF16)] + quarter + [shape_of((2, wide), F32), shape_of((T, width), BF16)],
        list(g_attn_all) + [out_w, q, k, v, seg_cols, seg_rows, val_rows, qkv_t],
        flops=8 * T * width * wide + 10 * T * seq * wide,
        name="attention_back",
    )
    rq, ry = settle_quarter(part_y, send_q, send_y)
    g_in, shift_one, scale_one = call(
        first_back_kernel,
        [shape_of((half, width), BF16)] + [shape_of((slots, width), F32)] * 2,
        [order, part_q, rq, ry, g_one, hid, mods_own, seg_q],
        in_specs=[SMEM] + [VMEM] * 7,
        name="first_back",
    )
    g_heads = reduce_dp(wgrad_dp([(0, 1, 384)], [m_one, gqkv], "grad_qkv"))
    g_qkv = g_heads
    g_out_t = reduce_dp(wgrad_dp([(0, 1, 384)], [g_attn_full, mixed], "grad_out"))

    g_mod = jnp.concatenate([shift_one, scale_one, gate_one, shift_two, scale_two, gate_two], axis=-1)
    early = jnp.concatenate([g_b1, g_b2, g_b3, g_fc2_b, g_out_b], axis=1)
    early = early + swap_core(early)
    both = jnp.concatenate([g_mod.reshape(1, -1), early], axis=1)
    both = both + swap_y(both)
    g_mod, early = both[:, : slots * 6 * width].reshape(slots, -1).astype(BF16), both[:, slots * 6 * width :]
    g_mod = exchange_dp(g_mod.reshape(slots, n_dp, -1).transpose(1, 0, 2))
    g_mod = pair([g_mod, swap_core(g_mod)], c, 1).reshape(n_dp * images, -1)
    g_ada_w = lax.dot_general(g_mod, cond_act, (((0,), (1,)), ((), ())), preferred_element_type=F32)
    g_ada_b = jnp.sum(g_mod.astype(F32), axis=0)
    g_cond = lax.dot_general(ada_w, g_mod, (((0,), (1,)), ((), ())), preferred_element_type=F32)
    g_cond = g_cond.reshape(outer, inner, feats, n_dp * images)
    rel = to_relative(to_relative(g_cond, i, inner, 1), o, outer, 0)
    v_now = rel[:, 0]
    for r in range(1, inner):
        v_now = v_now + from_inner(rel[:, inner - r], r)
    g_cond = v_now[0]
    for r in range(1, outer):
        g_cond = g_cond + from_outer(v_now[outer - r], r)
    g_cond = g_cond * silu_slope(condition)
    g_table = lax.dot_general(
        g_cond, class_hot.astype(F32), (((1,), (1,)), ((), ())), precision=lax.Precision.HIGHEST, preferred_element_type=F32
    )

    def total_dp(x):
        step = 1
        while step < n_dp:
            x = x + lax.ppermute(x, "dp", [(k_, k_ ^ step) for k_ in range(n_dp)])
            step *= 2
        return x

    sums = total_dp(jnp.concatenate([early, g_fc1_b, g_qv_b.reshape(1, 2 * wide)], axis=1)).reshape(-1)
    cuts = [hidden, hidden, repr_width, width, width, ff, 2 * wide]
    marks = [sum(cuts[:n]) for n in range(len(cuts) + 1)]
    s_one_b, s_two_b, s_three_b, s_fc2_b, s_out_b, s_fc1_b, s_qv_b = (sums[lo:hi] for lo, hi in zip(marks, marks[1:]))

    def my_part(x, n):
        return lax.dynamic_slice_in_dim(x.reshape(-1), d * n, n)

    s_b1, s_b2, s_b3 = my_part(s_one_b, n1), my_part(s_two_b, n2), my_part(s_three_b, n3)
    s_qv_b = s_qv_b.reshape(2, wide)

    def spread_tokens(block):
        other = swap_y(block)
        c0, c1 = swap_core(block), swap_core(other)
        own = pair([block, other], y, 0)
        peer = pair([c0, c1], y, 0)
        return pair([own, peer], c, 0).reshape(micro_count, rows_dev, seq, width)

    block_out = spread_tokens(h_low)
    grad_in = spread_tokens(g_in).astype(F32)
    depth = width // n_dp
    return (
        block_out,
        grad_in,
        g_table,
        g_ada_w,
        g_ada_b,
        jnp.stack([g_qkv[:, :wide], g_qkv[:, wide : 2 * wide], g_qkv[:, 2 * wide :]]),
        s_qv_b,
        g_out_t.T,
        s_out_b,
        g_fc1,
        s_fc1_b,
        g_fc2_t.T,
        s_fc2_b,
        g_w1,
        s_b1,
        g_w2,
        s_b2,
        g_w3,
        s_b3,
    )


def solution(mesh):
    dp, tensor = "dp", "tensor"
    rows4, rows3 = P(None, dp, None, None), P(None, dp, None)
    ins = (rows4, rows4, rows4, rows3, rows3, rows3, rows3, P(dp, None), P(dp, None), P(dp), P(None, None, tensor), P(None, tensor), P(tensor, None), P(), P(None, tensor), P(tensor), P(tensor, None), P(), P(dp, None), P(dp), P(dp, None), P(dp), P(dp, None), P(dp))
    outs = (rows4, rows4, P(dp, None), P(dp, None), P(dp), P(None, dp, tensor), P(None, tensor), P(tensor, dp), P(), P(dp, tensor), P(tensor), P(tensor, dp), P(), P(dp, None), P(dp), P(dp, None), P(dp), P(dp, None), P(dp))
    return jax.shard_map(functools.partial(body, mesh), mesh=mesh, in_specs=ins, out_specs=outs, check_vma=False)
```

```python
import functools
import math

import jax
import jax.numpy as jnp
from jax import lax
from jax.experimental import pallas as pl
from jax.experimental.pallas import tpu as pltpu
from jax.sharding import PartitionSpec as P

HEAD_DIM = 72
norm_eps = 1e-06
cos_eps = 1e-06
repa_weight = 0.5
F32 = jnp.float32
BF16 = jnp.bfloat16
VMEM = pl.BlockSpec(memory_space=pltpu.VMEM)
SMEM = pl.BlockSpec(memory_space=pltpu.SMEM)
ANY = pl.BlockSpec(memory_space=pl.ANY)
VMEM_LIMIT = 58 * 1024 * 1024


def shape_of(shape, dtype):
    return jax.ShapeDtypeStruct(tuple(shape), dtype)


def call(kernel, outs, ins, in_specs=None, out_specs=None, scratch=(), flops=0, limit=VMEM_LIMIT, name=None, after=()):
    n = len(ins)
    after = list(after)
    inner_kernel = kernel

    def kernel(*refs):
        inner_kernel(*refs[:n], *refs[n + len(after) :])

    moved = sum(math.prod(a.shape) * a.dtype.itemsize for a in list(ins) + list(outs))
    return pl.pallas_call(
        kernel,
        out_shape=tuple(outs),
        in_specs=list(in_specs or [VMEM] * n) + [ANY] * len(after),
        out_specs=tuple(out_specs or [VMEM] * len(outs)),
        scratch_shapes=list(scratch),
        compiler_params=pltpu.CompilerParams(vmem_limit_bytes=limit),
        cost_estimate=pl.CostEstimate(flops=0, bytes_accessed=0, transcendentals=0),
        name=name,
    )(*ins, *after)


def hold(arrays, after):
    n = len(arrays)
    return pl.pallas_call(
        lambda *refs: None,
        out_shape=tuple(shape_of(a.shape, a.dtype) for a in arrays),
        in_specs=[ANY] * (n + len(after)),
        out_specs=(ANY,) * n,
        input_output_aliases={k: k for k in range(n)},
        compiler_params=pltpu.CompilerParams(vmem_limit_bytes=1024 * 1024),
        name="hold",
    )(*arrays, *after)


def dot(a, b):
    return jnp.dot(a, b, preferred_element_type=F32)


def dot_nt(a, b):
    return lax.dot_general(a, b, (((1,), (1,)), ((), ())), preferred_element_type=F32)


def dot_tn(a, b):
    return lax.dot_general(a, b, (((0,), (0,)), ((), ())), preferred_element_type=F32)


def sigmoid(v):
    return 1.0 / (1.0 + jnp.exp(-v))


def silu_slope(v):
    s = sigmoid(v)
    return s * (1.0 + v * (1.0 - s))


def pick(seg, table):
    out = jnp.broadcast_to(table[0:1, :], (seg.shape[0], table.shape[1]))
    for s in range(1, table.shape[0]):
        out = jnp.where(seg == s, table[s : s + 1, :], out)
    return out


def by_image(seg, values, slots):
    rows = [jnp.sum(jnp.where(seg == s, values, 0.0), axis=0, keepdims=True) for s in range(slots)]
    return jnp.concatenate(rows, axis=0)


def norm_parts(v):
    centered = v - jnp.mean(v, axis=-1, keepdims=True)
    inv = lax.rsqrt(jnp.mean(centered * centered, axis=-1, keepdims=True) + norm_eps)
    return centered * inv, inv


def norm_back(g, xhat, inv):
    return inv * (g - jnp.mean(g, axis=-1, keepdims=True) - xhat * jnp.mean(g * xhat, axis=-1, keepdims=True))


def attend(q, k, v, open_mask, scale):
    s = dot_nt(q, k) * scale
    s = jnp.where(open_mask, s, -1e30)
    e = jnp.exp(s - jnp.max(s, axis=-1, keepdims=True))
    return e * (1.0 / jnp.sum(e, axis=-1, keepdims=True))


def open_of(segc, segr, valr):
    n = segc.shape[0]
    same = lax.broadcasted_iota(jnp.int32, (n, n), 0) == lax.broadcasted_iota(jnp.int32, (n, n), 1)
    return (segc == segr) & ((valr == 1) | same)


def fwd_kernel(heads, order, hid, mods, segc, segr, valr, w, b, m_ref, q_ref, k_ref, v_ref, mix_ref):
    half, width = hid.shape[1], hid.shape[2]
    seq = 2 * half
    scale = HEAD_DIM ** (-0.5)
    for micro in range(2):
        x = jnp.concatenate([hid[order[2 * micro]], hid[order[2 * micro + 1]]], axis=0).astype(F32)
        rows = slice(micro * seq, (micro + 1) * seq)
        seg = segc[rows, :]
        xhat, _ = norm_parts(x)
        shift = pick(seg, mods[micro][:, 0:width])
        scaling = pick(seg, mods[micro][:, width : 2 * width])
        m = (xhat * (1.0 + scaling) + shift).astype(BF16)
        m_ref[rows, :] = m
        q = (dot_nt(m, w[0]) + b[0:1, :]).astype(BF16)
        k = dot_nt(m, w[1]).astype(BF16)
        v = (dot_nt(m, w[2]) + b[1:2, :]).astype(BF16)
        q_ref[rows, :] = q
        k_ref[rows, :] = k
        v_ref[rows, :] = v
        mask = open_of(seg, segr[micro : micro + 1, :], valr[micro : micro + 1, :])
        mixed = []
        for h in range(heads):
            cols = slice(h * HEAD_DIM, (h + 1) * HEAD_DIM)
            p = attend(q[:, cols], k[:, cols], v[:, cols], mask, scale)
            mixed.append(dot(p.astype(BF16), v[:, cols]).astype(BF16))
        mix_ref[rows, :] = jnp.concatenate(mixed, axis=1)


def bwd_kernel(heads, g0, g1, g2, g3, out_w, q_ref, k_ref, v_ref, segc, segr, valr, w, gqkv_ref, part_q, part_y, send, bias_ref, gfull_ref):
    half = g0.shape[0]
    seq = 2 * half
    scale = HEAD_DIM ** (-0.5)
    wide = heads * HEAD_DIM
    sums = []
    for micro in range(2):
        rows = slice(micro * seq, (micro + 1) * seq)
        g = jnp.concatenate([g0[...], g1[...]] if micro == 0 else [g2[...], g3[...]], axis=0)
        gfull_ref[rows, :] = g
        gm = dot_nt(g, out_w[...]).astype(BF16)
        q, k, v = q_ref[rows, :], k_ref[rows, :], v_ref[rows, :]
        mask = open_of(segc[rows, :], segr[micro : micro + 1, :], valr[micro : micro + 1, :])
        gq, gk, gv = [], [], []
        for h in range(heads):
            cols = slice(h * HEAD_DIM, (h + 1) * HEAD_DIM)
            qh, kh, vh, gh = q[:, cols], k[:, cols], v[:, cols], gm[:, cols]
            p = attend(qh, kh, vh, mask, scale)
            gp = dot_nt(gh, vh)
            gs = (p * (gp - jnp.sum(p * gp, axis=-1, keepdims=True))).astype(BF16)
            gq.append((dot(gs, kh) * scale).astype(BF16))
            gk.append((dot_tn(gs, qh) * scale).astype(BF16))
            gv.append(dot_tn(p.astype(BF16), gh).astype(BF16))
        gq, gk, gv = (jnp.concatenate(a, axis=1) for a in (gq, gk, gv))
        gqkv_ref[rows, 0:wide] = gq
        gqkv_ref[rows, wide : 2 * wide] = gk
        gqkv_ref[rows, 2 * wide : 3 * wide] = gv
        spare = gqkv_ref.shape[1] - 3 * wide
        if spare:
            gqkv_ref[rows, 3 * wide :] = jnp.zeros((seq, spare), BF16)
        sums.append(
            jnp.concatenate(
                [jnp.sum(gq.astype(F32), axis=0, keepdims=True), jnp.sum(gv.astype(F32), axis=0, keepdims=True)],
                axis=0,
            )
        )
        part = dot(gq, w[0]) + dot(gk, w[1]) + dot(gv, w[2])
        if micro == 0:
            part_q[...] = part[:half]
            part_y[...] = part[half:]
        else:
            send[...] = part.astype(BF16)
    bias_ref[...] = sums[0] + sums[1]


def mid_kernel(order, hid, mods, segc, m0, m1, m2, m3, w0, w1, w2, w3, out_b, attn_q, h_q, m_two):
    half, width = hid.shape[1], hid.shape[2]
    seq = 2 * half
    x = jnp.concatenate([hid[order[0]], hid[order[1]]], axis=0).astype(F32)
    seg = segc[0:seq, :]
    m2, m3 = (jnp.concatenate([m[half:, :], m[:half, :]], axis=0) for m in (m2, m3))
    attn = dot(m0[...], w0[...]) + dot(m1[...], w1[...]) + dot(m2, w2[...]) + dot(m3, w3[...])
    attn = attn + out_b[...]
    h = x + pick(seg, mods[:, 2 * width : 3 * width]) * attn
    attn_q[...] = attn[:half]
    h_q[...] = h[:half]
    xhat, _ = norm_parts(h)
    m_two[...] = (
        xhat * (1.0 + pick(seg, mods[:, 4 * width : 5 * width])) + pick(seg, mods[:, 3 * width : 4 * width])
    ).astype(BF16)


SPLITS = ((0, 512), (512, 1152))
K0 = math.sqrt(2.0 / math.pi)


def mlp_kernel(m_own, m_par, fc1, b1, fc2, m_full, pre_ref, act_ref, part_q, part_y, send):
    seq = m_own.shape[0]
    half = seq // 2
    for micro, m_ref in enumerate((m_own, m_par)):
        rows = slice(micro * seq, (micro + 1) * seq)
        m = m_ref[...]
        m_full[rows, :] = m
        for lo, hi in SPLITS:
            pre = dot(m, fc1[:, lo:hi]) + b1[:, lo:hi]
            pre_ref[rows, lo:hi] = pre
            t = jnp.tanh(K0 * (pre + 0.044715 * (pre * pre * pre)))
            act_ref[rows, lo:hi] = (0.5 * pre * (1.0 + t)).astype(BF16)
        act = act_ref[rows, :]
        for lo, hi in SPLITS:
            part = dot(act, fc2[:, lo:hi])
            if micro == 0:
                part_q[:, lo:hi] = part[:half]
                part_y[:, lo:hi] = part[half:]
            else:
                send[:, lo:hi] = part.astype(BF16)


def mlp_back_kernel(g0, g1, g2, g3, pre_ref, fc1, fc2, g_full, gpre_ref, part_q, part_y, send, bias):
    half = g0.shape[0]
    seq = 2 * half
    for micro in range(2):
        rows = slice(micro * seq, (micro + 1) * seq)
        g = jnp.concatenate([g0[...], g1[...]] if micro == 0 else [g2[...], g3[...]], axis=0)
        g_full[rows, :] = g
        for lo, hi in SPLITS:
            ga = dot_nt(g, fc2[lo:hi, :])
            v = pre_ref[rows, lo:hi]
            t = jnp.tanh(K0 * (v + 0.044715 * (v * v * v)))
            slope = 0.5 * (1.0 + t) + 0.5 * v * (1.0 - t * t) * (K0 * (1.0 + 3.0 * 0.044715 * (v * v)))
            gp = (ga * slope).astype(BF16)
            gpre_ref[rows, lo:hi] = gp
            total = jnp.sum(gp.astype(F32), axis=0, keepdims=True)
            bias[:, lo:hi] = total if micro == 0 else bias[:, lo:hi] + total
        gp = gpre_ref[rows, :]
        for lo, hi in SPLITS:
            part = dot_nt(gp, fc1[lo:hi, :])
            if micro == 0:
                part_q[:, lo:hi] = part[:half]
                part_y[:, lo:hi] = part[half:]
            else:
                send[:, lo:hi] = part.astype(BF16)


def proj_kernel(plan, n_pieces, quarter_of, meta, *refs):
    (part, got, ry, h_one, mods, seg_ref, fc2_b, grad_out, feat_ref, keep_ref, b1, b2, b3) = refs[:13]
    pieces = refs[13 : 13 + n_pieces]
    (ins_ref, keep_out, send_out, grad_h, g_mlp, gate_sum, gb1, gb2, gb3, gbf) = refs[13 + n_pieces : 23 + n_pieces]
    w1, w2, w3, a1, a2, ga1_ref, ga2_ref, gz_ref, sems = refs[23 + n_pieces :]
    weights = (w1, w2, w3)
    half, width = h_one.shape
    slots = mods.shape[0]
    hidden = w1.shape[1]
    for which, load in enumerate(plan):
        for source, target in load(pieces, weights[which]):
            pltpu.make_async_copy(source, target, sems.at[which]).start()
    seg = seg_ref[...]
    gate = pick(seg, mods[:, 5 * width : 6 * width])
    mlp = part[...] + got[0:half, :].astype(F32) + ry[...].astype(F32) + fc2_b[...]
    h = h_one[...] + gate * mlp
    hl = h.astype(BF16)
    ins_ref[:, 2 * hidden :] = hl
    step = 512
    pltpu.make_async_copy(w1, w1, sems.at[0]).wait()
    for lo in range(0, hidden, step):
        a = dot(hl, w1[:, lo : lo + step]) + b1[:, lo : lo + step]
        a1[:, lo : lo + step] = a
        ins_ref[:, lo : lo + step] = (a * sigmoid(a)).astype(BF16)
    pltpu.make_async_copy(w2, w2, sems.at[1]).wait()
    s = ins_ref[:, 0:hidden]
    for lo in range(0, hidden, step):
        a = dot(s, w2[:, lo : lo + step]) + b2[:, lo : lo + step]
        a2[:, lo : lo + step] = a
        ins_ref[:, hidden + lo : hidden + lo + step] = (a * sigmoid(a)).astype(BF16)
    pltpu.make_async_copy(w3, w3, sems.at[2]).wait()
    z = dot(ins_ref[:, hidden : 2 * hidden], w3[...]) + b3[...]
    feat = feat_ref[...].astype(F32)
    inv_z = lax.rsqrt(jnp.sum(z * z, axis=-1, keepdims=True) + cos_eps)
    inv_f = lax.rsqrt(jnp.sum(feat * feat, axis=-1, keepdims=True) + cos_eps)
    zf = jnp.sum(z * feat, axis=-1, keepdims=True)
    coeff = -repa_weight * keep_ref[...] * inv_z * inv_f
    gz = (coeff * (feat - (zf * inv_z * inv_z) * z)).astype(BF16)
    gz_ref[...] = gz
    gb3[...] = jnp.sum(gz.astype(F32), axis=0, keepdims=True)
    for lo in range(0, hidden, step):
        g = (dot_nt(gz, w3[lo : lo + step, :]) * silu_slope(a2[:, lo : lo + step])).astype(BF16)
        ga2_ref[:, lo : lo + step] = g
        gb2[:, lo : lo + step] = jnp.sum(g.astype(F32), axis=0, keepdims=True)
    ga2 = ga2_ref[...]
    for lo in range(0, hidden, step):
        g = (dot_nt(ga2, w2[lo : lo + step, :]) * silu_slope(a1[:, lo : lo + step])).astype(BF16)
        ga1_ref[:, lo : lo + step] = g
        gb1[:, lo : lo + step] = jnp.sum(g.astype(F32), axis=0, keepdims=True)
    gh = grad_out[...].astype(F32) + dot_nt(ga1_ref[...], w1[...])
    grad_h[...] = gh
    gm = (gate * gh).astype(BF16)
    g_mlp[...] = gm
    gbf[...] = jnp.sum(gm.astype(F32), axis=0, keepdims=True)
    gate_sum[...] = by_image(seg, gh * mlp, slots)
    n, m = hidden // 4, gz.shape[1] // 4
    wide = 2 * n + m
    for out, cr in ((keep_out, 0), (send_out, 1)):
        for yr in range(2):
            q = quarter_of(meta, yr, cr)
            columns, low = pl.ds(pl.multiple_of(q * n, 128), n), pl.ds(pl.multiple_of(q * m, 128), m)
            out[:, yr * wide : yr * wide + n] = ga2_ref[:, columns]
            out[:, yr * wide + n : yr * wide + 2 * n] = ga1_ref[:, columns]
            out[:, yr * wide + 2 * n : (yr + 1) * wide] = gz_ref[:, low]


def proj_grad_kernel(hidden, place, n_outs, meta, f0, f1, f2, f3, keep, got, other, *refs):
    outs = refs[:n_outs]
    a, b, r2, r3, r1, in_sem, out_sem = refs[n_outs:]
    half = f0.shape[0]
    wide = b.shape[1]
    n = r2.shape[1]
    for at, piece in enumerate((f0, f1, f2, f3)):
        pltpu.make_async_copy(piece, a.at[at * half : (at + 1) * half, :], in_sem.at[0]).start()
    for at, piece in enumerate((keep.at[:, 0:wide], other.at[0], got.at[:, 0:wide], other.at[1])):
        pltpu.make_async_copy(piece, b.at[at * half : (at + 1) * half, :], in_sem.at[1]).start()
    pltpu.make_async_copy(b, b, in_sem.at[1]).wait()
    pltpu.make_async_copy(a, a, in_sem.at[0]).wait()
    for job, (first, cols, g, step) in enumerate(
        ((0, slice(0, n), r2, 512), (hidden, slice(2 * n, wide), r3, 512), (2 * hidden, slice(n, 2 * n), r1, 384))
    ):
        for lo in range(0, g.shape[0], step):
            g[lo : lo + step, :] = dot_tn(a[:, first + lo : first + lo + step], b[:, cols]).astype(BF16)
        for source, target in place(job, g, outs, meta):
            pltpu.make_async_copy(source, target, out_sem.at[job]).start()
    for job, g in enumerate((r2, r3, r1)):
        pltpu.make_async_copy(g, g, out_sem.at[job]).wait()


def second_back_kernel(part, rq, ry, grad_h, h_one, attn, mods, seg_ref, g_one, g_attn, gate_sum, shift_sum, scale_sum, bias):
    width = h_one.shape[1]
    slots = mods.shape[0]
    seg = seg_ref[...]
    g = part[...] + rq[0 : part.shape[0], :].astype(F32) + ry[...].astype(F32)
    xhat, inv = norm_parts(h_one[...])
    total = grad_h[...] + norm_back(g * (1.0 + pick(seg, mods[:, 4 * width : 5 * width])), xhat, inv)
    g_one[...] = total
    ga = (pick(seg, mods[:, 2 * width : 3 * width]) * total).astype(BF16)
    g_attn[...] = ga
    bias[...] = jnp.sum(ga.astype(F32), axis=0, keepdims=True)
    gate_sum[...] = by_image(seg, total * attn[...], slots)
    shift_sum[...] = by_image(seg, g, slots)
    scale_sum[...] = by_image(seg, g * xhat, slots)


def first_back_kernel(order, part, rq, ry, g_one, hid, mods, seg_ref, g_in, shift_sum, scale_sum):
    width = g_one.shape[1]
    slots = mods.shape[0]
    seg = seg_ref[...]
    g = part[...] + rq[0 : part.shape[0], :].astype(F32) + ry[...].astype(F32)
    xhat, inv = norm_parts(hid[order[0]].astype(F32))
    total = g_one[...] + norm_back(g * (1.0 + pick(seg, mods[:, width : 2 * width])), xhat, inv)
    g_in[...] = total.astype(BF16)
    shift_sum[...] = by_image(seg, g, slots)
    scale_sum[...] = by_image(seg, g * xhat, slots)


def wgrad_kernel(place, jobs, n_outs, *refs):
    meta = refs[0]
    n_ins = 1 + max(max(a, b) for a, b, _ in jobs)
    ins, outs, (*results, sem) = refs[1 : 1 + n_ins], refs[1 + n_ins : 1 + n_ins + n_outs], refs[1 + n_ins + n_outs :]
    for n, (a, b, step) in enumerate(jobs):
        g = results[n]
        rows = g.shape[0]
        for lo in range(0, rows, step):
            hi = min(lo + step, rows)
            g[lo:hi, :] = dot_tn(ins[a][:, lo:hi], ins[b][...]).astype(BF16)
        for source, target in place(n, g, outs, meta):
            pltpu.make_async_copy(source, target, sem.at[n]).start()
    for n, g in enumerate(results):
        pltpu.make_async_copy(g, g, sem.at[n]).wait()


def body(mesh, hidden_in, grad_out, features, seg_ids, valid_mask, time_ids, class_ids, class_table, ada_w, ada_b, qkv_w, qv_bias, out_w, out_b, fc1_w, fc1_b, fc2_w, fc2_b, repa_w1, repa_b1, repa_w2, repa_b2, repa_w3, repa_b3):
    n_dp = mesh.shape["dp"]
    top = n_dp // 2
    micro_count, rows_dev, seq, width = hidden_in.shape
    slots = time_ids.shape[-1]
    images = micro_count * rows_dev * slots
    half = seq // 2
    wide = qkv_w.shape[2]
    qkv_t = qkv_w.transpose(0, 2, 1)
    heads = wide // HEAD_DIM
    ff = fc1_w.shape[1]
    hidden = repa_w1.shape[1]
    repr_width = repa_w3.shape[1]

    d = lax.axis_index("dp")
    t = lax.axis_index("tensor")
    y, c = t // 2, t % 2
    meta = jnp.stack([d, d, y, c]).astype(jnp.int32)

    def flip_dp(x, mask):
        return lax.ppermute(x, "dp", [(k, k ^ mask) for k in range(n_dp)])

    def swap_y(x):
        return lax.ppermute(x, "tensor", [(0, 2), (2, 0), (1, 3), (3, 1)])

    def swap_core(x):
        return lax.ppermute(x, "tensor", [(0, 1), (1, 0), (2, 3), (3, 2)])

    def exchange_dp(x):
        return lax.all_to_all(x, "dp", 0, 0, tiled=True)

    def gather_dp(x):
        return exchange_dp(jnp.broadcast_to(x[None], (n_dp,) + x.shape))

    def cols_of(w):
        n = w.shape[1] // 4
        return lax.dynamic_slice_in_dim(w, t * n, n, axis=1)

    k1, k2, k3 = repa_w1.shape[0], repa_w2.shape[0], repa_w3.shape[0]
    block = hidden // 4
    third = repr_width // 4
    room = block // 2
    short = k3 // 2

    def cols_padded(w, axis_n):
        w = w.reshape(w.shape[:-1] + (4, axis_n // 4))
        return jnp.pad(w, [(0, 0)] * (w.ndim - 1) + [(0, room - axis_n // 4)]).reshape(w.shape[:-2] + (4 * room,))

    w3_mine = jnp.pad(cols_of(repa_w3), ((0, 0), (0, room - third)))
    w3_fold = jnp.concatenate([w3_mine[:short], w3_mine[short:]], axis=1)
    packed = jnp.concatenate([cols_of(repa_w2), w3_fold, cols_of(repa_w1)], axis=0)
    gathered = lax.all_gather(packed, ("dp", "tensor"), axis=0)
    off3, off1 = k2, k2 + short
    out_y = swap_y(out_w)
    out_c = swap_core(out_w)
    out_yc = swap_core(out_y)
    n1, n2, n3 = repa_b1.shape[0], repa_b2.shape[0], repa_b3.shape[0]

    ids = gather_dp(jnp.concatenate([class_ids.reshape(images), time_ids.reshape(images)]))
    all_class = ids[:, :images].reshape(1, n_dp * images)
    all_time = ids[:, images:].reshape(1, n_dp * images)
    feats = class_table.shape[0]
    class_hot = lax.broadcasted_iota(jnp.int32, (class_table.shape[1], n_dp * images), 0) == all_class
    place = d * feats + lax.broadcasted_iota(jnp.int32, (feats, 1), 0)
    half_width = width // 2
    freqs = jnp.exp(-math.log(10000.0) * (place % half_width).astype(F32) / half_width)
    angles = all_time.astype(F32) * freqs
    condition = jnp.where(place < half_width, jnp.cos(angles), jnp.sin(angles)) + dot(class_table, class_hot.astype(BF16))
    n_images = n_dp * images
    biases = jnp.concatenate([repa_b1, repa_b2, repa_b3])
    lines = -(-biases.shape[0] // n_images)
    biases = jnp.pad(biases, (0, lines * n_images - biases.shape[0])).reshape(lines, n_images)
    found = gather_dp(jnp.concatenate([jax.nn.silu(condition).astype(BF16), biases], axis=0))
    cond_act = found[:, :feats].reshape(width, n_images)
    b_all = found[:, feats:].reshape(n_dp, -1)
    b_one = b_all[:, :n1].reshape(1, -1).astype(F32)
    b_two = b_all[:, n1 : n1 + n2].reshape(1, -1).astype(F32)
    b_three = cols_padded(b_all[:, n1 + n2 : n1 + n2 + n3].reshape(1, -1).astype(F32), repr_width)
    mod_part = lax.dot_general(cond_act, ada_w, (((0,), (1,)), ((), ())), preferred_element_type=F32) + ada_b.astype(F32)
    mod_parts = exchange_dp(mod_part.reshape(n_dp, images, -1))
    modulation = mod_parts.transpose(1, 0, 2).reshape(micro_count, slots, -1)
    mods_own = lax.dynamic_index_in_dim(modulation, c, 0, keepdims=False)
    mods_par = lax.dynamic_index_in_dim(modulation, 1 - c, 0, keepdims=False)

    order = jnp.stack([2 * c + y, 2 * c + 1 - y, 2 * (1 - c) + y, 2 * (1 - c) + 1 - y]).astype(jnp.int32)
    hid = hidden_in.reshape(4, half, width)

    def ordered(a):
        a = a.reshape(4, half)
        return jnp.concatenate([lax.dynamic_index_in_dim(a, order[n], 0, keepdims=False) for n in range(4)])

    seg_line = ordered(seg_ids)
    val_line = ordered(valid_mask)
    seg_rows = seg_line.reshape(2, seq)
    val_rows = val_line.reshape(2, seq)
    seg_cols = seg_line.reshape(2 * seq, 1)
    seg_q = seg_cols[:half]
    keep_q = val_line[:half].reshape(half, 1).astype(F32)
    go_q = lax.dynamic_index_in_dim(grad_out.reshape(4, half, width), order[0], 0, keepdims=False)
    feat_q = cols_padded(lax.dynamic_index_in_dim(features.reshape(4, half, repr_width), order[0], 0, keepdims=False), repr_width)

    tokens = 2 * seq
    T = tokens

    def fwd(order_, hid_, a, b, *rest):
        return functools.partial(fwd_kernel, heads)(order_, hid_, (a, b), *rest)

    m_one, q, k, v, mixed = call(
        fwd,
        [shape_of((T, width), BF16)] + [shape_of((T, wide), BF16)] * 4,
        [order, hid, mods_own, mods_par, seg_cols, seg_rows, val_rows, qkv_t, qv_bias.astype(F32)],
        in_specs=[SMEM] + [VMEM] * 8,
        flops=2 * T * width * wide * 3 + 4 * T * seq * wide,
        name="attention",
    )

    mix_own, mix_send = mixed[:seq], mixed[seq:]
    mix_y = swap_y(mix_own)
    mix_c = swap_core(mix_send)
    mix_yc = swap_y(mix_c)
    attn_q, h_q, m_two = call(
        mid_kernel,
        [shape_of((half, width), F32), shape_of((half, width), F32), shape_of((seq, width), BF16)],
        [order, hid, mods_own, seg_cols, mix_own, mix_c, mix_y, mix_yc, out_w, out_c, out_y, out_yc, out_b.astype(F32).reshape(1, width)],
        in_specs=[SMEM] + [VMEM] * 12,
        flops=2 * seq * width * width,
        name="middle",
    )
    m_par = swap_core(m_two)

    quarter = [shape_of((half, width), F32), shape_of((half, width), F32), shape_of((seq, width), BF16)]

    def settle_quarter(part_y, send):
        got = swap_core(send)
        passed = swap_y((part_y + got[half:].astype(F32)).astype(BF16))
        return got, passed

    def spread_quarter(g):
        gy = swap_y(g)
        return g, gy, swap_core(g), swap_core(gy)

    m_full, pre, act, part_q, part_y, send = call(
        mlp_kernel,
        [shape_of((T, width), BF16), shape_of((T, ff), F32), shape_of((T, ff), BF16)] + quarter,
        [m_two, m_par, fc1_w, fc1_b.astype(F32).reshape(1, ff), fc2_w],
        flops=4 * T * width * ff,
        name="mlp",
    )
    rq, ry = settle_quarter(part_y, send)

    def k_of(w):
        return w.shape[0]

    def position(meta_, rel):
        return lax.bitwise_xor(meta_[0], jnp.int32(rel))

    def relative(nat):
        for bit in range(n_dp.bit_length() - 1):
            cut = nat.reshape((top >> bit, 2, 1 << bit) + nat.shape[1:])
            nat = jnp.where((d >> bit) & 1 == 0, cut, cut[:, ::-1]).reshape(nat.shape)
        return nat

    def quarter_of(meta_, yr, cr):
        ty = meta_[2] if yr == 0 else 1 - meta_[2]
        tc = meta_[3] if cr == 0 else 1 - meta_[3]
        return ty * 2 + tc

    def pair(stack, me, axis):
        first, second = stack
        same = me == 0
        return jnp.concatenate([jnp.where(same, first, second), jnp.where(same, second, first)], axis=axis)

    aligned = k1 % 16 == 0 and k2 % 16 == 0 and k3 % 32 == 0
    n_all = 4 * n_dp

    def load_two(refs, target):
        for s in range(n_all):
            at, part = s // 4, s % 4
            yield refs[0].at[s, 0:k2, :], target.at[at * k2 : (at + 1) * k2, part * block : (part + 1) * block]

    def load_one(refs, target):
        for s in range(n_all):
            at, part = s // 4, s % 4
            yield refs[0].at[s, off1 : off1 + k1, :], target.at[at * k1 : (at + 1) * k1, part * block : (part + 1) * block]

    def load_three(refs, target):
        for s in range(n_all):
            at, part = s // 4, s % 4
            for n in range(2):
                rows = slice(at * k3 + n * short, at * k3 + (n + 1) * short)
                yield refs[0].at[s, off3:off1, n * room : (n + 1) * room], target.at[rows, part * room : (part + 1) * room]

    def whole(n):
        def load(refs, target):
            yield refs[n], target

        return load

    if aligned:
        pieces = [gathered]
        plan = [load_one, load_two, load_three]
    else:
        by_cols = lambda a: a.reshape(n_dp, 4, -1, block).transpose(0, 2, 1, 3).reshape(-1, hidden)
        fold = gathered[:, off3:off1].reshape(n_dp, 4, short, 2, room).transpose(0, 3, 2, 1, 4).reshape(hidden, 4 * room)
        pieces = [by_cols(gathered[:, off1:]), by_cols(gathered[:, :off3]), fold]
        plan = [whole(0), whole(1), whole(2)]

    small_ins = [part_q, rq, ry, h_q, mods_own, seg_q, fc2_b.astype(F32).reshape(1, width), go_q, feat_q, keep_q, b_one, b_two, b_three]
    q_wide = 2 * block + room
    f_own, q_keep, q_send, grad_h, g_mlp, gate_two, g_b1, g_b2, g_b3, g_fc2_b = call(
        functools.partial(proj_kernel, plan, len(pieces), quarter_of),
        [
            shape_of((half, 2 * hidden + width), BF16),
            shape_of((half, 2 * q_wide), BF16),
            shape_of((half, 2 * q_wide), BF16),
            shape_of((half, width), F32),
            shape_of((half, width), BF16),
            shape_of((slots, width), F32),
            shape_of((1, hidden), F32),
            shape_of((1, hidden), F32),
            shape_of((1, 4 * room), F32),
            shape_of((1, width), F32),
        ],
        [meta] + small_ins + pieces,
        in_specs=[SMEM] + [VMEM] * len(small_ins) + [ANY] * len(pieces),
        scratch=[
            pltpu.VMEM((width, hidden), BF16),
            pltpu.VMEM((hidden, hidden), BF16),
            pltpu.VMEM((hidden, 4 * room), BF16),
            pltpu.VMEM((half, hidden), F32),
            pltpu.VMEM((half, hidden), F32),
            pltpu.VMEM((half, hidden), BF16),
            pltpu.VMEM((half, hidden), BF16),
            pltpu.VMEM((half, 4 * room), BF16),
            pltpu.SemaphoreType.DMA((3,)),
        ],
        flops=4 * half * (width * hidden + hidden * hidden + hidden * repr_width),
        name="projector",
    )
    g_mlp_y, g_mlp_c = swap_y(g_mlp), swap_core(g_mlp)
    g_mlp_yc = swap_core(g_mlp_y)
    (f_sent,) = hold([f_own], [g_mlp_y])
    f_y = swap_y(f_sent)
    q_got = swap_core(q_send)
    f_c = swap_core(f_own)
    f_yc = swap_core(f_y)
    q_other = swap_y(jnp.stack([q_keep[:, q_wide:], q_got[:, q_wide:]]))
    low_own, low_y, low_c, low_yc = (a[:, 2 * hidden :] for a in (f_own, f_y, f_c, f_yc))

    def wgrad(place, jobs, ins, outs, name, after=()):
        shapes = [(ins[a].shape[1], ins[b].shape[1]) for a, b, _ in jobs]
        return call(
            functools.partial(wgrad_kernel, place, jobs, len(outs)),
            outs,
            [meta] + ins,
            in_specs=[SMEM] + [VMEM] * len(ins),
            out_specs=[ANY] * len(outs),
            scratch=[pltpu.VMEM(s, BF16) for s in shapes] + [pltpu.SemaphoreType.DMA((len(jobs),))],
            flops=sum(2 * ins[a].shape[0] * r * n for (a, _, _), (r, n) in zip(jobs, shapes)),
            name=name,
            after=after,
        )

    def wgrad_natural(jobs, ins, name, after=()):
        outs = [shape_of((ins[a].shape[1], ins[b].shape[1]), BF16) for a, b, _ in jobs]
        return wgrad(lambda n, g, outs_, meta_: [(g, outs_[n])], jobs, ins, outs, name, after)

    ascending = [1 << n for n in range(n_dp.bit_length() - 1)]
    x_first, x_last = ascending, ascending[1:] + [1]

    def index_of(rel, masks):
        bits = [1 if rel & mask else 0 for mask in masks]
        entry = 0
        for bit in bits[1:]:
            entry = 2 * entry + bit
        return bits[0], entry

    def in_order(rel, masks):
        bits = len(masks)
        cut = rel.reshape((2,) * bits + rel.shape[1:])
        dims = [bits - mask.bit_length() for mask in masks]
        cut = cut.transpose(dims + list(range(bits, cut.ndim))).reshape(rel.shape)
        return cut[:top], cut[top:]

    def wgrad_dp(groups, ins, name, after=()):
        jobs = [job for group, _ in groups for job in group]
        owner = [(n, sum(ins[b].shape[1] for _, b, _ in group[:at])) for n, (group, _) in enumerate(groups) for at in range(len(group))]
        depths = [ins[group[0][0]].shape[1] // n_dp for group, _ in groups]
        widths = [sum(ins[b].shape[1] for _, b, _ in group) for group, _ in groups]
        if all(depth % 16 == 0 for depth in depths) and all(at % 128 == 0 for _, at in owner):

            def place(n, g, outs, meta_):
                group, lo = owner[n]
                depth = depths[group]
                for rel in range(n_dp):
                    at = pl.multiple_of(position(meta_, rel) * depth, 16)
                    side, entry = index_of(rel, groups[group][1])
                    yield g.at[pl.ds(at, depth), :], outs[2 * group + side].at[entry, :, lo : lo + g.shape[1]]

            outs = wgrad(place, jobs, ins, [shape_of((top, depth, w), BF16) for depth, w in zip(depths, widths) for _ in range(2)], name, after)
            return [(outs[2 * n], outs[2 * n + 1]) for n in range(len(groups))]
        nat = list(wgrad_natural(jobs, ins, name, after))
        found = []
        for n, (group, masks) in enumerate(groups):
            one = jnp.concatenate([nat.pop(0) for _ in group], axis=1).reshape(n_dp, depths[n], widths[n])
            found.append(in_order(relative(one), masks))
        return found

    def halves(v):
        return v.reshape((2, v.shape[0] // 2) + v.shape[1:])

    def halve(v, mask):
        return v[0].astype(F32) + flip_dp(v[1].astype(BF16), mask).astype(F32)

    def halve_all(v, masks):
        for mask in masks:
            v = halve(halves(v), mask)
        return v[0]

    f1 = k1 * block // (block + room)

    def proj_grads(after=()):
        ins = [meta, f_own, f_y, f_c, f_yc, q_keep, q_got, q_other]
        whole_rows = aligned and f1 % 32 == 0

        def place(job, g, outs, meta_):
            if not whole_rows:
                yield g, outs[job]
                return
            for rel in range(n_dp):
                side, entry = index_of(rel, x_first)
                to = outs[side].at[entry]
                at = position(meta_, rel)
                if job < 2:
                    columns = slice(0, block) if job == 0 else slice(block, block + room)
                    yield g.at[pl.ds(pl.multiple_of(at * k2, 16), k2), :], to.at[0:k2, columns]
                    continue
                low = f1 // 2
                yield g.at[pl.ds(pl.multiple_of(at * k1, 16), f1), :], to.at[k2 : k2 + f1, 0:block]
                for n in range(2):
                    yield (
                        g.at[pl.ds(pl.multiple_of(at * k1 + f1, 16), low), n * room : (n + 1) * room],
                        to.at[k2 + n * low : k2 + (n + 1) * low, block : block + room],
                    )

        grads = [(hidden, block), (hidden, room), (width, block)]
        shapes = [shape_of((top, k2 + f1, block + room), BF16)] * 2 if whole_rows else [shape_of(g, BF16) for g in grads]
        found = call(
            functools.partial(proj_grad_kernel, hidden, place, len(shapes)),
            shapes,
            ins,
            in_specs=[SMEM] + [ANY] * 7,
            out_specs=[ANY] * len(shapes),
            scratch=[
                pltpu.VMEM((T, 2 * hidden + width), BF16),
                pltpu.VMEM((T, q_wide), BF16),
                *[pltpu.VMEM(g, BF16) for g in grads],
                pltpu.SemaphoreType.DMA((2,)),
                pltpu.SemaphoreType.DMA((3,)),
            ],
            name="grad_projector",
            after=after,
        )
        if whole_rows:
            return found
        two, three, one = found
        one = one.reshape(n_dp, k1, block)
        low = one[:, f1:]
        folded = jnp.concatenate([one[:, :f1], jnp.concatenate([low[..., :room], low[..., room:]], axis=1)], axis=2)
        above = jnp.concatenate([two, three], axis=1).reshape(n_dp, k2, block + room)
        return in_order(relative(jnp.concatenate([above, folded], axis=1)), x_first)

    def unfolded(q):
        low = q[:, :, block:]
        return jnp.concatenate([q[:, :, :block], jnp.concatenate([low[:, : f1 // 2], low[:, f1 // 2 :]], axis=2)], axis=1)

    def quarters(mine):
        mine = mine.astype(BF16)
        other = swap_y(mine)
        c0, c1 = swap_core(mine), swap_core(other)
        own = pair([mine[None], c0[None]], c, 0)
        peer = pair([other[None], c1[None]], c, 0)
        return pair([own, peer], y, 0)

    def side_by_side(q):
        return jnp.concatenate([q[n] for n in range(4)], axis=1).astype(F32)

    g_mlp_full, gpre, part_q, part_y, send, g_fc1_b = call(
        mlp_back_kernel,
        [shape_of((T, width), BF16), shape_of((T, ff), BF16)] + quarter + [shape_of((1, ff), F32)],
        [g_mlp, g_mlp_y, g_mlp_c, g_mlp_yc, pre, fc1_w, fc2_w],
        flops=4 * T * width * ff,
        name="mlp_back",
        after=[f_c, q_got],
    )
    rq, ry = settle_quarter(part_y, send)
    fc2_parts, fc1_parts = wgrad_dp(
        [([(0, 1, 384)], x_last), ([(2, 3, 384)], x_first)], [g_mlp_full, act, m_full, gpre], "grad_fc"
    )
    fc2_got = flip_dp(fc2_parts[1], x_last[0])
    fc1_got = flip_dp(fc1_parts[1], 1)
    pg_first, pg_second = proj_grads(after=[fc1_parts[1]])
    pg_got = flip_dp(pg_second, 1)
    g_one, g_attn, gate_one, shift_two, scale_two, g_out_b = call(
        second_back_kernel,
        [shape_of((half, width), F32), shape_of((half, width), BF16)] + [shape_of((slots, width), F32)] * 3 + [shape_of((1, width), F32)],
        [part_q, rq, ry, grad_h, h_q, attn_q, mods_own, seg_q],
        name="second_back",
        after=[pg_second],
    )
    g_attn_all = spread_quarter(g_attn)
    fc2_got, fc1_got = hold([fc2_got, fc1_got], [g_attn])
    fc2_v = halves(fc2_parts[0].astype(F32) + fc2_got.astype(F32))
    fc2_next = flip_dp(fc2_v[1].astype(BF16), x_last[1])
    fc1_v = halves(fc1_parts[0].astype(F32) + fc1_got.astype(F32))
    fc1_next = flip_dp(fc1_v[1].astype(BF16), 2)

    gqkv, part_q, part_y, send, g_qv_b, g_attn_full = call(
        functools.partial(bwd_kernel, heads),
        [shape_of((T, -(-3 * wide // 128) * 128), BF16)] + quarter + [shape_of((2, wide), F32), shape_of((T, width), BF16)],
        list(g_attn_all) + [out_w, q, k, v, seg_cols, seg_rows, val_rows, qkv_t],
        flops=8 * T * width * wide + 10 * T * seq * wide,
        name="attention_back",
    )
    rq, ry = settle_quarter(part_y, send)
    ((heads_first, heads_second),) = wgrad_dp(
        [([(0, 1, 384), (2, 3, 384)], x_first)], [m_one, gqkv, g_attn_full, mixed], "grad_heads", after=[]
    )
    g_in, shift_one, scale_one = call(
        first_back_kernel,
        [shape_of((half, width), BF16)] + [shape_of((slots, width), F32)] * 2,
        [order, part_q, rq, ry, g_one, hid, mods_own, seg_q],
        in_specs=[SMEM] + [VMEM] * 7,
        name="first_back",
        after=[heads_second],
    )
    heads_got = flip_dp(heads_second, 1)

    fc2_next, fc1_next, pg_got = hold([fc2_next, fc1_next, pg_got], [g_in])
    pg_v = halves(pg_first.astype(F32) + pg_got.astype(F32))
    pg_sent = pg_v[1].astype(BF16)
    pg_got = flip_dp(pg_sent, 2)
    fc2_v = fc2_v[0] + fc2_next.astype(F32)
    fc1_v = halves(fc1_v[0] + fc1_next.astype(F32))
    fc2_v = halves(fc2_v)
    fc2_last = flip_dp(fc2_v[1].astype(BF16), x_last[2])
    fc1_last = flip_dp(fc1_v[1].astype(BF16), x_first[2])

    g_mod = jnp.concatenate([shift_one, scale_one, gate_one, shift_two, scale_two, gate_two], axis=-1)
    g_b3 = g_b3.reshape(4, room)[:, :third].reshape(1, repr_width)
    early = jnp.concatenate([g_b1, g_b2, g_b3, g_fc2_b, g_out_b], axis=1)
    early = early + swap_core(early)
    line = jnp.concatenate([g_mod.reshape(1, -1), early], axis=1)
    (line,) = hold([line], [pg_sent])
    line = line + swap_y(line)
    g_mod, early = line[:, : slots * 6 * width].reshape(slots, -1).astype(BF16), line[:, slots * 6 * width :]
    g_mod = exchange_dp(g_mod.reshape(slots, n_dp, -1).transpose(1, 0, 2))
    heads_got, g_in = hold([heads_got, g_in], [g_mod])
    heads_v = halves(heads_first.astype(F32) + heads_got.astype(F32))
    heads_sent = heads_v[1].astype(BF16)
    heads_got = flip_dp(heads_sent, 2)
    pg_v = halves(pg_v[0] + pg_got.astype(F32))
    pg_sent = pg_v[1].astype(BF16)
    pg_got = flip_dp(pg_sent, 4)
    fc2_last, fc1_last = hold([fc2_last, fc1_last], [g_mod])
    (g_mod,) = hold([g_mod], [heads_sent, pg_sent])
    g_mod = pair([g_mod, swap_core(g_mod)], c, 1).reshape(n_dp * images, -1)
    g_ada_w = lax.dot_general(g_mod, cond_act, (((0,), (1,)), ((), ())), preferred_element_type=F32)
    g_ada_b = jnp.sum(g_mod.astype(F32), axis=0)
    g_cond = lax.dot_general(ada_w, g_mod, (((0,), (1,)), ((), ())), preferred_element_type=F32)
    own = jnp.concatenate([early, g_fc1_b, g_qv_b.reshape(1, 2 * wide)], axis=1)
    sent = jnp.concatenate([g_cond.reshape(n_dp, feats * n_images), jnp.broadcast_to(own, (n_dp, own.shape[1]))], axis=1)
    sums = exchange_dp(sent)
    heads_v = halves(heads_v[0] + heads_got.astype(F32))
    heads_sent = heads_v[1].astype(BF16)
    heads_got = flip_dp(heads_sent, 4)
    mine = halve_all(pg_v[0] + pg_got.astype(F32), x_first[3:]).astype(BF16)
    found = quarters(mine)
    (sums,) = hold([sums], [heads_sent, mine])
    sums = jnp.sum(sums, axis=0)
    g_fc2_t = halve_all(fc2_v[0] + fc2_last.astype(F32), x_last[3:])
    g_fc1 = halve_all(fc1_v[0] + fc1_last.astype(F32), x_first[3:])
    g_heads = halve_all(heads_v[0] + heads_got.astype(F32), x_first[3:])
    g_qkv, g_out_t = g_heads[:, : 3 * wide], g_heads[:, gqkv.shape[1] :]
    g_w2 = side_by_side(found[:, :k2, :block])
    g_w3 = side_by_side(found[:, :k2, block : block + third])
    g_w1 = side_by_side(unfolded(found[:, k2:]))
    g_cond, sums = sums[: feats * n_images].reshape(feats, n_images), sums[feats * n_images :]
    g_cond = g_cond * silu_slope(condition)
    g_table = lax.dot_general(
        g_cond, class_hot.astype(F32), (((1,), (1,)), ((), ())), precision=lax.Precision.HIGHEST, preferred_element_type=F32
    )

    cuts = [hidden, hidden, repr_width, width, width, ff, 2 * wide]
    marks = [sum(cuts[:n]) for n in range(len(cuts) + 1)]
    s_one_b, s_two_b, s_three_b, s_fc2_b, s_out_b, s_fc1_b, s_qv_b = (sums[lo:hi] for lo, hi in zip(marks, marks[1:]))

    def my_part(x, n):
        return lax.dynamic_slice_in_dim(x.reshape(-1), d * n, n)

    s_b1, s_b2, s_b3 = my_part(s_one_b, n1), my_part(s_two_b, n2), my_part(s_three_b, n3)
    s_qv_b = s_qv_b.reshape(2, wide)

    def spread_tokens(block, other, c0, c1):
        own = pair([block, other], y, 0)
        peer = pair([c0, c1], y, 0)
        return pair([own, peer], c, 0).reshape(micro_count, rows_dev, seq, width)

    block_out = spread_tokens(low_own, low_y, low_c, low_yc)
    grad_in = spread_tokens(*spread_quarter(g_in)).astype(F32)
    depth = width // n_dp
    return (
        block_out,
        grad_in,
        g_table,
        g_ada_w,
        g_ada_b,
        jnp.stack([g_qkv[:, :wide], g_qkv[:, wide : 2 * wide], g_qkv[:, 2 * wide :]]),
        s_qv_b,
        g_out_t.T,
        s_out_b,
        g_fc1,
        s_fc1_b,
        g_fc2_t.T,
        s_fc2_b,
        g_w1,
        s_b1,
        g_w2,
        s_b2,
        g_w3,
        s_b3,
    )


def solution(mesh):
    dp, tensor = "dp", "tensor"
    rows4, rows3 = P(None, dp, None, None), P(None, dp, None)
    ins = (rows4, rows4, rows4, rows3, rows3, rows3, rows3, P(dp, None), P(dp, None), P(dp), P(None, None, tensor), P(None, tensor), P(tensor, None), P(), P(None, tensor), P(tensor), P(tensor, None), P(), P(dp, None), P(dp), P(dp, None), P(dp), P(dp, None), P(dp))
    outs = (rows4, rows4, P(dp, None), P(dp, None), P(dp), P(None, dp, tensor), P(None, tensor), P(tensor, dp), P(), P(dp, tensor), P(tensor), P(tensor, dp), P(), P(dp, None), P(dp), P(dp, None), P(dp), P(dp, None), P(dp))
    return jax.shard_map(functools.partial(body, mesh), mesh=mesh, in_specs=ins, out_specs=outs, check_vma=False)
```

```python
import functools
import math

import jax
import jax.numpy as jnp
from jax import lax
from jax.experimental import pallas as pl
from jax.experimental.pallas import tpu as pltpu
from jax.sharding import PartitionSpec as P

HEAD_DIM = 72
norm_eps = 1e-06
cos_eps = 1e-06
repa_weight = 0.5
F32 = jnp.float32
BF16 = jnp.bfloat16
VMEM = pl.BlockSpec(memory_space=pltpu.VMEM)
SMEM = pl.BlockSpec(memory_space=pltpu.SMEM)
ANY = pl.BlockSpec(memory_space=pl.ANY)
VMEM_LIMIT = 58 * 1024 * 1024


def shape_of(shape, dtype):
    return jax.ShapeDtypeStruct(tuple(shape), dtype)


def call(kernel, outs, ins, in_specs=None, out_specs=None, scratch=(), flops=0, limit=VMEM_LIMIT, name=None, after=()):
    n = len(ins)
    after = list(after)
    inner_kernel = kernel

    def kernel(*refs):
        inner_kernel(*refs[:n], *refs[n + len(after) :])

    moved = sum(math.prod(a.shape) * a.dtype.itemsize for a in list(ins) + list(outs))
    return pl.pallas_call(
        kernel,
        out_shape=tuple(outs),
        in_specs=list(in_specs or [VMEM] * n) + [ANY] * len(after),
        out_specs=tuple(out_specs or [VMEM] * len(outs)),
        scratch_shapes=list(scratch),
        compiler_params=pltpu.CompilerParams(vmem_limit_bytes=limit),
        cost_estimate=pl.CostEstimate(flops=0, bytes_accessed=0, transcendentals=0),
        name=name,
    )(*ins, *after)


def hold(arrays, after):
    n = len(arrays)
    return pl.pallas_call(
        lambda *refs: None,
        out_shape=tuple(shape_of(a.shape, a.dtype) for a in arrays),
        in_specs=[ANY] * (n + len(after)),
        out_specs=(ANY,) * n,
        input_output_aliases={k: k for k in range(n)},
        compiler_params=pltpu.CompilerParams(vmem_limit_bytes=1024 * 1024),
        name="hold",
    )(*arrays, *after)


def dot(a, b):
    return jnp.dot(a, b, preferred_element_type=F32)


def dot_nt(a, b):
    return lax.dot_general(a, b, (((1,), (1,)), ((), ())), preferred_element_type=F32)


def dot_tn(a, b):
    return lax.dot_general(a, b, (((0,), (0,)), ((), ())), preferred_element_type=F32)


def sigmoid(v):
    return 1.0 / (1.0 + jnp.exp(-v))


def silu_slope(v):
    s = sigmoid(v)
    return s * (1.0 + v * (1.0 - s))


def pick(seg, table):
    out = jnp.broadcast_to(table[0:1, :], (seg.shape[0], table.shape[1]))
    for s in range(1, table.shape[0]):
        out = jnp.where(seg == s, table[s : s + 1, :], out)
    return out


def by_image(seg, values, slots):
    rows = [jnp.sum(jnp.where(seg == s, values, 0.0), axis=0, keepdims=True) for s in range(slots)]
    return jnp.concatenate(rows, axis=0)


def norm_parts(v):
    centered = v - jnp.mean(v, axis=-1, keepdims=True)
    inv = lax.rsqrt(jnp.mean(centered * centered, axis=-1, keepdims=True) + norm_eps)
    return centered * inv, inv


def norm_back(g, xhat, inv):
    return inv * (g - jnp.mean(g, axis=-1, keepdims=True) - xhat * jnp.mean(g * xhat, axis=-1, keepdims=True))


def attend(q, k, v, open_mask, scale):
    s = dot_nt(q, k) * scale
    s = jnp.where(open_mask, s, -1e30)
    e = jnp.exp(s - jnp.max(s, axis=-1, keepdims=True))
    return e * (1.0 / jnp.sum(e, axis=-1, keepdims=True))


def open_of(segc, segr, valr):
    n = segc.shape[0]
    same = lax.broadcasted_iota(jnp.int32, (n, n), 0) == lax.broadcasted_iota(jnp.int32, (n, n), 1)
    return (segc == segr) & ((valr == 1) | same)


def fwd_kernel(heads, order, hid, mods, segc, segr, valr, w, b, m_ref, q_ref, k_ref, v_ref, mix_ref):
    half, width = hid.shape[1], hid.shape[2]
    seq = 2 * half
    scale = HEAD_DIM ** (-0.5)
    for micro in range(2):
        x = jnp.concatenate([hid[order[2 * micro]], hid[order[2 * micro + 1]]], axis=0).astype(F32)
        rows = slice(micro * seq, (micro + 1) * seq)
        seg = segc[rows, :]
        xhat, _ = norm_parts(x)
        shift = pick(seg, mods[micro][:, 0:width])
        scaling = pick(seg, mods[micro][:, width : 2 * width])
        m = (xhat * (1.0 + scaling) + shift).astype(BF16)
        m_ref[rows, :] = m
        q = (dot_nt(m, w[0]) + b[0:1, :]).astype(BF16)
        k = dot_nt(m, w[1]).astype(BF16)
        v = (dot_nt(m, w[2]) + b[1:2, :]).astype(BF16)
        q_ref[rows, :] = q
        k_ref[rows, :] = k
        v_ref[rows, :] = v
        mask = open_of(seg, segr[micro : micro + 1, :], valr[micro : micro + 1, :])
        mixed = []
        for h in range(heads):
            cols = slice(h * HEAD_DIM, (h + 1) * HEAD_DIM)
            p = attend(q[:, cols], k[:, cols], v[:, cols], mask, scale)
            mixed.append(dot(p.astype(BF16), v[:, cols]).astype(BF16))
        mix_ref[rows, :] = jnp.concatenate(mixed, axis=1)


def bwd_kernel(heads, g0, g1, g2, g3, out_w, q_ref, k_ref, v_ref, segc, segr, valr, w, gqkv_ref, part_q, part_y, send, bias_ref, gfull_ref):
    half = g0.shape[0]
    seq = 2 * half
    scale = HEAD_DIM ** (-0.5)
    wide = heads * HEAD_DIM
    sums = []
    for micro in range(2):
        rows = slice(micro * seq, (micro + 1) * seq)
        g = jnp.concatenate([g0[...], g1[...]] if micro == 0 else [g2[...], g3[...]], axis=0)
        gfull_ref[rows, :] = g
        gm = dot_nt(g, out_w[...]).astype(BF16)
        q, k, v = q_ref[rows, :], k_ref[rows, :], v_ref[rows, :]
        mask = open_of(segc[rows, :], segr[micro : micro + 1, :], valr[micro : micro + 1, :])
        gq, gk, gv = [], [], []
        for h in range(heads):
            cols = slice(h * HEAD_DIM, (h + 1) * HEAD_DIM)
            qh, kh, vh, gh = q[:, cols], k[:, cols], v[:, cols], gm[:, cols]
            p = attend(qh, kh, vh, mask, scale)
            gp = dot_nt(gh, vh)
            gs = (p * (gp - jnp.sum(p * gp, axis=-1, keepdims=True))).astype(BF16)
            gq.append((dot(gs, kh) * scale).astype(BF16))
            gk.append((dot_tn(gs, qh) * scale).astype(BF16))
            gv.append(dot_tn(p.astype(BF16), gh).astype(BF16))
        gq, gk, gv = (jnp.concatenate(a, axis=1) for a in (gq, gk, gv))
        gqkv_ref[rows, 0:wide] = gq
        gqkv_ref[rows, wide : 2 * wide] = gk
        gqkv_ref[rows, 2 * wide : 3 * wide] = gv
        spare = gqkv_ref.shape[1] - 3 * wide
        if spare:
            gqkv_ref[rows, 3 * wide :] = jnp.zeros((seq, spare), BF16)
        sums.append(
            jnp.concatenate(
                [jnp.sum(gq.astype(F32), axis=0, keepdims=True), jnp.sum(gv.astype(F32), axis=0, keepdims=True)],
                axis=0,
            )
        )
        part = dot(gq, w[0]) + dot(gk, w[1]) + dot(gv, w[2])
        if micro == 0:
            part_q[...] = part[:half]
            part_y[...] = part[half:]
        else:
            send[...] = part.astype(BF16)
    bias_ref[...] = sums[0] + sums[1]


def mid_kernel(order, hid, mods, segc, m0, m1, m2, m3, w0, w1, w2, w3, out_b, attn_q, h_q, m_two):
    half, width = hid.shape[1], hid.shape[2]
    seq = 2 * half
    x = jnp.concatenate([hid[order[0]], hid[order[1]]], axis=0).astype(F32)
    seg = segc[0:seq, :]
    m2, m3 = (jnp.concatenate([m[half:, :], m[:half, :]], axis=0) for m in (m2, m3))
    attn = dot(m0[...], w0[...]) + dot(m1[...], w1[...]) + dot(m2, w2[...]) + dot(m3, w3[...])
    attn = attn + out_b[...]
    h = x + pick(seg, mods[:, 2 * width : 3 * width]) * attn
    attn_q[...] = attn[:half]
    h_q[...] = h[:half]
    xhat, _ = norm_parts(h)
    m_two[...] = (
        xhat * (1.0 + pick(seg, mods[:, 4 * width : 5 * width])) + pick(seg, mods[:, 3 * width : 4 * width])
    ).astype(BF16)


SPLITS = ((0, 512), (512, 1152))
K0 = math.sqrt(2.0 / math.pi)


def mlp_kernel(m_own, m_par, fc1, b1, fc2, m_full, pre_ref, act_ref, part_q, part_y, send):
    seq = m_own.shape[0]
    half = seq // 2
    for micro, m_ref in enumerate((m_own, m_par)):
        rows = slice(micro * seq, (micro + 1) * seq)
        m = m_ref[...]
        m_full[rows, :] = m
        for lo, hi in SPLITS:
            pre = dot(m, fc1[:, lo:hi]) + b1[:, lo:hi]
            pre_ref[rows, lo:hi] = pre
            t = jnp.tanh(K0 * (pre + 0.044715 * (pre * pre * pre)))
            act_ref[rows, lo:hi] = (0.5 * pre * (1.0 + t)).astype(BF16)
        act = act_ref[rows, :]
        for lo, hi in SPLITS:
            part = dot(act, fc2[:, lo:hi])
            if micro == 0:
                part_q[:, lo:hi] = part[:half]
                part_y[:, lo:hi] = part[half:]
            else:
                send[:, lo:hi] = part.astype(BF16)


def mlp_back_kernel(g0, g1, g2, g3, pre_ref, fc1, fc2, g_full, gpre_ref, part_q, part_y, send, bias):
    half = g0.shape[0]
    seq = 2 * half
    for micro in range(2):
        rows = slice(micro * seq, (micro + 1) * seq)
        g = jnp.concatenate([g0[...], g1[...]] if micro == 0 else [g2[...], g3[...]], axis=0)
        g_full[rows, :] = g
        for lo, hi in SPLITS:
            ga = dot_nt(g, fc2[lo:hi, :])
            v = pre_ref[rows, lo:hi]
            t = jnp.tanh(K0 * (v + 0.044715 * (v * v * v)))
            slope = 0.5 * (1.0 + t) + 0.5 * v * (1.0 - t * t) * (K0 * (1.0 + 3.0 * 0.044715 * (v * v)))
            gp = (ga * slope).astype(BF16)
            gpre_ref[rows, lo:hi] = gp
            total = jnp.sum(gp.astype(F32), axis=0, keepdims=True)
            bias[:, lo:hi] = total if micro == 0 else bias[:, lo:hi] + total
        gp = gpre_ref[rows, :]
        for lo, hi in SPLITS:
            part = dot_nt(gp, fc1[lo:hi, :])
            if micro == 0:
                part_q[:, lo:hi] = part[:half]
                part_y[:, lo:hi] = part[half:]
            else:
                send[:, lo:hi] = part.astype(BF16)


def proj_kernel(plan, n_pieces, quarter_of, meta, *refs):
    (part, got, ry, h_one, mods, seg_ref, fc2_b, grad_out, feat_ref, keep_ref, b1, b2, b3) = refs[:13]
    pieces = refs[13 : 13 + n_pieces]
    (ins_ref, keep_out, send_out, grad_h, g_mlp, gate_sum, gb1, gb2, gb3, gbf) = refs[13 + n_pieces : 23 + n_pieces]
    w1, w2, w3, a1, a2, ga1_ref, ga2_ref, gz_ref, sems = refs[23 + n_pieces :]
    weights = (w1, w2, w3)
    half, width = h_one.shape
    slots = mods.shape[0]
    hidden = w1.shape[1]
    for which, load in enumerate(plan):
        for source, target in load(pieces, weights[which]):
            pltpu.make_async_copy(source, target, sems.at[which]).start()
    seg = seg_ref[...]
    gate = pick(seg, mods[:, 5 * width : 6 * width])
    mlp = part[...] + got[0:half, :].astype(F32) + ry[...].astype(F32) + fc2_b[...]
    h = h_one[...] + gate * mlp
    hl = h.astype(BF16)
    ins_ref[:, 2 * hidden :] = hl
    step = 512
    pltpu.make_async_copy(w1, w1, sems.at[0]).wait()
    for lo in range(0, hidden, step):
        a = dot(hl, w1[:, lo : lo + step]) + b1[:, lo : lo + step]
        a1[:, lo : lo + step] = a
        ins_ref[:, lo : lo + step] = (a * sigmoid(a)).astype(BF16)
    pltpu.make_async_copy(w2, w2, sems.at[1]).wait()
    s = ins_ref[:, 0:hidden]
    for lo in range(0, hidden, step):
        a = dot(s, w2[:, lo : lo + step]) + b2[:, lo : lo + step]
        a2[:, lo : lo + step] = a
        ins_ref[:, hidden + lo : hidden + lo + step] = (a * sigmoid(a)).astype(BF16)
    pltpu.make_async_copy(w3, w3, sems.at[2]).wait()
    z = dot(ins_ref[:, hidden : 2 * hidden], w3[...]) + b3[...]
    feat = feat_ref[...].astype(F32)
    inv_z = lax.rsqrt(jnp.sum(z * z, axis=-1, keepdims=True) + cos_eps)
    inv_f = lax.rsqrt(jnp.sum(feat * feat, axis=-1, keepdims=True) + cos_eps)
    zf = jnp.sum(z * feat, axis=-1, keepdims=True)
    coeff = -repa_weight * keep_ref[...] * inv_z * inv_f
    gz = (coeff * (feat - (zf * inv_z * inv_z) * z)).astype(BF16)
    gz_ref[...] = gz
    gb3[...] = jnp.sum(gz.astype(F32), axis=0, keepdims=True)
    for lo in range(0, hidden, step):
        g = (dot_nt(gz, w3[lo : lo + step, :]) * silu_slope(a2[:, lo : lo + step])).astype(BF16)
        ga2_ref[:, lo : lo + step] = g
        gb2[:, lo : lo + step] = jnp.sum(g.astype(F32), axis=0, keepdims=True)
    ga2 = ga2_ref[...]
    for lo in range(0, hidden, step):
        g = (dot_nt(ga2, w2[lo : lo + step, :]) * silu_slope(a1[:, lo : lo + step])).astype(BF16)
        ga1_ref[:, lo : lo + step] = g
        gb1[:, lo : lo + step] = jnp.sum(g.astype(F32), axis=0, keepdims=True)
    gh = grad_out[...].astype(F32) + dot_nt(ga1_ref[...], w1[...])
    grad_h[...] = gh
    gm = (gate * gh).astype(BF16)
    g_mlp[...] = gm
    gbf[...] = jnp.sum(gm.astype(F32), axis=0, keepdims=True)
    gate_sum[...] = by_image(seg, gh * mlp, slots)
    n, m = hidden // 4, gz.shape[1] // 4
    wide = 2 * n + m
    for out, cr in ((keep_out, 0), (send_out, 1)):
        for yr in range(2):
            q = quarter_of(meta, yr, cr)
            columns, low = pl.ds(pl.multiple_of(q * n, 128), n), pl.ds(pl.multiple_of(q * m, 128), m)
            out[:, yr * wide : yr * wide + n] = ga2_ref[:, columns]
            out[:, yr * wide + n : yr * wide + 2 * n] = ga1_ref[:, columns]
            out[:, yr * wide + 2 * n : (yr + 1) * wide] = gz_ref[:, low]


def proj_grad_kernel(hidden, place, n_outs, meta, f0, f1, f2, f3, keep, got, *refs):
    outs = refs[:n_outs]
    a, b, r2, r3, r1, in_sem, out_sem = refs[n_outs:]
    half = f0.shape[0]
    wide = b.shape[1]
    n = r2.shape[1]
    f_wide = a.shape[1]
    for at, piece in enumerate((f0, f1, f2, f3)):
        pltpu.make_async_copy(piece.at[:, 0:f_wide], a.at[at * half : (at + 1) * half, :], in_sem.at[0]).start()
    for at, piece in enumerate(
        (keep.at[:, 0:wide], f1.at[:, f_wide : f_wide + wide], got.at[:, 0:wide], f1.at[:, f_wide + wide : f_wide + 2 * wide])
    ):
        pltpu.make_async_copy(piece, b.at[at * half : (at + 1) * half, :], in_sem.at[1]).start()
    pltpu.make_async_copy(b, b, in_sem.at[1]).wait()
    pltpu.make_async_copy(a, a, in_sem.at[0]).wait()
    for job, (first, cols, g, step) in enumerate(
        ((0, slice(0, n), r2, 512), (hidden, slice(2 * n, wide), r3, 512), (2 * hidden, slice(n, 2 * n), r1, 384))
    ):
        for lo in range(0, g.shape[0], step):
            g[lo : lo + step, :] = dot_tn(a[:, first + lo : first + lo + step], b[:, cols]).astype(BF16)
        for source, target in place(job, g, outs, meta):
            pltpu.make_async_copy(source, target, out_sem.at[job]).start()
    for job, g in enumerate((r2, r3, r1)):
        pltpu.make_async_copy(g, g, out_sem.at[job]).wait()


def second_back_kernel(part, rq, ry, grad_h, h_one, attn, mods, seg_ref, g_one, g_attn, gate_sum, shift_sum, scale_sum, bias):
    width = h_one.shape[1]
    slots = mods.shape[0]
    seg = seg_ref[...]
    g = part[...] + rq[0 : part.shape[0], :].astype(F32) + ry[...].astype(F32)
    xhat, inv = norm_parts(h_one[...])
    total = grad_h[...] + norm_back(g * (1.0 + pick(seg, mods[:, 4 * width : 5 * width])), xhat, inv)
    g_one[...] = total
    ga = (pick(seg, mods[:, 2 * width : 3 * width]) * total).astype(BF16)
    g_attn[...] = ga
    bias[...] = jnp.sum(ga.astype(F32), axis=0, keepdims=True)
    gate_sum[...] = by_image(seg, total * attn[...], slots)
    shift_sum[...] = by_image(seg, g, slots)
    scale_sum[...] = by_image(seg, g * xhat, slots)


def first_back_kernel(order, part, rq, ry, g_one, hid, mods, seg_ref, g_in, shift_sum, scale_sum):
    width = g_one.shape[1]
    slots = mods.shape[0]
    seg = seg_ref[...]
    g = part[...] + rq[0 : part.shape[0], :].astype(F32) + ry[...].astype(F32)
    xhat, inv = norm_parts(hid[order[0]].astype(F32))
    total = g_one[...] + norm_back(g * (1.0 + pick(seg, mods[:, width : 2 * width])), xhat, inv)
    g_in[...] = total.astype(BF16)
    shift_sum[...] = by_image(seg, g, slots)
    scale_sum[...] = by_image(seg, g * xhat, slots)


def wgrad_kernel(place, jobs, n_outs, *refs):
    meta = refs[0]
    n_ins = 1 + max(max(a, b) for a, b, _ in jobs)
    ins, outs, (*results, sem) = refs[1 : 1 + n_ins], refs[1 + n_ins : 1 + n_ins + n_outs], refs[1 + n_ins + n_outs :]
    for n, (a, b, step) in enumerate(jobs):
        g = results[n]
        rows = g.shape[0]
        for lo in range(0, rows, step):
            hi = min(lo + step, rows)
            g[lo:hi, :] = dot_tn(ins[a][:, lo:hi], ins[b][...]).astype(BF16)
        for source, target in place(n, g, outs, meta):
            pltpu.make_async_copy(source, target, sem.at[n]).start()
    for n, g in enumerate(results):
        pltpu.make_async_copy(g, g, sem.at[n]).wait()


def body(mesh, hidden_in, grad_out, features, seg_ids, valid_mask, time_ids, class_ids, class_table, ada_w, ada_b, qkv_w, qv_bias, out_w, out_b, fc1_w, fc1_b, fc2_w, fc2_b, repa_w1, repa_b1, repa_w2, repa_b2, repa_w3, repa_b3):
    n_dp = mesh.shape["dp"]
    top = n_dp // 2
    micro_count, rows_dev, seq, width = hidden_in.shape
    slots = time_ids.shape[-1]
    images = micro_count * rows_dev * slots
    half = seq // 2
    wide = qkv_w.shape[2]
    qkv_t = qkv_w.transpose(0, 2, 1)
    heads = wide // HEAD_DIM
    ff = fc1_w.shape[1]
    hidden = repa_w1.shape[1]
    repr_width = repa_w3.shape[1]

    d = lax.axis_index("dp")
    t = lax.axis_index("tensor")
    y, c = t // 2, t % 2
    meta = jnp.stack([d, d, y, c]).astype(jnp.int32)

    def flip_dp(x, mask):
        return lax.ppermute(x, "dp", [(k, k ^ mask) for k in range(n_dp)])

    def swap_y(x):
        return lax.ppermute(x, "tensor", [(0, 2), (2, 0), (1, 3), (3, 1)])

    def swap_core(x):
        return lax.ppermute(x, "tensor", [(0, 1), (1, 0), (2, 3), (3, 2)])

    def exchange_dp(x):
        return lax.all_to_all(x, "dp", 0, 0, tiled=True)

    def gather_dp(x):
        return exchange_dp(jnp.broadcast_to(x[None], (n_dp,) + x.shape))

    def cols_of(w):
        n = w.shape[1] // 4
        return lax.dynamic_slice_in_dim(w, t * n, n, axis=1)

    k1, k2, k3 = repa_w1.shape[0], repa_w2.shape[0], repa_w3.shape[0]
    block = hidden // 4
    third = repr_width // 4
    room = block // 2
    short = k3 // 2

    def cols_padded(w, axis_n):
        w = w.reshape(w.shape[:-1] + (4, axis_n // 4))
        return jnp.pad(w, [(0, 0)] * (w.ndim - 1) + [(0, room - axis_n // 4)]).reshape(w.shape[:-2] + (4 * room,))

    w3_mine = jnp.pad(cols_of(repa_w3), ((0, 0), (0, room - third)))
    w3_fold = jnp.concatenate([w3_mine[:short], w3_mine[short:]], axis=1)
    packed = jnp.concatenate([cols_of(repa_w2), w3_fold, cols_of(repa_w1)], axis=0)
    gathered = lax.all_gather(packed, ("dp", "tensor"), axis=0)
    off3, off1 = k2, k2 + short
    out_y = swap_y(out_w)
    out_c = swap_core(out_w)
    out_yc = swap_core(out_y)
    n1, n2, n3 = repa_b1.shape[0], repa_b2.shape[0], repa_b3.shape[0]

    ids = gather_dp(jnp.concatenate([class_ids.reshape(images), time_ids.reshape(images)]))
    all_class = ids[:, :images].reshape(1, n_dp * images)
    all_time = ids[:, images:].reshape(1, n_dp * images)
    feats = class_table.shape[0]
    class_hot = lax.broadcasted_iota(jnp.int32, (class_table.shape[1], n_dp * images), 0) == all_class
    place = d * feats + lax.broadcasted_iota(jnp.int32, (feats, 1), 0)
    half_width = width // 2
    freqs = jnp.exp(-math.log(10000.0) * (place % half_width).astype(F32) / half_width)
    angles = all_time.astype(F32) * freqs
    condition = jnp.where(place < half_width, jnp.cos(angles), jnp.sin(angles)) + dot(class_table, class_hot.astype(BF16))
    n_images = n_dp * images
    biases = jnp.concatenate([repa_b1, repa_b2, repa_b3])
    lines = -(-biases.shape[0] // n_images)
    biases = jnp.pad(biases, (0, lines * n_images - biases.shape[0])).reshape(lines, n_images)
    found = gather_dp(jnp.concatenate([jax.nn.silu(condition).astype(BF16), biases], axis=0))
    cond_act = found[:, :feats].reshape(width, n_images)
    b_all = found[:, feats:].reshape(n_dp, -1)
    b_one = b_all[:, :n1].reshape(1, -1).astype(F32)
    b_two = b_all[:, n1 : n1 + n2].reshape(1, -1).astype(F32)
    b_three = cols_padded(b_all[:, n1 + n2 : n1 + n2 + n3].reshape(1, -1).astype(F32), repr_width)
    mod_part = lax.dot_general(cond_act, ada_w, (((0,), (1,)), ((), ())), preferred_element_type=F32) + ada_b.astype(F32)
    mod_parts = exchange_dp(mod_part.reshape(n_dp, images, -1))
    modulation = mod_parts.transpose(1, 0, 2).reshape(micro_count, slots, -1)
    mods_own = lax.dynamic_index_in_dim(modulation, c, 0, keepdims=False)
    mods_par = lax.dynamic_index_in_dim(modulation, 1 - c, 0, keepdims=False)

    order = jnp.stack([2 * c + y, 2 * c + 1 - y, 2 * (1 - c) + y, 2 * (1 - c) + 1 - y]).astype(jnp.int32)
    hid = hidden_in.reshape(4, half, width)

    def ordered(a):
        a = a.reshape(4, half)
        return jnp.concatenate([lax.dynamic_index_in_dim(a, order[n], 0, keepdims=False) for n in range(4)])

    seg_line = ordered(seg_ids)
    val_line = ordered(valid_mask)
    seg_rows = seg_line.reshape(2, seq)
    val_rows = val_line.reshape(2, seq)
    seg_cols = seg_line.reshape(2 * seq, 1)
    seg_q = seg_cols[:half]
    keep_q = val_line[:half].reshape(half, 1).astype(F32)
    go_q = lax.dynamic_index_in_dim(grad_out.reshape(4, half, width), order[0], 0, keepdims=False)
    feat_q = cols_padded(lax.dynamic_index_in_dim(features.reshape(4, half, repr_width), order[0], 0, keepdims=False), repr_width)

    tokens = 2 * seq
    T = tokens

    def fwd(order_, hid_, a, b, *rest):
        return functools.partial(fwd_kernel, heads)(order_, hid_, (a, b), *rest)

    m_one, q, k, v, mixed = call(
        fwd,
        [shape_of((T, width), BF16)] + [shape_of((T, wide), BF16)] * 4,
        [order, hid, mods_own, mods_par, seg_cols, seg_rows, val_rows, qkv_t, qv_bias.astype(F32)],
        in_specs=[SMEM] + [VMEM] * 8,
        flops=2 * T * width * wide * 3 + 4 * T * seq * wide,
        name="attention",
    )

    mix_own, mix_send = mixed[:seq], mixed[seq:]
    mix_y = swap_y(mix_own)
    mix_c = swap_core(mix_send)
    mix_yc = swap_y(mix_c)
    attn_q, h_q, m_two = call(
        mid_kernel,
        [shape_of((half, width), F32), shape_of((half, width), F32), shape_of((seq, width), BF16)],
        [order, hid, mods_own, seg_cols, mix_own, mix_c, mix_y, mix_yc, out_w, out_c, out_y, out_yc, out_b.astype(F32).reshape(1, width)],
        in_specs=[SMEM] + [VMEM] * 12,
        flops=2 * seq * width * width,
        name="middle",
    )
    m_par = swap_core(m_two)

    quarter = [shape_of((half, width), F32), shape_of((half, width), F32), shape_of((seq, width), BF16)]

    def settle_quarter(part_y, send):
        got = swap_core(send)
        sent = (part_y + got[half:].astype(F32)).astype(BF16)
        return got, swap_y(sent), sent

    def spread_quarter(g):
        gy = swap_y(g)
        return g, gy, swap_core(g), swap_core(gy)

    m_full, pre, act, part_q, part_y, send = call(
        mlp_kernel,
        [shape_of((T, width), BF16), shape_of((T, ff), F32), shape_of((T, ff), BF16)] + quarter,
        [m_two, m_par, fc1_w, fc1_b.astype(F32).reshape(1, ff), fc2_w],
        flops=4 * T * width * ff,
        name="mlp",
    )
    rq, ry, y_sent = settle_quarter(part_y, send)

    def k_of(w):
        return w.shape[0]

    def position(meta_, rel):
        return lax.bitwise_xor(meta_[0], jnp.int32(rel))

    def relative(nat):
        for bit in range(n_dp.bit_length() - 1):
            cut = nat.reshape((top >> bit, 2, 1 << bit) + nat.shape[1:])
            nat = jnp.where((d >> bit) & 1 == 0, cut, cut[:, ::-1]).reshape(nat.shape)
        return nat

    def quarter_of(meta_, yr, cr):
        ty = meta_[2] if yr == 0 else 1 - meta_[2]
        tc = meta_[3] if cr == 0 else 1 - meta_[3]
        return ty * 2 + tc

    def pair(stack, me, axis):
        first, second = stack
        same = me == 0
        return jnp.concatenate([jnp.where(same, first, second), jnp.where(same, second, first)], axis=axis)

    aligned = k1 % 16 == 0 and k2 % 16 == 0 and k3 % 32 == 0
    n_all = 4 * n_dp

    def load_two(refs, target):
        for s in range(n_all):
            at, part = s // 4, s % 4
            yield refs[0].at[s, 0:k2, :], target.at[at * k2 : (at + 1) * k2, part * block : (part + 1) * block]

    def load_one(refs, target):
        for s in range(n_all):
            at, part = s // 4, s % 4
            yield refs[0].at[s, off1 : off1 + k1, :], target.at[at * k1 : (at + 1) * k1, part * block : (part + 1) * block]

    def load_three(refs, target):
        for s in range(n_all):
            at, part = s // 4, s % 4
            for n in range(2):
                rows = slice(at * k3 + n * short, at * k3 + (n + 1) * short)
                yield refs[0].at[s, off3:off1, n * room : (n + 1) * room], target.at[rows, part * room : (part + 1) * room]

    def whole(n):
        def load(refs, target):
            yield refs[n], target

        return load

    if aligned:
        pieces = [gathered]
        plan = [load_one, load_two, load_three]
    else:
        by_cols = lambda a: a.reshape(n_dp, 4, -1, block).transpose(0, 2, 1, 3).reshape(-1, hidden)
        fold = gathered[:, off3:off1].reshape(n_dp, 4, short, 2, room).transpose(0, 3, 2, 1, 4).reshape(hidden, 4 * room)
        pieces = [by_cols(gathered[:, off1:]), by_cols(gathered[:, :off3]), fold]
        plan = [whole(0), whole(1), whole(2)]

    small_ins = [part_q, rq, ry, h_q, mods_own, seg_q, fc2_b.astype(F32).reshape(1, width), go_q, feat_q, keep_q, b_one, b_two, b_three]
    q_wide = 2 * block + room
    f_own, q_keep, q_send, grad_h, g_mlp, gate_two, g_b1, g_b2, g_b3, g_fc2_b = call(
        functools.partial(proj_kernel, plan, len(pieces), quarter_of),
        [
            shape_of((half, 2 * hidden + width), BF16),
            shape_of((half, 2 * q_wide), BF16),
            shape_of((half, 2 * q_wide), BF16),
            shape_of((half, width), F32),
            shape_of((half, width), BF16),
            shape_of((slots, width), F32),
            shape_of((1, hidden), F32),
            shape_of((1, hidden), F32),
            shape_of((1, 4 * room), F32),
            shape_of((1, width), F32),
        ],
        [meta] + small_ins + pieces,
        in_specs=[SMEM] + [VMEM] * len(small_ins) + [ANY] * len(pieces),
        scratch=[
            pltpu.VMEM((width, hidden), BF16),
            pltpu.VMEM((hidden, hidden), BF16),
            pltpu.VMEM((hidden, 4 * room), BF16),
            pltpu.VMEM((half, hidden), F32),
            pltpu.VMEM((half, hidden), F32),
            pltpu.VMEM((half, hidden), BF16),
            pltpu.VMEM((half, hidden), BF16),
            pltpu.VMEM((half, 4 * room), BF16),
            pltpu.SemaphoreType.DMA((3,)),
        ],
        flops=4 * half * (width * hidden + hidden * hidden + hidden * repr_width),
        name="projector",
    )
    g_mlp_y, g_mlp_c = swap_y(g_mlp), swap_core(g_mlp)
    g_mlp_yc = swap_core(g_mlp_y)
    q_got = swap_core(q_send)
    f_c = swap_core(f_own)
    (f_sent,) = hold([f_own], [g_mlp_y])
    f_wide = 2 * hidden + width
    f_sent = jnp.concatenate([f_sent, q_keep[:, q_wide:], q_got[:, q_wide:]], axis=1)
    f_y = swap_y(f_sent)

    def wgrad(place, jobs, ins, outs, name, after=()):
        shapes = [(ins[a].shape[1], ins[b].shape[1]) for a, b, _ in jobs]
        return call(
            functools.partial(wgrad_kernel, place, jobs, len(outs)),
            outs,
            [meta] + ins,
            in_specs=[SMEM] + [VMEM] * len(ins),
            out_specs=[ANY] * len(outs),
            scratch=[pltpu.VMEM(s, BF16) for s in shapes] + [pltpu.SemaphoreType.DMA((len(jobs),))],
            flops=sum(2 * ins[a].shape[0] * r * n for (a, _, _), (r, n) in zip(jobs, shapes)),
            name=name,
            after=after,
        )

    def wgrad_natural(jobs, ins, name, after=()):
        outs = [shape_of((ins[a].shape[1], ins[b].shape[1]), BF16) for a, b, _ in jobs]
        return wgrad(lambda n, g, outs_, meta_: [(g, outs_[n])], jobs, ins, outs, name, after)

    ascending = [1 << n for n in range(n_dp.bit_length() - 1)]
    x_first, x_last = ascending, ascending[1:] + [1]

    def index_of(rel, masks):
        bits = [1 if rel & mask else 0 for mask in masks]
        entry = 0
        for bit in bits[1:]:
            entry = 2 * entry + bit
        return bits[0], entry

    def in_order(rel, masks):
        bits = len(masks)
        cut = rel.reshape((2,) * bits + rel.shape[1:])
        dims = [bits - mask.bit_length() for mask in masks]
        cut = cut.transpose(dims + list(range(bits, cut.ndim))).reshape(rel.shape)
        return cut[:top], cut[top:]

    def wgrad_dp(groups, ins, name, after=()):
        jobs = [job for group, _ in groups for job in group]
        owner = [(n, sum(ins[b].shape[1] for _, b, _ in group[:at])) for n, (group, _) in enumerate(groups) for at in range(len(group))]
        depths = [ins[group[0][0]].shape[1] // n_dp for group, _ in groups]
        widths = [sum(ins[b].shape[1] for _, b, _ in group) for group, _ in groups]
        if all(depth % 16 == 0 for depth in depths) and all(at % 128 == 0 for _, at in owner):

            def place(n, g, outs, meta_):
                group, lo = owner[n]
                depth = depths[group]
                for rel in range(n_dp):
                    at = pl.multiple_of(position(meta_, rel) * depth, 16)
                    side, entry = index_of(rel, groups[group][1])
                    yield g.at[pl.ds(at, depth), :], outs[2 * group + side].at[entry, :, lo : lo + g.shape[1]]

            outs = wgrad(place, jobs, ins, [shape_of((top, depth, w), BF16) for depth, w in zip(depths, widths) for _ in range(2)], name, after)
            return [(outs[2 * n], outs[2 * n + 1]) for n in range(len(groups))]
        nat = list(wgrad_natural(jobs, ins, name, after))
        found = []
        for n, (group, masks) in enumerate(groups):
            one = jnp.concatenate([nat.pop(0) for _ in group], axis=1).reshape(n_dp, depths[n], widths[n])
            found.append(in_order(relative(one), masks))
        return found

    def halves(v):
        return v.reshape((2, v.shape[0] // 2) + v.shape[1:])

    def halve(v, mask):
        return v[0].astype(F32) + flip_dp(v[1].astype(BF16), mask).astype(F32)

    def halve_all(v, masks):
        for mask in masks:
            v = halve(halves(v), mask)
        return v[0]

    f1 = k1 * block // (block + room)

    def proj_grads(after=()):
        ins = [meta, f_own, f_y, f_c, f_yc, q_keep, q_got]
        whole_rows = aligned and f1 % 32 == 0

        def place(job, g, outs, meta_):
            if not whole_rows:
                yield g, outs[job]
                return
            for rel in range(n_dp):
                side, entry = index_of(rel, x_first)
                to = outs[side].at[entry]
                at = position(meta_, rel)
                if job < 2:
                    columns = slice(0, block) if job == 0 else slice(block, block + room)
                    yield g.at[pl.ds(pl.multiple_of(at * k2, 16), k2), :], to.at[0:k2, columns]
                    continue
                low = f1 // 2
                yield g.at[pl.ds(pl.multiple_of(at * k1, 16), f1), :], to.at[k2 : k2 + f1, 0:block]
                for n in range(2):
                    yield (
                        g.at[pl.ds(pl.multiple_of(at * k1 + f1, 16), low), n * room : (n + 1) * room],
                        to.at[k2 + n * low : k2 + (n + 1) * low, block : block + room],
                    )

        grads = [(hidden, block), (hidden, room), (width, block)]
        shapes = [shape_of((top, k2 + f1, block + room), BF16)] * 2 if whole_rows else [shape_of(g, BF16) for g in grads]
        found = call(
            functools.partial(proj_grad_kernel, hidden, place, len(shapes)),
            shapes,
            ins,
            in_specs=[SMEM] + [ANY] * 6,
            out_specs=[ANY] * len(shapes),
            scratch=[
                pltpu.VMEM((T, 2 * hidden + width), BF16),
                pltpu.VMEM((T, q_wide), BF16),
                *[pltpu.VMEM(g, BF16) for g in grads],
                pltpu.SemaphoreType.DMA((2,)),
                pltpu.SemaphoreType.DMA((3,)),
            ],
            name="grad_projector",
            after=after,
        )
        if whole_rows:
            return found
        two, three, one = found
        one = one.reshape(n_dp, k1, block)
        low = one[:, f1:]
        folded = jnp.concatenate([one[:, :f1], jnp.concatenate([low[..., :room], low[..., room:]], axis=1)], axis=2)
        above = jnp.concatenate([two, three], axis=1).reshape(n_dp, k2, block + room)
        return in_order(relative(jnp.concatenate([above, folded], axis=1)), x_first)

    def unfolded(q):
        low = q[:, :, block:]
        return jnp.concatenate([q[:, :, :block], jnp.concatenate([low[:, : f1 // 2], low[:, f1 // 2 :]], axis=2)], axis=1)

    def quarters(mine):
        mine = mine.astype(BF16)
        other = swap_y(mine)
        c0, c1 = swap_core(mine), swap_core(other)
        own = pair([mine[None], c0[None]], c, 0)
        peer = pair([other[None], c1[None]], c, 0)
        return pair([own, peer], y, 0)

    def side_by_side(q):
        return jnp.concatenate([q[n] for n in range(4)], axis=1).astype(F32)

    g_mlp_full, gpre, part_q, part_y, send, g_fc1_b = call(
        mlp_back_kernel,
        [shape_of((T, width), BF16), shape_of((T, ff), BF16)] + quarter + [shape_of((1, ff), F32)],
        [g_mlp, g_mlp_y, g_mlp_c, g_mlp_yc, pre, fc1_w, fc2_w],
        flops=4 * T * width * ff,
        name="mlp_back",
        after=[f_c, f_sent],
    )
    rq, ry, y_sent = settle_quarter(part_y, send)
    fc2_parts, fc1_parts = wgrad_dp(
        [([(0, 1, 384)], x_last), ([(2, 3, 384)], x_first)], [g_mlp_full, act, m_full, gpre], "grad_fc"
    )
    fc2_got = flip_dp(fc2_parts[1], x_last[0])
    fc1_got = flip_dp(fc1_parts[1], 1)
    (f_y,) = hold([f_y], [fc1_parts[1], y_sent])
    f_yc = swap_core(f_y)
    low_own, low_y, low_c, low_yc = (a[:, 2 * hidden : f_wide] for a in (f_own, f_y, f_c, f_yc))
    pg_first, pg_second = proj_grads(after=[fc1_parts[1]])
    pg_got = flip_dp(pg_second, 1)
    g_one, g_attn, gate_one, shift_two, scale_two, g_out_b = call(
        second_back_kernel,
        [shape_of((half, width), F32), shape_of((half, width), BF16)] + [shape_of((slots, width), F32)] * 3 + [shape_of((1, width), F32)],
        [part_q, rq, ry, grad_h, h_q, attn_q, mods_own, seg_q],
        name="second_back",
        after=[pg_second],
    )
    g_attn_all = spread_quarter(g_attn)
    fc2_got, fc1_got = hold([fc2_got, fc1_got], [g_attn])
    fc2_v = halves(fc2_parts[0].astype(F32) + fc2_got.astype(F32))
    fc2_next = flip_dp(fc2_v[1].astype(BF16), x_last[1])
    fc1_v = halves(fc1_parts[0].astype(F32) + fc1_got.astype(F32))
    fc1_next = flip_dp(fc1_v[1].astype(BF16), 2)

    gqkv, part_q, part_y, send, g_qv_b, g_attn_full = call(
        functools.partial(bwd_kernel, heads),
        [shape_of((T, -(-3 * wide // 128) * 128), BF16)] + quarter + [shape_of((2, wide), F32), shape_of((T, width), BF16)],
        list(g_attn_all) + [out_w, q, k, v, seg_cols, seg_rows, val_rows, qkv_t],
        flops=8 * T * width * wide + 10 * T * seq * wide,
        name="attention_back",
    )
    rq, ry, y_sent = settle_quarter(part_y, send)
    ((heads_first, heads_second),) = wgrad_dp(
        [([(0, 1, 384), (2, 3, 384)], x_first)], [m_one, gqkv, g_attn_full, mixed], "grad_heads", after=[]
    )
    g_in, shift_one, scale_one = call(
        first_back_kernel,
        [shape_of((half, width), BF16)] + [shape_of((slots, width), F32)] * 2,
        [order, part_q, rq, ry, g_one, hid, mods_own, seg_q],
        in_specs=[SMEM] + [VMEM] * 7,
        name="first_back",
        after=[heads_second],
    )
    heads_got = flip_dp(heads_second, 1)

    fc2_next, fc1_next, pg_got = hold([fc2_next, fc1_next, pg_got], [g_in])
    pg_v = halves(pg_first.astype(F32) + pg_got.astype(F32))
    pg_sent = pg_v[1].astype(BF16)
    pg_got = flip_dp(pg_sent, 2)
    fc2_v = fc2_v[0] + fc2_next.astype(F32)
    fc1_v = halves(fc1_v[0] + fc1_next.astype(F32))
    fc2_v = halves(fc2_v)
    fc2_last = flip_dp(fc2_v[1].astype(BF16), x_last[2])
    fc1_last = flip_dp(fc1_v[1].astype(BF16), x_first[2])

    g_mod = jnp.concatenate([shift_one, scale_one, gate_one, shift_two, scale_two, gate_two], axis=-1)
    g_b3 = g_b3.reshape(4, room)[:, :third].reshape(1, repr_width)
    early = jnp.concatenate([g_b1, g_b2, g_b3, g_fc2_b, g_out_b], axis=1)
    early = early + swap_core(early)
    line = jnp.concatenate([g_mod.reshape(1, -1), early], axis=1)
    (line,) = hold([line], [pg_sent])
    line = line + swap_y(line)
    g_mod, early = line[:, : slots * 6 * width].reshape(slots, -1).astype(BF16), line[:, slots * 6 * width :]
    g_mod = exchange_dp(g_mod.reshape(slots, n_dp, -1).transpose(1, 0, 2))
    pg_v = halves(pg_v[0] + pg_got.astype(F32))
    pg_sent = pg_v[1].astype(BF16)
    pg_got = flip_dp(pg_sent, 4)
    heads_got, g_in = hold([heads_got, g_in], [pg_sent])
    heads_v = halves(heads_first.astype(F32) + heads_got.astype(F32))
    heads_sent = heads_v[1].astype(BF16)
    heads_got = flip_dp(heads_sent, 2)
    (g_mod,) = hold([g_mod], [heads_sent])
    fc2_last, fc1_last = hold([fc2_last, fc1_last], [g_mod])
    g_mod = pair([g_mod, swap_core(g_mod)], c, 1).reshape(n_dp * images, -1)
    g_ada_w = lax.dot_general(g_mod, cond_act, (((0,), (1,)), ((), ())), preferred_element_type=F32)
    g_ada_b = jnp.sum(g_mod.astype(F32), axis=0)
    g_cond = lax.dot_general(ada_w, g_mod, (((0,), (1,)), ((), ())), preferred_element_type=F32)
    own = jnp.concatenate([early, g_fc1_b, g_qv_b.reshape(1, 2 * wide)], axis=1)
    sent = jnp.concatenate([g_cond.reshape(n_dp, feats * n_images), jnp.broadcast_to(own, (n_dp, own.shape[1]))], axis=1)
    heads_v = halves(heads_v[0] + heads_got.astype(F32))
    heads_sent = heads_v[1].astype(BF16)
    heads_got = flip_dp(heads_sent, 4)
    mine = halve_all(pg_v[0] + pg_got.astype(F32), x_first[3:]).astype(BF16)
    found = quarters(mine)
    (sent,) = hold([sent], [heads_sent, mine])
    sums = exchange_dp(sent)
    sums = jnp.sum(sums, axis=0)
    g_fc2_t = halve_all(fc2_v[0] + fc2_last.astype(F32), x_last[3:])
    g_fc1 = halve_all(fc1_v[0] + fc1_last.astype(F32), x_first[3:])
    g_heads = halve_all(heads_v[0] + heads_got.astype(F32), x_first[3:])
    g_qkv, g_out_t = g_heads[:, : 3 * wide], g_heads[:, gqkv.shape[1] :]
    g_w2 = side_by_side(found[:, :k2, :block])
    g_w3 = side_by_side(found[:, :k2, block : block + third])
    g_w1 = side_by_side(unfolded(found[:, k2:]))
    g_cond, sums = sums[: feats * n_images].reshape(feats, n_images), sums[feats * n_images :]
    g_cond = g_cond * silu_slope(condition)
    g_table = lax.dot_general(
        g_cond, class_hot.astype(F32), (((1,), (1,)), ((), ())), precision=lax.Precision.HIGHEST, preferred_element_type=F32
    )

    cuts = [hidden, hidden, repr_width, width, width, ff, 2 * wide]
    marks = [sum(cuts[:n]) for n in range(len(cuts) + 1)]
    s_one_b, s_two_b, s_three_b, s_fc2_b, s_out_b, s_fc1_b, s_qv_b = (sums[lo:hi] for lo, hi in zip(marks, marks[1:]))

    def my_part(x, n):
        return lax.dynamic_slice_in_dim(x.reshape(-1), d * n, n)

    s_b1, s_b2, s_b3 = my_part(s_one_b, n1), my_part(s_two_b, n2), my_part(s_three_b, n3)
    s_qv_b = s_qv_b.reshape(2, wide)

    def spread_tokens(block, other, c0, c1):
        own = pair([block, other], y, 0)
        peer = pair([c0, c1], y, 0)
        return pair([own, peer], c, 0).reshape(micro_count, rows_dev, seq, width)

    block_out = spread_tokens(low_own, low_y, low_c, low_yc)
    grad_in = spread_tokens(*spread_quarter(g_in)).astype(F32)
    depth = width // n_dp
    return (
        block_out,
        grad_in,
        g_table,
        g_ada_w,
        g_ada_b,
        jnp.stack([g_qkv[:, :wide], g_qkv[:, wide : 2 * wide], g_qkv[:, 2 * wide :]]),
        s_qv_b,
        g_out_t.T,
        s_out_b,
        g_fc1,
        s_fc1_b,
        g_fc2_t.T,
        s_fc2_b,
        g_w1,
        s_b1,
        g_w2,
        s_b2,
        g_w3,
        s_b3,
    )


def solution(mesh):
    dp, tensor = "dp", "tensor"
    rows4, rows3 = P(None, dp, None, None), P(None, dp, None)
    ins = (rows4, rows4, rows4, rows3, rows3, rows3, rows3, P(dp, None), P(dp, None), P(dp), P(None, None, tensor), P(None, tensor), P(tensor, None), P(), P(None, tensor), P(tensor), P(tensor, None), P(), P(dp, None), P(dp), P(dp, None), P(dp), P(dp, None), P(dp))
    outs = (rows4, rows4, P(dp, None), P(dp, None), P(dp), P(None, dp, tensor), P(None, tensor), P(tensor, dp), P(), P(dp, tensor), P(tensor), P(tensor, dp), P(), P(dp, None), P(dp), P(dp, None), P(dp), P(dp, None), P(dp))
    return jax.shard_map(functools.partial(body, mesh), mesh=mesh, in_specs=ins, out_specs=outs, check_vma=False)
```

```python
import functools
import math

import jax
import jax.numpy as jnp
from jax import lax
from jax.experimental import pallas as pl
from jax.experimental.pallas import tpu as pltpu
from jax.sharding import PartitionSpec as P

HEAD_DIM = 72
norm_eps = 1e-06
cos_eps = 1e-06
repa_weight = 0.5
F32 = jnp.float32
BF16 = jnp.bfloat16
VMEM = pl.BlockSpec(memory_space=pltpu.VMEM)
SMEM = pl.BlockSpec(memory_space=pltpu.SMEM)
ANY = pl.BlockSpec(memory_space=pl.ANY)
VMEM_LIMIT = 58 * 1024 * 1024


def shape_of(shape, dtype):
    return jax.ShapeDtypeStruct(tuple(shape), dtype)


def call(kernel, outs, ins, in_specs=None, out_specs=None, scratch=(), flops=0, limit=VMEM_LIMIT, name=None, after=()):
    n = len(ins)
    after = list(after)
    inner_kernel = kernel

    def kernel(*refs):
        inner_kernel(*refs[:n], *refs[n + len(after) :])

    moved = sum(math.prod(a.shape) * a.dtype.itemsize for a in list(ins) + list(outs))
    return pl.pallas_call(
        kernel,
        out_shape=tuple(outs),
        in_specs=list(in_specs or [VMEM] * n) + [ANY] * len(after),
        out_specs=tuple(out_specs or [VMEM] * len(outs)),
        scratch_shapes=list(scratch),
        compiler_params=pltpu.CompilerParams(vmem_limit_bytes=limit),
        cost_estimate=pl.CostEstimate(flops=0, bytes_accessed=0, transcendentals=0),
        name=name,
    )(*ins, *after)


def hold(arrays, after):
    n = len(arrays)
    return pl.pallas_call(
        lambda *refs: None,
        out_shape=tuple(shape_of(a.shape, a.dtype) for a in arrays),
        in_specs=[ANY] * (n + len(after)),
        out_specs=(ANY,) * n,
        input_output_aliases={k: k for k in range(n)},
        compiler_params=pltpu.CompilerParams(vmem_limit_bytes=1024 * 1024),
        name="hold",
    )(*arrays, *after)


def dot(a, b):
    return jnp.dot(a, b, preferred_element_type=F32)


def dot_nt(a, b):
    return lax.dot_general(a, b, (((1,), (1,)), ((), ())), preferred_element_type=F32)


def dot_tn(a, b):
    return lax.dot_general(a, b, (((0,), (0,)), ((), ())), preferred_element_type=F32)


def sigmoid(v):
    return 1.0 / (1.0 + jnp.exp(-v))


def silu_slope(v):
    s = sigmoid(v)
    return s * (1.0 + v * (1.0 - s))


def pick(seg, table):
    out = jnp.broadcast_to(table[0:1, :], (seg.shape[0], table.shape[1]))
    for s in range(1, table.shape[0]):
        out = jnp.where(seg == s, table[s : s + 1, :], out)
    return out


def by_image(seg, values, slots):
    rows = [jnp.sum(jnp.where(seg == s, values, 0.0), axis=0, keepdims=True) for s in range(slots)]
    return jnp.concatenate(rows, axis=0)


def norm_parts(v):
    centered = v - jnp.mean(v, axis=-1, keepdims=True)
    inv = lax.rsqrt(jnp.mean(centered * centered, axis=-1, keepdims=True) + norm_eps)
    return centered * inv, inv


def norm_back(g, xhat, inv):
    return inv * (g - jnp.mean(g, axis=-1, keepdims=True) - xhat * jnp.mean(g * xhat, axis=-1, keepdims=True))


def attend(q, k, v, open_mask, scale):
    s = dot_nt(q, k) * scale
    s = jnp.where(open_mask, s, -1e30)
    e = jnp.exp(s - jnp.max(s, axis=-1, keepdims=True))
    return e * (1.0 / jnp.sum(e, axis=-1, keepdims=True))


def open_of(segc, segr, valr):
    n = segc.shape[0]
    same = lax.broadcasted_iota(jnp.int32, (n, n), 0) == lax.broadcasted_iota(jnp.int32, (n, n), 1)
    return (segc == segr) & ((valr == 1) | same)


def fwd_kernel(heads, order, hid, mods, segc, segr, valr, w, b, m_ref, q_ref, k_ref, v_ref, mix_ref):
    half, width = hid.shape[1], hid.shape[2]
    seq = 2 * half
    scale = HEAD_DIM ** (-0.5)
    for micro in range(2):
        x = jnp.concatenate([hid[order[2 * micro]], hid[order[2 * micro + 1]]], axis=0).astype(F32)
        rows = slice(micro * seq, (micro + 1) * seq)
        seg = segc[rows, :]
        xhat, _ = norm_parts(x)
        shift = pick(seg, mods[micro][:, 0:width])
        scaling = pick(seg, mods[micro][:, width : 2 * width])
        m = (xhat * (1.0 + scaling) + shift).astype(BF16)
        m_ref[rows, :] = m
        q = (dot_nt(m, w[0]) + b[0:1, :]).astype(BF16)
        k = dot_nt(m, w[1]).astype(BF16)
        v = (dot_nt(m, w[2]) + b[1:2, :]).astype(BF16)
        q_ref[rows, :] = q
        k_ref[rows, :] = k
        v_ref[rows, :] = v
        mask = open_of(seg, segr[micro : micro + 1, :], valr[micro : micro + 1, :])
        mixed = []
        for h in range(heads):
            cols = slice(h * HEAD_DIM, (h + 1) * HEAD_DIM)
            p = attend(q[:, cols], k[:, cols], v[:, cols], mask, scale)
            mixed.append(dot(p.astype(BF16), v[:, cols]).astype(BF16))
        mix_ref[rows, :] = jnp.concatenate(mixed, axis=1)


def bwd_kernel(heads, g0, g1, g2, g3, out_w, q_ref, k_ref, v_ref, segc, segr, valr, w, gqkv_ref, part_q, part_y, send, bias_ref, gfull_ref):
    half = g0.shape[0]
    seq = 2 * half
    scale = HEAD_DIM ** (-0.5)
    wide = heads * HEAD_DIM
    sums = []
    for micro in range(2):
        rows = slice(micro * seq, (micro + 1) * seq)
        g = jnp.concatenate([g0[...], g1[...]] if micro == 0 else [g2[...], g3[...]], axis=0)
        gfull_ref[rows, :] = g
        gm = dot_nt(g, out_w[...]).astype(BF16)
        q, k, v = q_ref[rows, :], k_ref[rows, :], v_ref[rows, :]
        mask = open_of(segc[rows, :], segr[micro : micro + 1, :], valr[micro : micro + 1, :])
        gq, gk, gv = [], [], []
        for h in range(heads):
            cols = slice(h * HEAD_DIM, (h + 1) * HEAD_DIM)
            qh, kh, vh, gh = q[:, cols], k[:, cols], v[:, cols], gm[:, cols]
            p = attend(qh, kh, vh, mask, scale)
            gp = dot_nt(gh, vh)
            gs = (p * (gp - jnp.sum(p * gp, axis=-1, keepdims=True))).astype(BF16)
            gq.append((dot(gs, kh) * scale).astype(BF16))
            gk.append((dot_tn(gs, qh) * scale).astype(BF16))
            gv.append(dot_tn(p.astype(BF16), gh).astype(BF16))
        gq, gk, gv = (jnp.concatenate(a, axis=1) for a in (gq, gk, gv))
        gqkv_ref[rows, 0:wide] = gq
        gqkv_ref[rows, wide : 2 * wide] = gk
        gqkv_ref[rows, 2 * wide : 3 * wide] = gv
        spare = gqkv_ref.shape[1] - 3 * wide
        if spare:
            gqkv_ref[rows, 3 * wide :] = jnp.zeros((seq, spare), BF16)
        sums.append(
            jnp.concatenate(
                [jnp.sum(gq.astype(F32), axis=0, keepdims=True), jnp.sum(gv.astype(F32), axis=0, keepdims=True)],
                axis=0,
            )
        )
        part = dot(gq, w[0]) + dot(gk, w[1]) + dot(gv, w[2])
        if micro == 0:
            part_q[...] = part[:half]
            part_y[...] = part[half:]
        else:
            send[...] = part.astype(BF16)
    bias_ref[...] = sums[0] + sums[1]


def mid_kernel(order, hid, mods, segc, m0, m1, m2, m3, w0, w1, w2, w3, out_b, attn_q, h_q, m_two):
    half, width = hid.shape[1], hid.shape[2]
    seq = 2 * half
    x = jnp.concatenate([hid[order[0]], hid[order[1]]], axis=0).astype(F32)
    seg = segc[0:seq, :]
    m2, m3 = (jnp.concatenate([m[half:, :], m[:half, :]], axis=0) for m in (m2, m3))
    attn = dot(m0[...], w0[...]) + dot(m1[...], w1[...]) + dot(m2, w2[...]) + dot(m3, w3[...])
    attn = attn + out_b[...]
    h = x + pick(seg, mods[:, 2 * width : 3 * width]) * attn
    attn_q[...] = attn[:half]
    h_q[...] = h[:half]
    xhat, _ = norm_parts(h)
    m_two[...] = (
        xhat * (1.0 + pick(seg, mods[:, 4 * width : 5 * width])) + pick(seg, mods[:, 3 * width : 4 * width])
    ).astype(BF16)


SPLITS = ((0, 512), (512, 1152))
K0 = math.sqrt(2.0 / math.pi)


def mlp_kernel(m_own, m_par, fc1, b1, fc2, m_full, pre_ref, act_ref, part_q, part_y, send):
    seq = m_own.shape[0]
    half = seq // 2
    for micro, m_ref in enumerate((m_own, m_par)):
        rows = slice(micro * seq, (micro + 1) * seq)
        m = m_ref[...]
        m_full[rows, :] = m
        for lo, hi in SPLITS:
            pre = dot(m, fc1[:, lo:hi]) + b1[:, lo:hi]
            pre_ref[rows, lo:hi] = pre
            t = jnp.tanh(K0 * (pre + 0.044715 * (pre * pre * pre)))
            act_ref[rows, lo:hi] = (0.5 * pre * (1.0 + t)).astype(BF16)
        act = act_ref[rows, :]
        for lo, hi in SPLITS:
            part = dot(act, fc2[:, lo:hi])
            if micro == 0:
                part_q[:, lo:hi] = part[:half]
                part_y[:, lo:hi] = part[half:]
            else:
                send[:, lo:hi] = part.astype(BF16)


def mlp_back_kernel(g0, g1, g2, g3, pre_ref, fc1, fc2, g_full, gpre_ref, part_q, part_y, send, bias):
    half = g0.shape[0]
    seq = 2 * half
    for micro in range(2):
        rows = slice(micro * seq, (micro + 1) * seq)
        g = jnp.concatenate([g0[...], g1[...]] if micro == 0 else [g2[...], g3[...]], axis=0)
        g_full[rows, :] = g
        for lo, hi in SPLITS:
            ga = dot_nt(g, fc2[lo:hi, :])
            v = pre_ref[rows, lo:hi]
            t = jnp.tanh(K0 * (v + 0.044715 * (v * v * v)))
            slope = 0.5 * (1.0 + t) + 0.5 * v * (1.0 - t * t) * (K0 * (1.0 + 3.0 * 0.044715 * (v * v)))
            gp = (ga * slope).astype(BF16)
            gpre_ref[rows, lo:hi] = gp
            total = jnp.sum(gp.astype(F32), axis=0, keepdims=True)
            bias[:, lo:hi] = total if micro == 0 else bias[:, lo:hi] + total
        gp = gpre_ref[rows, :]
        for lo, hi in SPLITS:
            part = dot_nt(gp, fc1[lo:hi, :])
            if micro == 0:
                part_q[:, lo:hi] = part[:half]
                part_y[:, lo:hi] = part[half:]
            else:
                send[:, lo:hi] = part.astype(BF16)


def proj_kernel(plan, n_pieces, quarter_of, meta, *refs):
    (part, got, ry, h_one, mods, seg_ref, fc2_b, grad_out, feat_ref, keep_ref, b1, b2, b3) = refs[:13]
    pieces = refs[13 : 13 + n_pieces]
    (ins_ref, keep_out, send_out, grad_h, g_mlp, gate_sum, gb1, gb2, gb3, gbf) = refs[13 + n_pieces : 23 + n_pieces]
    w1, w2, w3, a1, a2, ga1_ref, ga2_ref, gz_ref, sems = refs[23 + n_pieces :]
    weights = (w1, w2, w3)
    half, width = h_one.shape
    slots = mods.shape[0]
    hidden = w1.shape[1]
    for which, load in enumerate(plan):
        for source, target in load(pieces, weights[which]):
            pltpu.make_async_copy(source, target, sems.at[which]).start()
    seg = seg_ref[...]
    gate = pick(seg, mods[:, 5 * width : 6 * width])
    mlp = part[...] + got[0:half, :].astype(F32) + ry[...].astype(F32) + fc2_b[...]
    h = h_one[...] + gate * mlp
    hl = h.astype(BF16)
    ins_ref[:, 2 * hidden :] = hl
    step = 512
    pltpu.make_async_copy(w1, w1, sems.at[0]).wait()
    for lo in range(0, hidden, step):
        a = dot(hl, w1[:, lo : lo + step]) + b1[:, lo : lo + step]
        a1[:, lo : lo + step] = a
        ins_ref[:, lo : lo + step] = (a * sigmoid(a)).astype(BF16)
    pltpu.make_async_copy(w2, w2, sems.at[1]).wait()
    s = ins_ref[:, 0:hidden]
    for lo in range(0, hidden, step):
        a = dot(s, w2[:, lo : lo + step]) + b2[:, lo : lo + step]
        a2[:, lo : lo + step] = a
        ins_ref[:, hidden + lo : hidden + lo + step] = (a * sigmoid(a)).astype(BF16)
    pltpu.make_async_copy(w3, w3, sems.at[2]).wait()
    z = dot(ins_ref[:, hidden : 2 * hidden], w3[...]) + b3[...]
    feat = feat_ref[...].astype(F32)
    inv_z = lax.rsqrt(jnp.sum(z * z, axis=-1, keepdims=True) + cos_eps)
    inv_f = lax.rsqrt(jnp.sum(feat * feat, axis=-1, keepdims=True) + cos_eps)
    zf = jnp.sum(z * feat, axis=-1, keepdims=True)
    coeff = -repa_weight * keep_ref[...] * inv_z * inv_f
    gz = (coeff * (feat - (zf * inv_z * inv_z) * z)).astype(BF16)
    gz_ref[...] = gz
    gb3[...] = jnp.sum(gz.astype(F32), axis=0, keepdims=True)
    for lo in range(0, hidden, step):
        g = (dot_nt(gz, w3[lo : lo + step, :]) * silu_slope(a2[:, lo : lo + step])).astype(BF16)
        ga2_ref[:, lo : lo + step] = g
        gb2[:, lo : lo + step] = jnp.sum(g.astype(F32), axis=0, keepdims=True)
    ga2 = ga2_ref[...]
    for lo in range(0, hidden, step):
        g = (dot_nt(ga2, w2[lo : lo + step, :]) * silu_slope(a1[:, lo : lo + step])).astype(BF16)
        ga1_ref[:, lo : lo + step] = g
        gb1[:, lo : lo + step] = jnp.sum(g.astype(F32), axis=0, keepdims=True)
    gh = grad_out[...].astype(F32) + dot_nt(ga1_ref[...], w1[...])
    grad_h[...] = gh
    gm = (gate * gh).astype(BF16)
    g_mlp[...] = gm
    gbf[...] = jnp.sum(gm.astype(F32), axis=0, keepdims=True)
    gate_sum[...] = by_image(seg, gh * mlp, slots)
    n, m = hidden // 4, gz.shape[1] // 4
    wide = 2 * n + m
    for out, cr in ((keep_out, 0), (send_out, 1)):
        for yr in range(2):
            q = quarter_of(meta, yr, cr)
            columns, low = pl.ds(pl.multiple_of(q * n, 128), n), pl.ds(pl.multiple_of(q * m, 128), m)
            out[:, yr * wide : yr * wide + n] = ga2_ref[:, columns]
            out[:, yr * wide + n : yr * wide + 2 * n] = ga1_ref[:, columns]
            out[:, yr * wide + 2 * n : (yr + 1) * wide] = gz_ref[:, low]


def proj_grad_kernel(hidden, place, n_outs, meta, f0, f1, f2, f3, keep, got, *refs):
    outs = refs[:n_outs]
    a, b, r2, r3, r1, in_sem, out_sem = refs[n_outs:]
    half = f0.shape[0]
    wide = b.shape[1]
    n = r2.shape[1]
    f_wide = a.shape[1]
    for at, piece in enumerate((f0, f1, f2, f3)):
        pltpu.make_async_copy(piece.at[:, 0:f_wide], a.at[at * half : (at + 1) * half, :], in_sem.at[0]).start()
    for at, piece in enumerate(
        (keep.at[:, 0:wide], f1.at[:, f_wide : f_wide + wide], got.at[:, 0:wide], f1.at[:, f_wide + wide : f_wide + 2 * wide])
    ):
        pltpu.make_async_copy(piece, b.at[at * half : (at + 1) * half, :], in_sem.at[1]).start()
    pltpu.make_async_copy(b, b, in_sem.at[1]).wait()
    pltpu.make_async_copy(a, a, in_sem.at[0]).wait()
    for job, (first, cols, g, step) in enumerate(
        ((0, slice(0, n), r2, 512), (hidden, slice(2 * n, wide), r3, 512), (2 * hidden, slice(n, 2 * n), r1, 384))
    ):
        for lo in range(0, g.shape[0], step):
            g[lo : lo + step, :] = dot_tn(a[:, first + lo : first + lo + step], b[:, cols]).astype(BF16)
        for source, target in place(job, g, outs, meta):
            pltpu.make_async_copy(source, target, out_sem.at[job]).start()
    for job, g in enumerate((r2, r3, r1)):
        pltpu.make_async_copy(g, g, out_sem.at[job]).wait()


def second_back_kernel(part, rq, ry, grad_h, h_one, attn, mods, seg_ref, g_one, g_attn, gate_sum, shift_sum, scale_sum, bias):
    width = h_one.shape[1]
    slots = mods.shape[0]
    seg = seg_ref[...]
    g = part[...] + rq[0 : part.shape[0], :].astype(F32) + ry[...].astype(F32)
    xhat, inv = norm_parts(h_one[...])
    total = grad_h[...] + norm_back(g * (1.0 + pick(seg, mods[:, 4 * width : 5 * width])), xhat, inv)
    g_one[...] = total
    ga = (pick(seg, mods[:, 2 * width : 3 * width]) * total).astype(BF16)
    g_attn[...] = ga
    bias[...] = jnp.sum(ga.astype(F32), axis=0, keepdims=True)
    gate_sum[...] = by_image(seg, total * attn[...], slots)
    shift_sum[...] = by_image(seg, g, slots)
    scale_sum[...] = by_image(seg, g * xhat, slots)


def first_back_kernel(order, part, rq, ry, g_one, hid, mods, seg_ref, g_in, shift_sum, scale_sum):
    width = g_one.shape[1]
    slots = mods.shape[0]
    seg = seg_ref[...]
    g = part[...] + rq[0 : part.shape[0], :].astype(F32) + ry[...].astype(F32)
    xhat, inv = norm_parts(hid[order[0]].astype(F32))
    total = g_one[...] + norm_back(g * (1.0 + pick(seg, mods[:, width : 2 * width])), xhat, inv)
    g_in[...] = total.astype(BF16)
    shift_sum[...] = by_image(seg, g, slots)
    scale_sum[...] = by_image(seg, g * xhat, slots)


def wgrad_kernel(place, jobs, n_outs, *refs):
    meta = refs[0]
    n_ins = 1 + max(max(a, b) for a, b, _ in jobs)
    ins, outs, (*results, sem) = refs[1 : 1 + n_ins], refs[1 + n_ins : 1 + n_ins + n_outs], refs[1 + n_ins + n_outs :]
    for n, (a, b, step) in enumerate(jobs):
        g = results[n]
        rows = g.shape[0]
        for lo in range(0, rows, step):
            hi = min(lo + step, rows)
            g[lo:hi, :] = dot_tn(ins[a][:, lo:hi], ins[b][...]).astype(BF16)
        for source, target in place(n, g, outs, meta):
            pltpu.make_async_copy(source, target, sem.at[n]).start()
    for n, g in enumerate(results):
        pltpu.make_async_copy(g, g, sem.at[n]).wait()


def body(mesh, hidden_in, grad_out, features, seg_ids, valid_mask, time_ids, class_ids, class_table, ada_w, ada_b, qkv_w, qv_bias, out_w, out_b, fc1_w, fc1_b, fc2_w, fc2_b, repa_w1, repa_b1, repa_w2, repa_b2, repa_w3, repa_b3):
    n_dp = mesh.shape["dp"]
    top = n_dp // 2
    micro_count, rows_dev, seq, width = hidden_in.shape
    slots = time_ids.shape[-1]
    images = micro_count * rows_dev * slots
    half = seq // 2
    wide = qkv_w.shape[2]
    qkv_t = qkv_w.transpose(0, 2, 1)
    heads = wide // HEAD_DIM
    ff = fc1_w.shape[1]
    hidden = repa_w1.shape[1]
    repr_width = repa_w3.shape[1]

    d = lax.axis_index("dp")
    t = lax.axis_index("tensor")
    y, c = t // 2, t % 2
    meta = jnp.stack([d, d, y, c]).astype(jnp.int32)

    def flip_dp(x, mask):
        return lax.ppermute(x, "dp", [(k, k ^ mask) for k in range(n_dp)])

    def swap_y(x):
        return lax.ppermute(x, "tensor", [(0, 2), (2, 0), (1, 3), (3, 1)])

    def swap_core(x):
        return lax.ppermute(x, "tensor", [(0, 1), (1, 0), (2, 3), (3, 2)])

    def exchange_dp(x):
        return lax.all_to_all(x, "dp", 0, 0, tiled=True)

    def gather_dp(x):
        return exchange_dp(jnp.broadcast_to(x[None], (n_dp,) + x.shape))

    def cols_of(w):
        n = w.shape[1] // 4
        return lax.dynamic_slice_in_dim(w, t * n, n, axis=1)

    k1, k2, k3 = repa_w1.shape[0], repa_w2.shape[0], repa_w3.shape[0]
    block = hidden // 4
    third = repr_width // 4
    room = block // 2
    short = k3 // 2

    def cols_padded(w, axis_n):
        w = w.reshape(w.shape[:-1] + (4, axis_n // 4))
        return jnp.pad(w, [(0, 0)] * (w.ndim - 1) + [(0, room - axis_n // 4)]).reshape(w.shape[:-2] + (4 * room,))

    w3_mine = jnp.pad(cols_of(repa_w3), ((0, 0), (0, room - third)))
    w3_fold = jnp.concatenate([w3_mine[:short], w3_mine[short:]], axis=1)
    packed = jnp.concatenate([cols_of(repa_w2), w3_fold, cols_of(repa_w1)], axis=0)
    gathered = lax.all_gather(packed, ("dp", "tensor"), axis=0)
    off3, off1 = k2, k2 + short
    out_y = swap_y(out_w)
    out_c = swap_core(out_w)
    out_yc = swap_core(out_y)
    n1, n2, n3 = repa_b1.shape[0], repa_b2.shape[0], repa_b3.shape[0]

    ids = gather_dp(jnp.concatenate([class_ids.reshape(images), time_ids.reshape(images)]))
    all_class = ids[:, :images].reshape(1, n_dp * images)
    all_time = ids[:, images:].reshape(1, n_dp * images)
    feats = class_table.shape[0]
    class_hot = lax.broadcasted_iota(jnp.int32, (class_table.shape[1], n_dp * images), 0) == all_class
    place = d * feats + lax.broadcasted_iota(jnp.int32, (feats, 1), 0)
    half_width = width // 2
    freqs = jnp.exp(-math.log(10000.0) * (place % half_width).astype(F32) / half_width)
    angles = all_time.astype(F32) * freqs
    condition = jnp.where(place < half_width, jnp.cos(angles), jnp.sin(angles)) + dot(class_table, class_hot.astype(BF16))
    n_images = n_dp * images
    biases = jnp.concatenate([repa_b1, repa_b2, repa_b3])
    lines = -(-biases.shape[0] // n_images)
    biases = jnp.pad(biases, (0, lines * n_images - biases.shape[0])).reshape(lines, n_images)
    found = gather_dp(jnp.concatenate([jax.nn.silu(condition).astype(BF16), biases], axis=0))
    cond_act = found[:, :feats].reshape(width, n_images)
    b_all = found[:, feats:].reshape(n_dp, -1)
    b_one = b_all[:, :n1].reshape(1, -1).astype(F32)
    b_two = b_all[:, n1 : n1 + n2].reshape(1, -1).astype(F32)
    b_three = cols_padded(b_all[:, n1 + n2 : n1 + n2 + n3].reshape(1, -1).astype(F32), repr_width)
    mod_part = lax.dot_general(cond_act, ada_w, (((0,), (1,)), ((), ())), preferred_element_type=F32) + ada_b.astype(F32)
    mod_parts = exchange_dp(mod_part.reshape(n_dp, images, -1))
    modulation = mod_parts.transpose(1, 0, 2).reshape(micro_count, slots, -1)
    mods_own = lax.dynamic_index_in_dim(modulation, c, 0, keepdims=False)
    mods_par = lax.dynamic_index_in_dim(modulation, 1 - c, 0, keepdims=False)

    order = jnp.stack([2 * c + y, 2 * c + 1 - y, 2 * (1 - c) + y, 2 * (1 - c) + 1 - y]).astype(jnp.int32)
    hid = hidden_in.reshape(4, half, width)

    def ordered(a):
        a = a.reshape(4, half)
        return jnp.concatenate([lax.dynamic_index_in_dim(a, order[n], 0, keepdims=False) for n in range(4)])

    seg_line = ordered(seg_ids)
    val_line = ordered(valid_mask)
    seg_rows = seg_line.reshape(2, seq)
    val_rows = val_line.reshape(2, seq)
    seg_cols = seg_line.reshape(2 * seq, 1)
    seg_q = seg_cols[:half]
    keep_q = val_line[:half].reshape(half, 1).astype(F32)
    go_q = lax.dynamic_index_in_dim(grad_out.reshape(4, half, width), order[0], 0, keepdims=False)
    feat_q = cols_padded(lax.dynamic_index_in_dim(features.reshape(4, half, repr_width), order[0], 0, keepdims=False), repr_width)

    tokens = 2 * seq
    T = tokens

    def fwd(order_, hid_, a, b, *rest):
        return functools.partial(fwd_kernel, heads)(order_, hid_, (a, b), *rest)

    m_one, q, k, v, mixed = call(
        fwd,
        [shape_of((T, width), BF16)] + [shape_of((T, wide), BF16)] * 4,
        [order, hid, mods_own, mods_par, seg_cols, seg_rows, val_rows, qkv_t, qv_bias.astype(F32)],
        in_specs=[SMEM] + [VMEM] * 8,
        flops=2 * T * width * wide * 3 + 4 * T * seq * wide,
        name="attention",
    )

    mix_own, mix_send = mixed[:seq], mixed[seq:]
    mix_y = swap_y(mix_own)
    mix_c = swap_core(mix_send)
    mix_yc = swap_y(mix_c)
    attn_q, h_q, m_two = call(
        mid_kernel,
        [shape_of((half, width), F32), shape_of((half, width), F32), shape_of((seq, width), BF16)],
        [order, hid, mods_own, seg_cols, mix_own, mix_c, mix_y, mix_yc, out_w, out_c, out_y, out_yc, out_b.astype(F32).reshape(1, width)],
        in_specs=[SMEM] + [VMEM] * 12,
        flops=2 * seq * width * width,
        name="middle",
    )
    m_par = swap_core(m_two)

    quarter = [shape_of((half, width), F32), shape_of((half, width), F32), shape_of((seq, width), BF16)]

    def settle_quarter(part_y, send):
        got = swap_core(send)
        sent = (part_y + got[half:].astype(F32)).astype(BF16)
        return got, swap_y(sent), sent

    def spread_quarter(g):
        gy = swap_y(g)
        return g, gy, swap_core(g), swap_core(gy)

    m_full, pre, act, part_q, part_y, send = call(
        mlp_kernel,
        [shape_of((T, width), BF16), shape_of((T, ff), F32), shape_of((T, ff), BF16)] + quarter,
        [m_two, m_par, fc1_w, fc1_b.astype(F32).reshape(1, ff), fc2_w],
        flops=4 * T * width * ff,
        name="mlp",
    )
    rq, ry, y_sent = settle_quarter(part_y, send)

    def k_of(w):
        return w.shape[0]

    def position(meta_, rel):
        return lax.bitwise_xor(meta_[0], jnp.int32(rel))

    def relative(nat):
        for bit in range(n_dp.bit_length() - 1):
            cut = nat.reshape((top >> bit, 2, 1 << bit) + nat.shape[1:])
            nat = jnp.where((d >> bit) & 1 == 0, cut, cut[:, ::-1]).reshape(nat.shape)
        return nat

    def quarter_of(meta_, yr, cr):
        ty = meta_[2] if yr == 0 else 1 - meta_[2]
        tc = meta_[3] if cr == 0 else 1 - meta_[3]
        return ty * 2 + tc

    def pair(stack, me, axis):
        first, second = stack
        same = me == 0
        return jnp.concatenate([jnp.where(same, first, second), jnp.where(same, second, first)], axis=axis)

    aligned = k1 % 16 == 0 and k2 % 16 == 0 and k3 % 32 == 0
    n_all = 4 * n_dp

    def load_two(refs, target):
        for s in range(n_all):
            at, part = s // 4, s % 4
            yield refs[0].at[s, 0:k2, :], target.at[at * k2 : (at + 1) * k2, part * block : (part + 1) * block]

    def load_one(refs, target):
        for s in range(n_all):
            at, part = s // 4, s % 4
            yield refs[0].at[s, off1 : off1 + k1, :], target.at[at * k1 : (at + 1) * k1, part * block : (part + 1) * block]

    def load_three(refs, target):
        for s in range(n_all):
            at, part = s // 4, s % 4
            for n in range(2):
                rows = slice(at * k3 + n * short, at * k3 + (n + 1) * short)
                yield refs[0].at[s, off3:off1, n * room : (n + 1) * room], target.at[rows, part * room : (part + 1) * room]

    def whole(n):
        def load(refs, target):
            yield refs[n], target

        return load

    if aligned:
        pieces = [gathered]
        plan = [load_one, load_two, load_three]
    else:
        by_cols = lambda a: a.reshape(n_dp, 4, -1, block).transpose(0, 2, 1, 3).reshape(-1, hidden)
        fold = gathered[:, off3:off1].reshape(n_dp, 4, short, 2, room).transpose(0, 3, 2, 1, 4).reshape(hidden, 4 * room)
        pieces = [by_cols(gathered[:, off1:]), by_cols(gathered[:, :off3]), fold]
        plan = [whole(0), whole(1), whole(2)]

    small_ins = [part_q, rq, ry, h_q, mods_own, seg_q, fc2_b.astype(F32).reshape(1, width), go_q, feat_q, keep_q, b_one, b_two, b_three]
    q_wide = 2 * block + room
    f_own, q_keep, q_send, grad_h, g_mlp, gate_two, g_b1, g_b2, g_b3, g_fc2_b = call(
        functools.partial(proj_kernel, plan, len(pieces), quarter_of),
        [
            shape_of((half, 2 * hidden + width), BF16),
            shape_of((half, 2 * q_wide), BF16),
            shape_of((half, 2 * q_wide), BF16),
            shape_of((half, width), F32),
            shape_of((half, width), BF16),
            shape_of((slots, width), F32),
            shape_of((1, hidden), F32),
            shape_of((1, hidden), F32),
            shape_of((1, 4 * room), F32),
            shape_of((1, width), F32),
        ],
        [meta] + small_ins + pieces,
        in_specs=[SMEM] + [VMEM] * len(small_ins) + [ANY] * len(pieces),
        scratch=[
            pltpu.VMEM((width, hidden), BF16),
            pltpu.VMEM((hidden, hidden), BF16),
            pltpu.VMEM((hidden, 4 * room), BF16),
            pltpu.VMEM((half, hidden), F32),
            pltpu.VMEM((half, hidden), F32),
            pltpu.VMEM((half, hidden), BF16),
            pltpu.VMEM((half, hidden), BF16),
            pltpu.VMEM((half, 4 * room), BF16),
            pltpu.SemaphoreType.DMA((3,)),
        ],
        flops=4 * half * (width * hidden + hidden * hidden + hidden * repr_width),
        name="projector",
    )
    g_mlp_y, g_mlp_c = swap_y(g_mlp), swap_core(g_mlp)
    g_mlp_yc = swap_core(g_mlp_y)
    q_got = swap_core(q_send)
    f_c = swap_core(f_own)
    (f_sent,) = hold([f_own], [g_mlp_y])
    f_wide = 2 * hidden + width
    f_sent = jnp.concatenate([f_sent, q_keep[:, q_wide:], q_got[:, q_wide:]], axis=1)
    f_y = swap_y(f_sent)

    def wgrad(place, jobs, ins, outs, name, after=()):
        shapes = [(ins[a].shape[1], ins[b].shape[1]) for a, b, _ in jobs]
        return call(
            functools.partial(wgrad_kernel, place, jobs, len(outs)),
            outs,
            [meta] + ins,
            in_specs=[SMEM] + [VMEM] * len(ins),
            out_specs=[ANY] * len(outs),
            scratch=[pltpu.VMEM(s, BF16) for s in shapes] + [pltpu.SemaphoreType.DMA((len(jobs),))],
            flops=sum(2 * ins[a].shape[0] * r * n for (a, _, _), (r, n) in zip(jobs, shapes)),
            name=name,
            after=after,
        )

    def wgrad_natural(jobs, ins, name, after=()):
        outs = [shape_of((ins[a].shape[1], ins[b].shape[1]), BF16) for a, b, _ in jobs]
        return wgrad(lambda n, g, outs_, meta_: [(g, outs_[n])], jobs, ins, outs, name, after)

    ascending = [1 << n for n in range(n_dp.bit_length() - 1)]
    x_first, x_last = ascending, ascending[1:] + [1]

    def index_of(rel, masks):
        bits = [1 if rel & mask else 0 for mask in masks]
        entry = 0
        for bit in bits[1:]:
            entry = 2 * entry + bit
        return bits[0], entry

    def in_order(rel, masks):
        bits = len(masks)
        cut = rel.reshape((2,) * bits + rel.shape[1:])
        dims = [bits - mask.bit_length() for mask in masks]
        cut = cut.transpose(dims + list(range(bits, cut.ndim))).reshape(rel.shape)
        return cut[:top], cut[top:]

    def wgrad_dp(groups, ins, name, after=()):
        jobs = [job for group, _ in groups for job in group]
        owner = [(n, sum(ins[b].shape[1] for _, b, _ in group[:at])) for n, (group, _) in enumerate(groups) for at in range(len(group))]
        depths = [ins[group[0][0]].shape[1] // n_dp for group, _ in groups]
        widths = [sum(ins[b].shape[1] for _, b, _ in group) for group, _ in groups]
        if all(depth % 16 == 0 for depth in depths) and all(at % 128 == 0 for _, at in owner):

            def place(n, g, outs, meta_):
                group, lo = owner[n]
                depth = depths[group]
                for rel in range(n_dp):
                    at = pl.multiple_of(position(meta_, rel) * depth, 16)
                    side, entry = index_of(rel, groups[group][1])
                    yield g.at[pl.ds(at, depth), :], outs[2 * group + side].at[entry, :, lo : lo + g.shape[1]]

            outs = wgrad(place, jobs, ins, [shape_of((top, depth, w), BF16) for depth, w in zip(depths, widths) for _ in range(2)], name, after)
            return [(outs[2 * n], outs[2 * n + 1]) for n in range(len(groups))]
        nat = list(wgrad_natural(jobs, ins, name, after))
        found = []
        for n, (group, masks) in enumerate(groups):
            one = jnp.concatenate([nat.pop(0) for _ in group], axis=1).reshape(n_dp, depths[n], widths[n])
            found.append(in_order(relative(one), masks))
        return found

    def halves(v):
        return v.reshape((2, v.shape[0] // 2) + v.shape[1:])

    def halve(v, mask):
        return v[0].astype(F32) + flip_dp(v[1].astype(BF16), mask).astype(F32)

    def halve_all(v, masks):
        for mask in masks:
            v = halve(halves(v), mask)
        return v[0]

    f1 = k1 * block // (block + room)

    def proj_grads(after=()):
        ins = [meta, f_own, f_y, f_c, f_yc, q_keep, q_got]
        whole_rows = aligned and f1 % 32 == 0

        def place(job, g, outs, meta_):
            if not whole_rows:
                yield g, outs[job]
                return
            for rel in range(n_dp):
                side, entry = index_of(rel, x_first)
                to = outs[side].at[entry]
                at = position(meta_, rel)
                if job < 2:
                    columns = slice(0, block) if job == 0 else slice(block, block + room)
                    yield g.at[pl.ds(pl.multiple_of(at * k2, 16), k2), :], to.at[0:k2, columns]
                    continue
                low = f1 // 2
                yield g.at[pl.ds(pl.multiple_of(at * k1, 16), f1), :], to.at[k2 : k2 + f1, 0:block]
                for n in range(2):
                    yield (
                        g.at[pl.ds(pl.multiple_of(at * k1 + f1, 16), low), n * room : (n + 1) * room],
                        to.at[k2 + n * low : k2 + (n + 1) * low, block : block + room],
                    )

        grads = [(hidden, block), (hidden, room), (width, block)]
        shapes = [shape_of((top, k2 + f1, block + room), BF16)] * 2 if whole_rows else [shape_of(g, BF16) for g in grads]
        found = call(
            functools.partial(proj_grad_kernel, hidden, place, len(shapes)),
            shapes,
            ins,
            in_specs=[SMEM] + [ANY] * 6,
            out_specs=[ANY] * len(shapes),
            scratch=[
                pltpu.VMEM((T, 2 * hidden + width), BF16),
                pltpu.VMEM((T, q_wide), BF16),
                *[pltpu.VMEM(g, BF16) for g in grads],
                pltpu.SemaphoreType.DMA((2,)),
                pltpu.SemaphoreType.DMA((3,)),
            ],
            name="grad_projector",
            after=after,
        )
        if whole_rows:
            return found
        two, three, one = found
        one = one.reshape(n_dp, k1, block)
        low = one[:, f1:]
        folded = jnp.concatenate([one[:, :f1], jnp.concatenate([low[..., :room], low[..., room:]], axis=1)], axis=2)
        above = jnp.concatenate([two, three], axis=1).reshape(n_dp, k2, block + room)
        return in_order(relative(jnp.concatenate([above, folded], axis=1)), x_first)

    def unfolded(q):
        low = q[:, :, block:]
        return jnp.concatenate([q[:, :, :block], jnp.concatenate([low[:, : f1 // 2], low[:, f1 // 2 :]], axis=2)], axis=1)

    def quarters(mine):
        mine = mine.astype(BF16)
        other = swap_y(mine)
        c0, c1 = swap_core(mine), swap_core(other)
        own = pair([mine[None], c0[None]], c, 0)
        peer = pair([other[None], c1[None]], c, 0)
        return pair([own, peer], y, 0)

    def side_by_side(q):
        return jnp.concatenate([q[n] for n in range(4)], axis=1).astype(F32)

    g_mlp_full, gpre, part_q, part_y, send, g_fc1_b = call(
        mlp_back_kernel,
        [shape_of((T, width), BF16), shape_of((T, ff), BF16)] + quarter + [shape_of((1, ff), F32)],
        [g_mlp, g_mlp_y, g_mlp_c, g_mlp_yc, pre, fc1_w, fc2_w],
        flops=4 * T * width * ff,
        name="mlp_back",
        after=[f_c, f_sent],
    )
    rq, ry, y_sent = settle_quarter(part_y, send)
    fc2_parts, fc1_parts = wgrad_dp(
        [([(0, 1, 384)], x_last), ([(2, 3, 384)], x_first)], [g_mlp_full, act, m_full, gpre], "grad_fc"
    )
    fc2_got = flip_dp(fc2_parts[1], x_last[0])
    fc1_got = flip_dp(fc1_parts[1], 1)
    (f_y,) = hold([f_y], [fc1_parts[1], y_sent])
    f_yc = swap_core(f_y)
    low_own, low_y, low_c, low_yc = (a[:, 2 * hidden : f_wide] for a in (f_own, f_y, f_c, f_yc))
    pg_first, pg_second = proj_grads(after=[fc1_parts[1]])
    pg_got = flip_dp(pg_second, 1)
    g_one, g_attn, gate_one, shift_two, scale_two, g_out_b = call(
        second_back_kernel,
        [shape_of((half, width), F32), shape_of((half, width), BF16)] + [shape_of((slots, width), F32)] * 3 + [shape_of((1, width), F32)],
        [part_q, rq, ry, grad_h, h_q, attn_q, mods_own, seg_q],
        name="second_back",
        after=[pg_second],
    )
    g_attn_all = spread_quarter(g_attn)
    fc2_got, fc1_got = hold([fc2_got, fc1_got], [g_attn])
    fc2_v = halves(fc2_parts[0].astype(F32) + fc2_got.astype(F32))
    fc2_next = flip_dp(fc2_v[1].astype(BF16), x_last[1])
    fc1_v = halves(fc1_parts[0].astype(F32) + fc1_got.astype(F32))
    fc1_next = flip_dp(fc1_v[1].astype(BF16), 2)

    gqkv, part_q, part_y, send, g_qv_b, g_attn_full = call(
        functools.partial(bwd_kernel, heads),
        [shape_of((T, -(-3 * wide // 128) * 128), BF16)] + quarter + [shape_of((2, wide), F32), shape_of((T, width), BF16)],
        list(g_attn_all) + [out_w, q, k, v, seg_cols, seg_rows, val_rows, qkv_t],
        flops=8 * T * width * wide + 10 * T * seq * wide,
        name="attention_back",
    )
    rq, ry, y_sent = settle_quarter(part_y, send)
    ((heads_first, heads_second),) = wgrad_dp(
        [([(0, 1, 384), (2, 3, 384)], x_first)], [m_one, gqkv, g_attn_full, mixed], "grad_heads", after=[]
    )
    g_in, shift_one, scale_one = call(
        first_back_kernel,
        [shape_of((half, width), BF16)] + [shape_of((slots, width), F32)] * 2,
        [order, part_q, rq, ry, g_one, hid, mods_own, seg_q],
        in_specs=[SMEM] + [VMEM] * 7,
        name="first_back",
        after=[heads_second],
    )
    heads_got = flip_dp(heads_second, 1)

    (pg_got,) = hold([pg_got], [g_in])
    pg_v = halves(pg_first.astype(F32) + pg_got.astype(F32))
    pg_sent = pg_v[1].astype(BF16)
    pg_got = flip_dp(pg_sent, 2)
    fc2_next, fc1_next = hold([fc2_next, fc1_next], [pg_sent])
    fc2_v = fc2_v[0] + fc2_next.astype(F32)
    fc1_v = halves(fc1_v[0] + fc1_next.astype(F32))
    fc2_v = halves(fc2_v)
    fc2_last = flip_dp(fc2_v[1].astype(BF16), x_last[2])
    fc1_last = flip_dp(fc1_v[1].astype(BF16), x_first[2])

    g_mod = jnp.concatenate([shift_one, scale_one, gate_one, shift_two, scale_two, gate_two], axis=-1)
    g_b3 = g_b3.reshape(4, room)[:, :third].reshape(1, repr_width)
    early = jnp.concatenate([g_b1, g_b2, g_b3, g_fc2_b, g_out_b], axis=1)
    early = early + swap_core(early)
    line = jnp.concatenate([g_mod.reshape(1, -1), early], axis=1)
    (line,) = hold([line], [pg_sent])
    line = line + swap_y(line)
    g_mod, early = line[:, : slots * 6 * width].reshape(slots, -1).astype(BF16), line[:, slots * 6 * width :]
    g_mod = exchange_dp(g_mod.reshape(slots, n_dp, -1).transpose(1, 0, 2))
    pg_v = halves(pg_v[0] + pg_got.astype(F32))
    pg_sent = pg_v[1].astype(BF16)
    pg_got = flip_dp(pg_sent, 4)
    heads_got, g_in = hold([heads_got, g_in], [pg_sent])
    heads_v = halves(heads_first.astype(F32) + heads_got.astype(F32))
    heads_sent = heads_v[1].astype(BF16)
    heads_got = flip_dp(heads_sent, 2)
    (g_mod,) = hold([g_mod], [heads_sent])
    fc2_last, fc1_last = hold([fc2_last, fc1_last], [g_mod])
    g_mod = pair([g_mod, swap_core(g_mod)], c, 1).reshape(n_dp * images, -1)
    g_ada_w = lax.dot_general(g_mod, cond_act, (((0,), (1,)), ((), ())), preferred_element_type=F32)
    g_ada_b = jnp.sum(g_mod.astype(F32), axis=0)
    g_cond = lax.dot_general(ada_w, g_mod, (((0,), (1,)), ((), ())), preferred_element_type=F32)
    own = jnp.concatenate([early, g_fc1_b, g_qv_b.reshape(1, 2 * wide)], axis=1)
    sent = jnp.concatenate([g_cond.reshape(n_dp, feats * n_images), jnp.broadcast_to(own, (n_dp, own.shape[1]))], axis=1)
    heads_v = halves(heads_v[0] + heads_got.astype(F32))
    heads_sent = heads_v[1].astype(BF16)
    heads_got = flip_dp(heads_sent, 4)
    mine = halve_all(pg_v[0] + pg_got.astype(F32), x_first[3:]).astype(BF16)
    found = quarters(mine)
    (sent,) = hold([sent], [heads_sent, mine])
    sums = exchange_dp(sent)
    sums = jnp.sum(sums, axis=0)
    g_fc2_t = halve_all(fc2_v[0] + fc2_last.astype(F32), x_last[3:])
    g_fc1 = halve_all(fc1_v[0] + fc1_last.astype(F32), x_first[3:])
    g_heads = halve_all(heads_v[0] + heads_got.astype(F32), x_first[3:])
    g_qkv, g_out_t = g_heads[:, : 3 * wide], g_heads[:, gqkv.shape[1] :]
    g_w2 = side_by_side(found[:, :k2, :block])
    g_w3 = side_by_side(found[:, :k2, block : block + third])
    g_w1 = side_by_side(unfolded(found[:, k2:]))
    g_cond, sums = sums[: feats * n_images].reshape(feats, n_images), sums[feats * n_images :]
    g_cond = g_cond * silu_slope(condition)
    g_table = lax.dot_general(
        g_cond, class_hot.astype(F32), (((1,), (1,)), ((), ())), precision=lax.Precision.HIGHEST, preferred_element_type=F32
    )

    cuts = [hidden, hidden, repr_width, width, width, ff, 2 * wide]
    marks = [sum(cuts[:n]) for n in range(len(cuts) + 1)]
    s_one_b, s_two_b, s_three_b, s_fc2_b, s_out_b, s_fc1_b, s_qv_b = (sums[lo:hi] for lo, hi in zip(marks, marks[1:]))

    def my_part(x, n):
        return lax.dynamic_slice_in_dim(x.reshape(-1), d * n, n)

    s_b1, s_b2, s_b3 = my_part(s_one_b, n1), my_part(s_two_b, n2), my_part(s_three_b, n3)
    s_qv_b = s_qv_b.reshape(2, wide)

    def spread_tokens(block, other, c0, c1):
        own = pair([block, other], y, 0)
        peer = pair([c0, c1], y, 0)
        return pair([own, peer], c, 0).reshape(micro_count, rows_dev, seq, width)

    block_out = spread_tokens(low_own, low_y, low_c, low_yc)
    grad_in = spread_tokens(*spread_quarter(g_in)).astype(F32)
    depth = width // n_dp
    return (
        block_out,
        grad_in,
        g_table,
        g_ada_w,
        g_ada_b,
        jnp.stack([g_qkv[:, :wide], g_qkv[:, wide : 2 * wide], g_qkv[:, 2 * wide :]]),
        s_qv_b,
        g_out_t.T,
        s_out_b,
        g_fc1,
        s_fc1_b,
        g_fc2_t.T,
        s_fc2_b,
        g_w1,
        s_b1,
        g_w2,
        s_b2,
        g_w3,
        s_b3,
    )


def solution(mesh):
    dp, tensor = "dp", "tensor"
    rows4, rows3 = P(None, dp, None, None), P(None, dp, None)
    ins = (rows4, rows4, rows4, rows3, rows3, rows3, rows3, P(dp, None), P(dp, None), P(dp), P(None, None, tensor), P(None, tensor), P(tensor, None), P(), P(None, tensor), P(tensor), P(tensor, None), P(), P(dp, None), P(dp), P(dp, None), P(dp), P(dp, None), P(dp))
    outs = (rows4, rows4, P(dp, None), P(dp, None), P(dp), P(None, dp, tensor), P(None, tensor), P(tensor, dp), P(), P(dp, tensor), P(tensor), P(tensor, dp), P(), P(dp, None), P(dp), P(dp, None), P(dp), P(dp, None), P(dp))
    return jax.shard_map(functools.partial(body, mesh), mesh=mesh, in_specs=ins, out_specs=outs, check_vma=False)
```
